128 devices in a mesh: gz: 32 (over z, y, core), gy: 4 (over x).
Axes of the slice: x: 4, y: 4, z: 4, core: 2. Of those that a mesh axis runs over, the one named last changes fastest.
Arguments:
- activation: float32 [20, 128, 256, 256], P(None, 'gz', 'gy'), may hold values from -6 to 6
- pointwise: float32 [20, 20], replicated, may hold values from -1.25 to 1.25
- bias_term: float32 [20], replicated, may hold values from -3 to 3
- spectral_weight: float32 [32, 16, 2, 20, 20, 32], P('gz', 'gy'), may hold values from -20 to 20
- cotangent: float32 [20, 128, 256, 256], P(None, 'gz', 'gy'), may hold values from -6 to 6
Outputs:
- output_field: float32 [20, 128, 256, 256], P(None, 'gz', 'gy')
- input_grad: float32 [20, 128, 256, 256], P(None, 'gz', 'gy')
The draws below stay inside these ranges and needn't reach their ends.
All inputs are finite; a program needn't handle non-finite values.
Results may differ from the reference program's by a relative error of at most 0.000078.
Values sent between devices are 32-bit elements; how exact they have to be, the bound alone decides.
A program may use at most 128 MiB of HBM per device.

```python
import math
import jax
import jax.numpy as jnp
from jax import lax

C = 20
M = 16
NX = 256
NY = 256
NZ = 128


def block_levels(key, shape, cuts, smallest, high):
    gain = 1.0
    for axis_at, parts in cuts:
        steps = jax.random.uniform(jax.random.fold_in(jax.random.fold_in(key, 6), axis_at), (parts,), jnp.float32, smallest / len(cuts), high / len(cuts))
        gain = gain * jnp.repeat(jnp.exp(steps), shape[axis_at] // parts).reshape((-1,) + (1,) * (len(shape) - 1 - axis_at))
    return gain


def bell_draw(own_key, dims, spread, limit, pieces=(), kind=jnp.bfloat16):
    entries = spread * jax.random.normal(own_key, dims, jnp.float32)
    if pieces:
        entries = entries * block_levels(own_key, dims, pieces, -0.22, 0.18)
    return jnp.clip(entries, -limit, limit).astype(kind)


def setup_inputs(seed: int = 0) -> dict:
    splits = jax.random.split(jax.random.key(seed), 6)
    return {
        "activation": bell_draw(splits[0], (C, NZ, NY, NX), 1.0, 6.0, ((1, 32), (2, 4)), jnp.float32),
        "pointwise": bell_draw(splits[1], (C, C), C ** -0.5, 1.25, (), jnp.float32),
        "bias_term": bell_draw(splits[2], (C,), 0.5, 3.0, (), jnp.float32),
        "spectral_weight": bell_draw(splits[3], (2 * M, M, 2, C, C, 2 * M), ((NX * NY * NZ / (8 * C * M * M * M)) ** 0.5), 20.0, ((0, 32), (1, 4)), jnp.float32),
        "cotangent": bell_draw(splits[4], (C, NZ, NY, NX), 1.0, 6.0, ((1, 32), (2, 4)), jnp.float32),
    }


HIGHEST = lax.Precision.HIGHEST

def trig_tables(positions, frequency, length):
    phase = positions[:, None] * frequency[None, :] % length
    angle = phase.astype(jnp.float32) * (2.0 * math.pi / length)
    return (jnp.cos(angle), jnp.sin(angle))

def wave_numbers(modes_kept):
    lowest = jnp.arange(modes_kept, dtype=jnp.int32)
    return jnp.concatenate([lowest, lowest - modes_kept])

def along(spectrum, dimension, cosine, sine_table, direction):
    real_part = spectrum[..., 0]
    imag_part = spectrum[..., 1]

    def contract(values, table):
        product = jnp.tensordot(values, table, axes=((dimension,), (0,)), precision=HIGHEST)
        return jnp.moveaxis(product, -1, dimension)
    new_real = contract(real_part, cosine) - direction * contract(imag_part, sine_table)
    new_imag = contract(imag_part, cosine) + direction * contract(real_part, sine_table)
    return jnp.stack([new_real, new_imag], axis=-1)

def mode_product(spectrum, weights, adjoint):
    real_part = spectrum[..., 0]
    imag_part = spectrum[..., 1]
    weight_real = weights[:, :, 0]
    weight_imag = weights[:, :, 1]
    if adjoint:
        subscripts = 'klcoj,oljk->cljk'
        new_real = jnp.einsum(subscripts, weight_real, real_part, precision=HIGHEST) + jnp.einsum(subscripts, weight_imag, imag_part, precision=HIGHEST)
        new_imag = jnp.einsum(subscripts, weight_real, imag_part, precision=HIGHEST) - jnp.einsum(subscripts, weight_imag, real_part, precision=HIGHEST)
    else:
        subscripts = 'klcoj,cljk->oljk'
        new_real = jnp.einsum(subscripts, weight_real, real_part, precision=HIGHEST) - jnp.einsum(subscripts, weight_imag, imag_part, precision=HIGHEST)
        new_imag = jnp.einsum(subscripts, weight_real, imag_part, precision=HIGHEST) + jnp.einsum(subscripts, weight_imag, real_part, precision=HIGHEST)
    return jnp.stack([new_real, new_imag], axis=-1)

def kz_factor(kz_ids):
    return jnp.where(kz_ids == 0, 1.0, 2.0).astype(jnp.float32) / float(NX * NY * NZ)

def spectral(volume, weights):
    cos_x, sin_x = trig_tables(jnp.arange(NX, dtype=jnp.int32), wave_numbers(M), NX)
    cos_y, sin_y = trig_tables(jnp.arange(NY, dtype=jnp.int32), wave_numbers(M), NY)
    cos_z, sin_z = trig_tables(jnp.arange(NZ, dtype=jnp.int32), jnp.arange(M, dtype=jnp.int32), NZ)
    real_part = jnp.einsum('czyx,xk->czyk', volume, cos_x, precision=HIGHEST)
    imag_part = -jnp.einsum('czyx,xk->czyk', volume, sin_x, precision=HIGHEST)
    spectrum = jnp.stack([real_part, imag_part], axis=-1)
    spectrum = along(spectrum, 2, cos_y, sin_y, -1.0)
    spectrum = along(spectrum, 1, cos_z, sin_z, -1.0)
    spectrum = mode_product(spectrum, weights, False)
    spectrum = spectrum * kz_factor(jnp.arange(M, dtype=jnp.int32))[None, :, None, None, None]
    spectrum = along(spectrum, 1, cos_z.T, sin_z.T, 1.0)
    spectrum = along(spectrum, 2, cos_y.T, sin_y.T, 1.0)
    return jnp.einsum('ozyk,kx->ozyx', spectrum[..., 0], cos_x.T, precision=HIGHEST) - jnp.einsum('ozyk,kx->ozyx', spectrum[..., 1], sin_x.T, precision=HIGHEST)

def reference(activation, pointwise, bias_term, spectral_weight, cotangent):

    def layer(volume):
        mixed = jnp.einsum('co,czyx->ozyx', pointwise, volume, precision=HIGHEST)
        mixed = mixed + bias_term[:, None, None, None] + spectral(volume, spectral_weight)
        return jax.nn.gelu(mixed, approximate=False)
    output_field, pullback = jax.vjp(layer, activation)
    input_grad = pullback(cotangent)[0]
    return (output_field, input_grad)
```

```python
import functools
import math

import jax
import jax.numpy as jnp
import ml_dtypes
import numpy as np
from jax import lax
from jax.experimental import pallas as pl
from jax.experimental.pallas import tpu as pltpu
from jax.sharding import PartitionSpec as P

C = 20
M = 16
NX = 256
NY = 256
NZ = 128
GZ = 32
GY = 4
ND = GZ * GY
ZL = NZ // GZ
YL = NY // GY
CELLS = ZL * YL
LANES = 128
MAIN = 5
FULL = 10
ROWS = ND * FULL
WROWS = 160
MESH = pl.DeviceIdType.MESH
BF = jnp.bfloat16
F32 = jnp.float32


def _cos(k, n, length):
    return np.cos(2.0 * np.pi * ((k * n) % length) / length)


def _sin(k, n, length):
    return np.sin(2.0 * np.pi * ((k * n) % length) / length)


def _halves(table):
    high = table.astype(np.float32).astype(ml_dtypes.bfloat16)
    low = (table - high.astype(np.float64)).astype(ml_dtypes.bfloat16)
    return high, low


def _x_table():
    x = np.arange(NX)
    rows = np.zeros((64, NX))
    for p in range(M):
        rows[p] = _cos(p, x, NX)
        rows[16 + p] = _sin(p, x, NX) if p else _cos(16, x, NX)
    rows[32] = _sin(16, x, NX)
    return rows


def _y_table(gy):
    y = gy * YL + np.arange(YL)
    rows = np.zeros((144, ZL, YL))
    for q in range(8):
        basis = [
            _cos(q, y, NY),
            _sin(q, y, NY) if q else _cos(16, y, NY),
            _cos(q + 8, y, NY),
            _sin(q + 8, y, NY),
        ]
        for yb in range(4):
            for zl in range(ZL):
                rows[q * 16 + yb * 4 + zl, zl] = basis[yb]
    for s in range(4):
        for zl in range(ZL):
            rows[128 + s * 4 + zl, zl] = _sin(16, y, NY)
    return rows.reshape(144, CELLS)


def _mode_tables(p_zero, q_zero):
    xs = [([1, 0, 0], [0, 0, 0]), ([0, 1, 0], [0, 0, -1])] if p_zero else [([1, 0, 0], [0, 1, 0]), ([1, 0, 0], [0, -1, 0])]
    ys = [
        ([1, 0, 0, 0, 0], [0, 0, 0, 0, 0]),
        ([0, 1, 0, 0, 0], [0, 0, 0, 0, -1]),
    ] if q_zero else [([1, 0, 0, 0, 0], [0, 1, 0, 0, 0]), ([1, 0, 0, 0, 0], [0, -1, 0, 0, 0])]
    ys = ys + [([0, 0, 1, 0, 0], [0, 0, 0, 1, 0]), ([0, 0, 1, 0, 0], [0, 0, 0, -1, 0])]
    u = np.zeros((16, 8))
    v = np.zeros((16, 8))
    for i, (cx, sx) in enumerate(xs):
        for j, (cy, sy) in enumerate(ys):
            both_u = np.outer(cx, cy) - np.outer(sx, sy)
            both_v = np.outer(sx, cy) + np.outer(cx, sy)
            for xb in range(3):
                for yb in range(5):
                    if yb < 4:
                        slot = xb * 4 + yb
                    else:
                        slot = 12 + xb
                    u[slot, i * 4 + j] = both_u[xb, yb]
                    v[slot, i * 4 + j] = both_v[xb, yb]
    return u, v


def _mode_maps():
    g = np.zeros((4, 512, 256))
    gi = np.zeros((4, 256, 512))
    for variant in range(4):
        u, v = _mode_tables(variant // 2, variant % 2)
        gv = np.zeros((2, 2, 4, 8, 4, 2, 4, 8, 4))
        giv = np.zeros((2, 4, 8, 4, 2, 2, 4, 8, 4))
        for half in range(2):
            us = u[half * 8 : half * 8 + 8]
            vs = v[half * 8 : half * 8 + 8]
            for ch in range(4):
                for zl in range(4):
                    for rep in range(4):
                        gv[half, 0, ch, :, zl, 0, rep, :, ch] = us
                        gv[half, 1, ch, :, zl, 0, rep, :, ch] = -vs
                        gv[half, 0, ch, :, zl, 1, rep, :, ch] = -vs
                        gv[half, 1, ch, :, zl, 1, rep, :, ch] = -us
                        giv[0, rep, :, ch, half, 0, ch, :, zl] = us.T
                        giv[1, rep, :, ch, half, 0, ch, :, zl] = -vs.T
                        giv[0, rep, :, ch, half, 1, ch, :, zl] = -vs.T
                        giv[1, rep, :, ch, half, 1, ch, :, zl] = -us.T
        g[variant] = gv.reshape(512, 256)
        gi[variant] = giv.reshape(256, 512)
    return g.astype(ml_dtypes.bfloat16), gi.astype(ml_dtypes.bfloat16)


def _expand_maps():
    e = np.zeros((8, 4, 8, 4, 4, 32))
    for m in range(8):
        for ch in range(4):
            e[m, 0, m, ch, ch, :] = 1
    return e.reshape(8, 128, 128).astype(ml_dtypes.bfloat16)


def _pick_map():
    pick = np.zeros((32, 32))
    for q in range(8):
        for j, k in enumerate([q, (-q if q else -16), q + 8, -(q + 8)]):
            pick[j * 8 + q, k % 32] = 1
    return pick.astype(ml_dtypes.bfloat16)


@functools.cache
def tables():
    xh, xl = _halves(_x_table())
    tf = np.concatenate([xh, xl], axis=0)
    ti = np.concatenate([xh, xh, xl, np.zeros_like(xl)], axis=0)
    kf, ki = [], []
    for gy in range(GY):
        h, l = _halves(_y_table(gy))
        kf.append(np.concatenate([h, l], axis=0))
        ht, lt = h.T, l.T
        pad = np.zeros((CELLS, 80), ml_dtypes.bfloat16)
        ki.append(np.concatenate([ht[:, :128], lt[:, :128], ht[:, :128], ht[:, 128:], ht[:, 128:], lt[:, 128:], pad], axis=1))
    kz = np.arange(M)[:, None]
    far = 4 * (np.arange(ND)[None, :] // GY)
    h, l = _halves(np.concatenate([_cos(kz, far, NZ), _sin(kz, far, NZ)], axis=0))
    zf = np.concatenate([h, l], axis=0)
    far = 4 * np.arange(GZ)[None, :]
    factor = np.where(kz == 0, 1.0, 2.0) / float(NX * NY * NZ)
    h, l = _halves(np.concatenate([factor * _cos(kz, far, NZ), factor * _sin(kz, far, NZ)], axis=0).T)
    zi = np.concatenate([h, h, l], axis=1)
    near = np.arange(LANES)[None, :] % 4
    tw = np.stack([_cos(kz, near, NZ), _sin(kz, near, NZ)]).astype(np.float32)
    g, gi = _mode_maps()
    return dict(tf=tf, ti=ti, kf=np.stack(kf), ki=np.stack(ki), zf=zf, zi=zi, tw=tw, g=g, gi=gi, e=_expand_maps(), pick=_pick_map())


def nn(a, b):
    return lax.dot_general(a, b, (((1,), (0,)), ((), ())), preferred_element_type=F32)


def nt(a, b):
    return lax.dot_general(a, b, (((1,), (1,)), ((), ())), preferred_element_type=F32)


def halves(value):
    high = value.astype(BF)
    low = (value - high.astype(F32)).astype(BF)
    return high, low


def swap_blocks(tiles, width):
    tiles = list(tiles)
    lane = lax.broadcasted_iota(jnp.int32, tiles[0].shape, 1)
    block = lax.rem(lane // width, 8)
    for bit in (1, 2, 4):
        upper = lax.rem(block // bit, 2) == 1
        shift = bit * width
        for i in range(8):
            if i & bit:
                continue
            a, b = tiles[i], tiles[i | bit]
            tiles[i] = jnp.where(upper, pltpu.roll(b, shift, 1), a)
            tiles[i | bit] = jnp.where(upper, b, pltpu.roll(a, LANES - shift, 1))
    return tiles


def forward_channel(volume, kf, tf):
    ah, al = halves(volume)
    b = nn(kf, ah)
    b = b[:144] + b[144:] + nn(kf[:144], al)
    bh, bl = halves(b)
    o = nt(tf, bh)
    return o[:64] + o[64:] + nt(tf[:64], bl)


def put_channel(o, sx, c):
    for h in range(3):
        sx[c, h] = o[16 * h : 16 * h + 16, :128]
    group = lax.broadcasted_iota(jnp.int32, (16, 16), 1) // 4
    zero = jnp.zeros((16, 16), F32)
    e = zero
    for s in range(3):
        e = e + jnp.where(group == s, o[16 * s : 16 * s + 16, 128:144], zero)
    sx[c, 3, :, 0:16] = e


def pack(sx, sb):
    for r in range(MAIN):
        for half in range(2):
            tiles = [sx[4 * r + i // 2, 2 * half + i % 2] for i in range(8)]
            tiles = swap_blocks(tiles, 16)
            for q in range(8):
                sb[pl.ds(q * FULL + half * MAIN + r, 16, stride=8 * FULL), :] = tiles[q]


def unpack(rb, cx):
    for r in range(MAIN):
        for half in range(2):
            tiles = [rb[pl.ds(q * FULL + half * MAIN + r, 16, stride=8 * FULL), :] for q in range(8)]
            tiles = swap_blocks(tiles, 16)
            for i in range(8):
                cx[4 * r + i // 2, 2 * half + i % 2] = tiles[i]


def inverse_channel(cx, o, ki, ti):
    zero = jnp.zeros((16, LANES), F32)
    c = jnp.concatenate([cx[o, 0], cx[o, 1], cx[o, 2], zero], axis=0)
    e = cx[o, 3]
    group = lax.broadcasted_iota(jnp.int32, (16, LANES), 1) // 4
    e = jnp.concatenate([jnp.where(group == s, e, zero) for s in range(3)] + [zero], axis=0)
    ch, cl = halves(c)
    eh = e.astype(BF).astype(F32)
    el = (e - eh).astype(BF).astype(F32)
    ee = (eh + pltpu.roll(el, 16, 1) + pltpu.roll(eh, 32, 1)).astype(BF)
    one = jnp.concatenate([ch, ch], axis=1)
    two = jnp.concatenate([cl, ee], axis=1)
    one = jnp.concatenate([one, one], axis=0)
    two = jnp.concatenate([two, two], axis=0)
    h = nt(ki[:, :256], one) + nt(ki[:, 256:], two)
    hh = h.astype(BF)
    hl = (h - hh.astype(F32)).astype(BF)
    low = lax.broadcasted_iota(jnp.int32, h.shape, 1) < 64
    mix = jnp.where(low, hh.astype(F32), hl.astype(F32)).astype(BF)
    return nn(jnp.concatenate([mix, hh], axis=1), ti[...])


def owner_step(rb, sb, wt, g, gi, e_ref, zf, zi, tw, adjoint):
    d = jnp.concatenate([rb[pl.ds(r, ND, stride=FULL), :] for r in range(FULL)], axis=1)
    dh, dl = halves(d)
    zfv = zf[...]
    f = nn(zfv, dh)
    f = f[:32] + f[32:] + nn(zfv[:32], dl)
    cb = tw[0]
    sb_near = tw[1]

    def turned(r):
        fc = f[:16, r * LANES : (r + 1) * LANES]
        fs = f[16:, r * LANES : (r + 1) * LANES]
        return jnp.concatenate([fc * cb - fs * sb_near, fs * cb + fc * sb_near], axis=1)

    z = jnp.concatenate(
        [jnp.concatenate([turned(r), turned(r + MAIN)], axis=1) for r in range(MAIN)], axis=0
    )
    zh, zlow = halves(z)
    x = nn(jnp.concatenate([zh, zlow], axis=0), g[...])
    x = x[:80] + x[80:]
    xre, xim = x[:, :LANES], x[:, LANES:]

    def weight(ri, m, r):
        return wt[pl.ds(((ri * 8 + m) * MAIN + r) * 16, 16), :]

    zero = jnp.zeros((16, LANES), F32)
    if not adjoint:
        pieces = jnp.concatenate(halves(xre) + halves(xim), axis=0)
        yre, yim = [], []
        for m in range(8):
            xm = nn(pieces, e_ref[m])
            xmr = xm[:80] + xm[80:160]
            xmi = xm[160:240] + xm[240:]
            sr, si = zero, zero
            for r in range(MAIN):
                wr, wi = weight(0, m, r), weight(1, m, r)
                ar, ai = xmr[16 * r : 16 * r + 16], xmi[16 * r : 16 * r + 16]
                sr = sr + wr * ar - wi * ai
                si = si + wr * ai + wi * ar
            yre.append(sr)
            yim.append(si)
        vre = swap_blocks(yre, 4)[:MAIN]
        vim = swap_blocks(yim, 4)[:MAIN]
        v = jnp.concatenate([jnp.concatenate([a, b], axis=1) for a, b in zip(vre, vim)], axis=0)
    else:
        gre = swap_blocks([xre[16 * t : 16 * t + 16] for t in range(MAIN)] + [zero] * 3, 4)
        gim = swap_blocks([xim[16 * t : 16 * t + 16] for t in range(MAIN)] + [zero] * 3, 4)
        total = None
        for m in range(8):
            yr, yi = [], []
            for r in range(MAIN):
                wr, wi = weight(0, m, r), weight(1, m, r)
                yr.append(wr * gre[m] + wi * gim[m])
                yi.append(wr * gim[m] - wi * gre[m])
            pieces = jnp.concatenate(
                halves(jnp.concatenate(yr, axis=0)) + halves(jnp.concatenate(yi, axis=0)), axis=0
            )
            part = nt(pieces, e_ref[m])
            total = part if total is None else total + part
        v = jnp.concatenate([total[:80] + total[80:160], total[160:240] + total[240:]], axis=1)
    vh, vl = halves(v)
    c = nn(jnp.concatenate([vh, vl], axis=0), gi[...])
    c = c[:80] + c[80:]

    def back(t, half):
        cc = c[16 * t : 16 * t + 16, half * 256 : half * 256 + LANES]
        cs = c[16 * t : 16 * t + 16, half * 256 + LANES : half * 256 + 256]
        return jnp.concatenate([cc * cb + cs * sb_near, cs * cb - cc * sb_near], axis=0)

    r = jnp.concatenate([back(t, 0) for t in range(MAIN)] + [back(t, 1) for t in range(MAIN)], axis=1)
    rh, rl = halves(r)
    out = nn(zi[...], jnp.concatenate([rh, rl, rh], axis=0))
    for t in range(FULL):
        sb[pl.ds(t, GZ, stride=FULL), :] = out[:, t * LANES : (t + 1) * LANES]


def owner_of(z, y):
    i = z // 16
    p = lax.rem(z * (1 - 2 * i) + 32 * i, 16)
    h = lax.rem(i + p, 2)
    q = 4 * h + lax.rem(y + 8 - p // 2, 4)
    return p, i, q


def owner_device(p, q):
    i = lax.rem(q // 4 + p, 2)
    first = (16 - p) // 16
    z = p + i * (32 - 2 * p - 16 * first)
    y = lax.rem(lax.rem(q, 4) + p // 2, 4)
    return z, y


def is_extra(p, q):
    return p * q == 0


def layer_kernel(
    act, cot, w, pk, bias, tf, ti, kf, ki, zf, zi, tw, g, gi, e_ref, pick,
    out, pg, rb_out,
    av, cv, pm, kfv, kiv, gv, giv, sx, ws, wb, wt,
    sb1, rb1, sb2, rb2, sb3, rb3, sb4, rb4,
    act_sem, cot_sem, tab_sem, out_sem, pg_sem, end_sem, w_send, w_recv, send_sem, recv_sem,
):
    gz = lax.axis_index("gz")
    gy = lax.axis_index("gy")
    p, sign, q = owner_of(gz, gy)
    mine = p * 8 + q
    extra = is_extra(p, q)
    variant = 2 * ((16 - p) // 16) + (8 - q) // 8

    def act_copy(c):
        return pltpu.make_async_copy(act.at[c], av.at[c], act_sem.at[c])

    def cot_copy(c):
        return pltpu.make_async_copy(cot.at[c], cv.at[c], cot_sem.at[c])

    table_copies = [
        pltpu.make_async_copy(kf.at[gy], kfv, tab_sem.at[0]),
        pltpu.make_async_copy(ki.at[gy], kiv, tab_sem.at[1]),
        pltpu.make_async_copy(g.at[variant], gv, tab_sem.at[2]),
        pltpu.make_async_copy(gi.at[variant], giv, tab_sem.at[3]),
    ]
    table_copies[0].start()
    lax.fori_loop(0, C, lambda c, _: (act_copy(c).start(), 0)[1], 0)
    for copy in table_copies[1:]:
        copy.start()
    lax.fori_loop(0, C, lambda c, _: (cot_copy(c).start(), 0)[1], 0)

    rb1[...] = jnp.zeros_like(rb1)
    rb2[...] = jnp.zeros_like(rb2)
    rb3[...] = jnp.zeros_like(rb3)
    rb4[...] = jnp.zeros_like(rb4)
    sx[...] = jnp.zeros_like(sx)

    def peer(s):
        return lax.rem(gz + s // 4, GZ), lax.rem(gy + lax.rem(s, 4), GY)

    barrier = pltpu.get_barrier_semaphore()

    def greet(s, _):
        pl.semaphore_signal(barrier, 1, device_id=peer(s), device_id_type=MESH)
        return 0

    lax.fori_loop(1, ND, greet, 0)

    pickv = pick[...]

    def weight_rows(n, _):
        k = n // 2
        ri = lax.rem(n, 2)
        block = w[k, ri]
        block = jnp.concatenate([block, jnp.zeros((C, 12, 32), F32)], axis=1).reshape(C * 32, 32)
        bh, bl = halves(block)
        rows = nt(pickv, bh) + nt(pickv, bl)
        for j in range(4):
            for r in range(MAIN):
                ws[pl.ds(ri * 80 + (j * MAIN + r) * 4 + k, 8, stride=WROWS), :] = rows[
                    8 * j : 8 * j + 8, r * LANES : (r + 1) * LANES
                ]
        return 0

    lax.fori_loop(0, 8, weight_rows, 0)
    pl.semaphore_wait(barrier, ND - 1)

    slot = (sign * 4 + gy) * WROWS

    def send_weights(to, _):
        z, y = owner_device(p, to)

        @pl.when(to == q)
        def _():
            pltpu.make_async_copy(ws.at[pl.ds(to * WROWS, WROWS)], wb.at[pl.ds(slot, WROWS)], w_recv).start()

        @pl.when(to != q)
        def _():
            pltpu.make_async_remote_copy(
                src_ref=ws.at[pl.ds(to * WROWS, WROWS)],
                dst_ref=wb.at[pl.ds(slot, WROWS)],
                send_sem=w_send,
                recv_sem=w_recv,
                device_id=(z, y),
                device_id_type=MESH,
            ).start()

        return 0

    lax.fori_loop(0, 8, send_weights, 0)

    def exchange_out(n, src, dst):
        def send(s, _):
            z, y = peer(s)
            tp, _, tq = owner_of(z, y)
            to = tp * 8 + tq

            def start(rows):
                pltpu.make_async_remote_copy(
                    src_ref=src.at[pl.ds(to * FULL, rows)],
                    dst_ref=dst.at[pl.ds((gz * GY + gy) * FULL, rows)],
                    send_sem=send_sem.at[n],
                    recv_sem=recv_sem.at[n],
                    device_id=(z, y),
                    device_id_type=MESH,
                ).start()

            pl.when(is_extra(tp, tq))(lambda: start(FULL))
            pl.when(tp * tq != 0)(lambda: start(MAIN))
            return 0

        def keep(rows):
            pltpu.make_async_copy(
                src.at[pl.ds(mine * FULL, rows)], dst.at[pl.ds((gz * GY + gy) * FULL, rows)], recv_sem.at[n]
            ).start()

        pl.when(extra)(lambda: keep(FULL))
        pl.when(p * q != 0)(lambda: keep(MAIN))
        lax.fori_loop(1, ND, send, 0)

    def exchange_back(n, src, dst):
        def start_all(rows):
            def send(s, _):
                z, y = peer(s)
                pltpu.make_async_remote_copy(
                    src_ref=src.at[pl.ds(z * FULL, rows)],
                    dst_ref=dst.at[pl.ds(mine * FULL, rows)],
                    send_sem=send_sem.at[n],
                    recv_sem=recv_sem.at[n],
                    device_id=(z, y),
                    device_id_type=MESH,
                ).start()
                return 0

            pltpu.make_async_copy(
                src.at[pl.ds(gz * FULL, rows)], dst.at[pl.ds(mine * FULL, rows)], recv_sem.at[n]
            ).start()
            lax.fori_loop(1, ND, send, 0)

        pl.when(extra)(lambda: start_all(FULL))
        pl.when(p * q != 0)(lambda: start_all(MAIN))

    def await_rows(ref, rows, sem):
        pltpu.make_async_copy(ref.at[pl.ds(0, rows)], ref.at[pl.ds(0, rows)], sem).wait()

    def received_out(n, dst):
        pl.when(extra)(lambda: await_rows(dst, ND * FULL, recv_sem.at[n]))
        pl.when(p * q != 0)(lambda: await_rows(dst, ND * MAIN, recv_sem.at[n]))

    def received_back(n, dst):
        await_rows(dst, ND * MAIN + 23 * (FULL - MAIN), recv_sem.at[n])

    def sent_out(n, src):
        pl.when(extra)(lambda: await_rows(src, (ND - 1) * MAIN + 22 * (FULL - MAIN), send_sem.at[n]))
        pl.when(p * q != 0)(lambda: await_rows(src, (ND - 1) * MAIN + 23 * (FULL - MAIN), send_sem.at[n]))

    def sent_back(n, dst):
        pl.when(extra)(lambda: await_rows(dst, (ND - 1) * FULL, send_sem.at[n]))
        pl.when(p * q != 0)(lambda: await_rows(dst, (ND - 1) * MAIN, send_sem.at[n]))

    table_copies[0].wait()

    def first(c, _):
        act_copy(c).wait()
        put_channel(forward_channel(av[c], kfv[...], tf[...]), sx, c)
        return 0

    lax.fori_loop(0, C, first, 0)
    pack(sx, sb1)
    exchange_out(0, sb1, rb1)

    def mix(which, src, dst):
        ph, plow = halves(pk[which])
        both = jnp.concatenate([ph, plow], axis=0)

        def step(b, _):
            rows = pl.ds(pl.multiple_of(b * 8, 8), 8)
            sh, sl = halves(src[:, rows, :].reshape(C * 8, NX))
            o = nn(both, sh)
            o = o[: C * 8] + o[C * 8 :] + nn(ph, sl)
            dst[:, rows, :] = o.reshape(C, 8, NX)
            return 0

        lax.fori_loop(0, CELLS // 8, step, 0)

    mix(0, av, pm)
    for copy in table_copies[1:]:
        copy.wait()

    await_rows(wb, 8 * WROWS, w_recv)

    def spread(n, _):
        ri = n // 20
        j = lax.rem(n, 20) // MAIN
        r = lax.rem(n, MAIN)
        for k in range(4):
            v = wb[pl.ds(n * 4 + k, 8, stride=WROWS), :]
            base = ((ri * 8 + j) * MAIN + r) * 16 + k
            for i in range(2):
                wt[pl.ds(base + i * 4 * MAIN * 16, 4, stride=4), :] = v[4 * i : 4 * i + 4]
        return 0

    lax.fori_loop(0, 40, spread, 0)

    received_out(0, rb1)
    owner_step(rb1, sb2, wt, gv, giv, e_ref, zf, zi, tw, False)
    exchange_back(1, sb2, rb2)
    received_back(1, rb2)
    unpack(rb2, sx)

    def out_copy(o):
        return pltpu.make_async_copy(pm.at[o], out.at[o], out_sem.at[o])

    def middle(o, _):
        cot_copy(o).wait()
        mixed = pm[o] + bias[o] + inverse_channel(sx, o, kiv, ti)
        cdf = 0.5 * (1.0 + lax.erf(mixed * (1.0 / math.sqrt(2.0))))
        density = jnp.exp(-0.5 * mixed * mixed) * (1.0 / math.sqrt(2.0 * math.pi))
        pm[o] = mixed * cdf
        out_copy(o).start()
        grad = cv[o] * (cdf + mixed * density)
        cv[o] = grad
        put_channel(forward_channel(grad, kfv[...], tf[...]), sx, o)
        return 0

    lax.fori_loop(0, C, middle, 0)
    pack(sx, sb3)
    exchange_out(2, sb3, rb3)
    mix(1, cv, av)

    def pg_copy(c):
        return pltpu.make_async_copy(av.at[c], pg.at[c], pg_sem.at[c])

    lax.fori_loop(0, C, lambda c, _: (pg_copy(c).start(), 0)[1], 0)
    received_out(2, rb3)
    owner_step(rb3, sb4, wt, gv, giv, e_ref, zf, zi, tw, True)
    exchange_back(3, sb4, rb4)
    lax.fori_loop(0, C, lambda c, _: (out_copy(c).wait(), 0)[1], 0)
    lax.fori_loop(0, C, lambda c, _: (pg_copy(c).wait(), 0)[1], 0)
    sent_out(0, sb1)
    sent_back(1, rb2)
    sent_out(2, sb3)
    await_rows(ws, 7 * WROWS, w_send)
    received_back(3, rb4)
    end = pltpu.make_async_copy(rb4, rb_out, end_sem)
    end.start()
    end.wait()
    sent_back(3, rb1)


def final_kernel(rb, pg, tmp, ti, ki, out, grad, cx, kiv, sem):
    gy = lax.axis_index("gy")
    step = pl.program_id(0)
    move = pltpu.make_async_copy(tmp, out, sem.at[0])

    @pl.when(step == 0)
    def _():
        move.start()
        table = pltpu.make_async_copy(ki.at[gy], kiv, sem.at[1])
        table.start()
        unpack(rb, cx)
        table.wait()

    grad[0] = pg[0] + inverse_channel(cx, step, kiv, ti)

    @pl.when(step == pl.num_programs(0) - 1)
    def _():
        move.wait()


def local(activation, pointwise, bias_term, spectral_weight, cotangent):
    t = {name: jnp.asarray(value) for name, value in tables().items()}
    eye = jnp.eye(8, dtype=F32)
    pk = jnp.stack(
        [
            (pointwise.T[:, None, :, None] * eye[None, :, None, :]).reshape(C * 8, C * 8),
            (pointwise[:, None, :, None] * eye[None, :, None, :]).reshape(C * 8, C * 8),
        ]
    )
    volume = (C, CELLS, NX)
    any_spec = pl.BlockSpec(memory_space=pl.ANY)
    vmem = pl.BlockSpec(memory_space=pltpu.VMEM)
    smem = pl.BlockSpec(memory_space=pltpu.SMEM)
    message = pltpu.VMEM((ROWS, LANES), F32)
    dma = pltpu.SemaphoreType.DMA
    tmp, pg, rb = pl.pallas_call(
        layer_kernel,
        out_shape=[
            jax.ShapeDtypeStruct(volume, F32),
            jax.ShapeDtypeStruct(volume, F32),
            jax.ShapeDtypeStruct((ROWS, LANES), F32),
        ],
        in_specs=[
            any_spec, any_spec, vmem, vmem, smem,
            vmem, vmem, any_spec, any_spec, vmem, vmem, vmem, any_spec, any_spec, vmem, vmem,
        ],
        out_specs=[any_spec, any_spec, any_spec],
        scratch_shapes=[
            pltpu.VMEM(volume, F32),
            pltpu.VMEM(volume, F32),
            pltpu.VMEM(volume, F32),
            pltpu.VMEM((288, CELLS), BF),
            pltpu.VMEM((CELLS, 512), BF),
            pltpu.VMEM((512, 256), BF),
            pltpu.VMEM((256, 512), BF),
            pltpu.VMEM((C, 4, 16, LANES), F32),
            message,
            message,
            message,
        ]
        + [message] * 8
        + [dma((C,)), dma((C,)), dma((4,)), dma((C,)), dma((C,)), dma, dma, dma, dma((4,)), dma((4,))],
        compiler_params=pltpu.CompilerParams(
            collective_id=0, has_side_effects=True, vmem_limit_bytes=56 * 1024 * 1024
        ),
        name="layer",
    )(
        activation.reshape(volume), cotangent.reshape(volume), spectral_weight.reshape(4, 2, C, C, 32), pk, bias_term,
        t["tf"], t["ti"], t["kf"], t["ki"], t["zf"], t["zi"], t["tw"], t["g"], t["gi"], t["e"], t["pick"],
    )
    block = pl.BlockSpec((1, CELLS, NX), lambda i: (i, 0, 0))
    out, grad = pl.pallas_call(
        final_kernel,
        grid=(C,),
        out_shape=[jax.ShapeDtypeStruct(volume, F32), jax.ShapeDtypeStruct(volume, F32)],
        in_specs=[vmem, block, any_spec, vmem, any_spec],
        out_specs=[any_spec, block],
        scratch_shapes=[pltpu.VMEM((C, 4, 16, LANES), F32), pltpu.VMEM((CELLS, 512), BF), dma((2,))],
        compiler_params=pltpu.CompilerParams(vmem_limit_bytes=32 * 1024 * 1024),
        name="final",
    )(rb, pg, tmp, t["ti"], t["ki"])
    shape = (C, ZL, YL, NX)
    return out.reshape(shape), grad.reshape(shape)


def solution(mesh):
    return jax.shard_map(
        local,
        mesh=mesh,
        in_specs=(
            P(None, "gz", "gy", None),
            P(),
            P(),
            P("gz", "gy", None, None, None, None),
            P(None, "gz", "gy", None),
        ),
        out_specs=(P(None, "gz", "gy", None), P(None, "gz", "gy", None)),
        check_vma=False,
    )
```

```python
import functools
import math

import jax
import jax.numpy as jnp
import ml_dtypes
import numpy as np
from jax import lax
from jax.experimental import pallas as pl
from jax.experimental.pallas import tpu as pltpu
from jax.sharding import PartitionSpec as P

C = 20
M = 16
NX = 256
NY = 256
NZ = 128
GZ = 32
GY = 4
ND = GZ * GY
ZL = NZ // GZ
YL = NY // GY
CELLS = ZL * YL
LANES = 128
PAIRS = C // 2
MAIN = 5
FULL = 10
WROWS = 160
WIN = ZL * C * C * 2
MESH = pl.DeviceIdType.MESH
BF = jnp.bfloat16
F32 = jnp.float32


def _cos(k, n, length):
    return np.cos(2.0 * np.pi * ((k * n) % length) / length)


def _sin(k, n, length):
    return np.sin(2.0 * np.pi * ((k * n) % length) / length)


def _halves(table):
    high = table.astype(np.float32).astype(ml_dtypes.bfloat16)
    low = (table - high.astype(np.float64)).astype(ml_dtypes.bfloat16)
    return high, low


def _x_table():
    x = np.arange(NX)
    rows = np.zeros((64, NX))
    for p in range(M):
        rows[p] = _cos(p, x, NX)
        rows[16 + p] = _sin(p, x, NX) if p else _cos(16, x, NX)
    rows[32] = _sin(16, x, NX)
    return rows


def _y_table(gy):
    y = gy * YL + np.arange(YL)
    rows = np.zeros((144, ZL, YL))
    for q in range(8):
        basis = [
            _cos(q, y, NY),
            _sin(q, y, NY) if q else _cos(16, y, NY),
            _cos(q + 8, y, NY),
            _sin(q + 8, y, NY),
        ]
        for yb in range(4):
            for zl in range(ZL):
                rows[q * 16 + yb * 4 + zl, zl] = basis[yb]
    for s in range(4):
        for zl in range(ZL):
            rows[128 + s * 4 + zl, zl] = _sin(16, y, NY)
    return rows.reshape(144, CELLS)


def _mode_tables(p_zero, q_zero):
    xs = [([1, 0, 0], [0, 0, 0]), ([0, 1, 0], [0, 0, -1])] if p_zero else [([1, 0, 0], [0, 1, 0]), ([1, 0, 0], [0, -1, 0])]
    ys = [
        ([1, 0, 0, 0, 0], [0, 0, 0, 0, 0]),
        ([0, 1, 0, 0, 0], [0, 0, 0, 0, -1]),
    ] if q_zero else [([1, 0, 0, 0, 0], [0, 1, 0, 0, 0]), ([1, 0, 0, 0, 0], [0, -1, 0, 0, 0])]
    ys = ys + [([0, 0, 1, 0, 0], [0, 0, 0, 1, 0]), ([0, 0, 1, 0, 0], [0, 0, 0, -1, 0])]
    u = np.zeros((16, 8))
    v = np.zeros((16, 8))
    for i, (cx, sx) in enumerate(xs):
        for j, (cy, sy) in enumerate(ys):
            both_u = np.outer(cx, cy) - np.outer(sx, sy)
            both_v = np.outer(sx, cy) + np.outer(cx, sy)
            for xb in range(3):
                for yb in range(5):
                    if yb < 4:
                        slot = xb * 4 + yb
                    else:
                        slot = 12 + xb
                    u[slot, i * 4 + j] = both_u[xb, yb]
                    v[slot, i * 4 + j] = both_v[xb, yb]
    return u, v


def _mode_maps():
    g = np.zeros((4, 512, 256))
    gi = np.zeros((4, 256, 512))
    for variant in range(4):
        u, v = _mode_tables(variant // 2, variant % 2)
        gv = np.zeros((2, 2, 4, 8, 4, 2, 4, 8, 4))
        giv = np.zeros((2, 4, 8, 4, 2, 2, 4, 8, 4))
        for half in range(2):
            us = u[half * 8 : half * 8 + 8]
            vs = v[half * 8 : half * 8 + 8]
            for ch in range(4):
                for zl in range(4):
                    for rep in range(4):
                        gv[half, 0, ch, :, zl, 0, rep, :, ch] = us
                        gv[half, 1, ch, :, zl, 0, rep, :, ch] = -vs
                        gv[half, 0, ch, :, zl, 1, rep, :, ch] = -vs
                        gv[half, 1, ch, :, zl, 1, rep, :, ch] = -us
                        giv[0, rep, :, ch, half, 0, ch, :, zl] = us.T
                        giv[1, rep, :, ch, half, 0, ch, :, zl] = -vs.T
                        giv[0, rep, :, ch, half, 1, ch, :, zl] = -vs.T
                        giv[1, rep, :, ch, half, 1, ch, :, zl] = -us.T
        g[variant] = gv.reshape(512, 256)
        gi[variant] = giv.reshape(256, 512)
    return g.astype(ml_dtypes.bfloat16), gi.astype(ml_dtypes.bfloat16)


def _expand_maps():
    e = np.zeros((8, 4, 8, 4, 4, 32))
    for m in range(8):
        for ch in range(4):
            e[m, 0, m, ch, ch, :] = 1
    return e.reshape(8, 128, 128).astype(ml_dtypes.bfloat16)


def _pick_map():
    pick = np.zeros((32, 32))
    for q in range(8):
        for j, k in enumerate([q, (-q if q else -16), q + 8, -(q + 8)]):
            pick[j * 8 + q, k % 32] = 1
    return pick.astype(ml_dtypes.bfloat16)


@functools.cache
def tables():
    xh, xl = _halves(_x_table())
    tf = np.zeros((2, NX, 256), ml_dtypes.bfloat16)
    for j in range(2):
        tf[j, :, 64 * j : 64 * j + 64] = xh.T
        tf[j, :, 128 + 64 * j : 192 + 64 * j] = xl.T
    ti = np.concatenate([xh, xh, xl, np.zeros_like(xl)], axis=0)
    kf, ki = [], []
    for gy in range(GY):
        h, l = _halves(_y_table(gy))
        kf.append(np.concatenate([h, l], axis=0))
        ht, lt = h.T, l.T
        pad = np.zeros((CELLS, 80), ml_dtypes.bfloat16)
        ki.append(np.concatenate([ht[:, :128], lt[:, :128], ht[:, :128], ht[:, 128:], ht[:, 128:], lt[:, 128:], pad], axis=1))
    kz = np.arange(M)[:, None]
    far = 4 * (np.arange(ND)[None, :] // GY)
    h, l = _halves(np.concatenate([_cos(kz, far, NZ), _sin(kz, far, NZ)], axis=0))
    zf = np.concatenate([h, l], axis=0)
    far = 4 * np.arange(GZ)[None, :]
    factor = np.where(kz == 0, 1.0, 2.0) / float(NX * NY * NZ)
    h, l = _halves(np.concatenate([factor * _cos(kz, far, NZ), factor * _sin(kz, far, NZ)], axis=0).T)
    zi = np.concatenate([h, h, l], axis=1)
    near = np.arange(LANES)[None, :] % 4
    tw = np.stack([_cos(kz, near, NZ), _sin(kz, near, NZ)]).astype(np.float32)
    g, gi = _mode_maps()
    return dict(tf=tf, ti=ti, kf=np.stack(kf), ki=np.stack(ki), zf=zf, zi=zi, tw=tw, g=g, gi=gi, e=_expand_maps(), pick=_pick_map())


def nn(a, b):
    return lax.dot_general(a, b, (((1,), (0,)), ((), ())), preferred_element_type=F32)


def nt(a, b):
    return lax.dot_general(a, b, (((1,), (1,)), ((), ())), preferred_element_type=F32)


def halves(value):
    high = value.astype(BF)
    low = (value - high.astype(F32)).astype(BF)
    return high, low


def lanes_of(value):
    return lax.broadcasted_iota(jnp.int32, value.shape, 1)


def swap_blocks(tiles, width):
    tiles = list(tiles)
    block = lax.rem(lanes_of(tiles[0]) // width, 8)
    for bit in (1, 2, 4):
        upper = lax.rem(block // bit, 2) == 1
        shift = bit * width
        for i in range(8):
            if i & bit:
                continue
            a, b = tiles[i], tiles[i | bit]
            tiles[i] = jnp.where(upper, pltpu.roll(b, shift, 1), a)
            tiles[i | bit] = jnp.where(upper, b, pltpu.roll(a, LANES - shift, 1))
    return tiles


def forward_pair(pair, kf, tf, sx, ey, n):
    parts = []
    for volume in pair:
        ah, al = halves(volume)
        b = nn(kf[...], ah)
        parts.append(halves(b[:144] + b[144:] + nn(kf[:144], al)))
    (h0, l0), (h1, l1) = parts
    o = nn(h0, tf[0]) + nn(h1, tf[1])
    o = o[:, :LANES] + o[:, LANES:] + nn(l0, tf[0, :, :LANES]) + nn(l1, tf[1, :, :LANES])
    sx[n] = o[:LANES].T
    ey[pl.ds(pl.multiple_of(n * 16, 16), 16), :] = o[LANES:]


def pack(sx, ey, sb):
    for r in range(MAIN):
        tiles = swap_blocks([sx[2 * r + i // 4, pl.ds((i // 2 % 2) * 64 + (i % 2) * 16, 16), :] for i in range(8)], 16)
        for q in range(8):
            sb[r, 16 * q : 16 * q + 16, :] = tiles[q]
    turned = [ey[0:LANES, :].T, ey[LANES : 2 * LANES, :].T]
    slot = lax.rem(lax.broadcasted_iota(jnp.int32, (16, LANES), 1) // 4, 4)
    block = lax.broadcasted_iota(jnp.int32, (16, LANES), 1) // 16
    zero = jnp.zeros((16, LANES), F32)
    by_ch = [
        [
            sum((jnp.where(slot == h, t[64 * ch + 16 * h : 64 * ch + 16 * h + 16], zero) for h in range(3)), zero)
            for ch in range(2)
        ]
        for t in turned
    ]
    none = jnp.zeros((8, LANES), F32)
    for r in range(MAIN):
        tiles = []
        for c in range(4):
            tiles += [sx[2 * r + c // 2, pl.ds((c % 2) * 64 + 32, 8), :], none]
        tiles = swap_blocks(tiles, 16)
        first = zero
        for c in range(4):
            n = 2 * r + c // 2
            moved = pltpu.roll(by_ch[n // 8][c % 2], (2 * c + 1 - n % 8) % 8 * 16, 1)
            first = first + jnp.where(block == 2 * c + 1, moved, zero)
        sb[MAIN + r, 0:8, :] = first[:8] + tiles[0]
        sb[MAIN + r, 8:16, :] = first[8:]
        for q in range(1, 8):
            sb[MAIN + r, 16 * q : 16 * q + 8, :] = tiles[q]


def unpack(rb, cx, ex):
    for r in range(MAIN):
        tiles = swap_blocks([rb[r, 16 * q : 16 * q + 16, :] for q in range(8)], 16)
        for i in range(8):
            cx[2 * r + i // 4, pl.ds((i // 2 % 2) * 64 + (i % 2) * 16, 16), :] = tiles[i]
        tiles = swap_blocks([rb[MAIN + r, 16 * q : 16 * q + 8, :] for q in range(8)], 16)
        for c in range(4):
            cx[2 * r + c // 2, pl.ds((c % 2) * 64 + 32, 8), :] = tiles[2 * c]
    rows = [rb[MAIN + r, 0:16, :] for r in range(MAIN)] + [jnp.zeros((48, LANES), F32)]
    turned = jnp.concatenate(rows, axis=0).T
    row = lax.broadcasted_iota(jnp.int32, (16, LANES), 0)
    block = lax.broadcasted_iota(jnp.int32, (16, LANES), 1) // 16
    keep = lax.rem(block, 4) == row // 4
    zero = jnp.zeros((16, LANES), F32)
    for r in range(MAIN):
        for c in range(4):
            e = jnp.where(block == r, turned[32 * c + 16 : 32 * c + 32], zero)
            for shift in (16, 32, 64):
                e = e + pltpu.roll(e, shift, 1)
            ex[2 * r + c // 2, pl.ds((c % 2) * 16, 16), :] = jnp.where(keep, e, zero)


def clear_rest(cx):
    for n in range(PAIRS):
        for ch in range(2):
            cx[n, pl.ds(64 * ch + 40, 24), :] = jnp.zeros((24, LANES), F32)


def inverse_pair(cx, ex, n, ki, ti):
    c = cx[n].T
    low = lanes_of(c) < 64
    other = pltpu.roll(c, 64, 1)
    d = jnp.concatenate([jnp.where(low, c, other), jnp.where(low, other, c)], axis=1)
    dh, dl = halves(d)
    e = ex[n]
    eh, el = halves(jnp.concatenate([e[:16], e[16:]], axis=1))
    one = jnp.concatenate([dh, dh], axis=0)
    two = jnp.concatenate([dl, eh, el, eh, jnp.zeros((80, 256), BF)], axis=0)
    h = nn(ki[:, :256], one) + nn(ki[:, 256:], two)
    hh, hl = halves(h)
    out = []
    for j in range(2):
        high = hh[:, LANES * j : LANES * j + LANES]
        rest = hl[:, LANES * j : LANES * j + LANES]
        mix = jnp.where(lanes_of(high) < 64, high.astype(F32), rest.astype(F32)).astype(BF)
        out.append(nn(jnp.concatenate([mix, high], axis=1), ti[...]))
    return out


def owner_step(rb, sb, wt, g, gi, e_ref, zf, zi, tw, adjoint):
    d = jnp.concatenate([rb[r] for r in range(FULL)], axis=1)
    dh, dl = halves(d)
    zfv = zf[...]
    f = nn(zfv, dh)
    f = f[:32] + f[32:] + nn(zfv[:32], dl)
    cb = tw[0]
    sb_near = tw[1]

    def turned(r):
        fc = f[:16, r * LANES : (r + 1) * LANES]
        fs = f[16:, r * LANES : (r + 1) * LANES]
        return jnp.concatenate([fc * cb - fs * sb_near, fs * cb + fc * sb_near], axis=1)

    z = jnp.concatenate(
        [jnp.concatenate([turned(r), turned(r + MAIN)], axis=1) for r in range(MAIN)], axis=0
    )
    zh, zlow = halves(z)
    x = nn(jnp.concatenate([zh, zlow], axis=0), g[...])
    x = x[:80] + x[80:]
    xre, xim = x[:, :LANES], x[:, LANES:]

    def weight(ri, m, r):
        return wt[pl.ds(((ri * 8 + m) * MAIN + r) * 16, 16), :]

    zero = jnp.zeros((16, LANES), F32)
    if not adjoint:
        pieces = jnp.concatenate(halves(xre) + halves(xim), axis=0)
        yre, yim = [], []
        for m in range(8):
            xm = nn(pieces, e_ref[m])
            xmr = xm[:80] + xm[80:160]
            xmi = xm[160:240] + xm[240:]
            sr, si = zero, zero
            for r in range(MAIN):
                wr, wi = weight(0, m, r), weight(1, m, r)
                ar, ai = xmr[16 * r : 16 * r + 16], xmi[16 * r : 16 * r + 16]
                sr = sr + wr * ar - wi * ai
                si = si + wr * ai + wi * ar
            yre.append(sr)
            yim.append(si)
        vre = swap_blocks(yre, 4)[:MAIN]
        vim = swap_blocks(yim, 4)[:MAIN]
        v = jnp.concatenate([jnp.concatenate([a, b], axis=1) for a, b in zip(vre, vim)], axis=0)
    else:
        gre = swap_blocks([xre[16 * t : 16 * t + 16] for t in range(MAIN)] + [zero] * 3, 4)
        gim = swap_blocks([xim[16 * t : 16 * t + 16] for t in range(MAIN)] + [zero] * 3, 4)
        total = None
        for m in range(8):
            yr, yi = [], []
            for r in range(MAIN):
                wr, wi = weight(0, m, r), weight(1, m, r)
                yr.append(wr * gre[m] + wi * gim[m])
                yi.append(wr * gim[m] - wi * gre[m])
            pieces = jnp.concatenate(
                halves(jnp.concatenate(yr, axis=0)) + halves(jnp.concatenate(yi, axis=0)), axis=0
            )
            part = nt(pieces, e_ref[m])
            total = part if total is None else total + part
        v = jnp.concatenate([total[:80] + total[80:160], total[160:240] + total[240:]], axis=1)
    vh, vl = halves(v)
    c = nn(jnp.concatenate([vh, vl], axis=0), gi[...])
    c = c[:80] + c[80:]

    def back(t, half):
        cc = c[16 * t : 16 * t + 16, half * 256 : half * 256 + LANES]
        cs = c[16 * t : 16 * t + 16, half * 256 + LANES : half * 256 + 256]
        return jnp.concatenate([cc * cb + cs * sb_near, cs * cb - cc * sb_near], axis=0)

    r = jnp.concatenate([back(t, 0) for t in range(MAIN)] + [back(t, 1) for t in range(MAIN)], axis=1)
    rh, rl = halves(r)
    out = nn(zi[...], jnp.concatenate([rh, rl, rh], axis=0))
    for t in range(FULL):
        sb[t] = out[:, t * LANES : (t + 1) * LANES]


def owner_of(z):
    i = z // 16
    p = lax.rem(z * (1 - 2 * i) + 32 * i, 16)
    return p, i, lax.rem(i + p, 2)


def group_of(p, h, y):
    return 4 * h + lax.rem(y + 8 - p // 2, 4)


def owner_device(p, q):
    i = lax.rem(q // 4 + p, 2)
    first = (16 - p) // 16
    z = p + i * (32 - 2 * p - 16 * first)
    y = lax.rem(lax.rem(q, 4) + p // 2, 4)
    return z, y


def weight_step(wv, ws, pick, k):
    for ri in range(2):
        block = jnp.concatenate([wv[pl.ds(k * 800 + c * 40 + ri, 32, stride=2), :] for c in range(C)], axis=0)
        bh, bl = halves(block)
        rows = nt(pick, bh) + nt(pick, bl)
        for j in range(4):
            for r in range(MAIN):
                ws[pl.ds(ri * 80 + (j * MAIN + r) * 4 + k, 8, stride=WROWS), :] = rows[
                    8 * j : 8 * j + 8, r * LANES : (r + 1) * LANES
                ]


def weight_spread(wb, wt, n):
    ri = n // 20
    j = lax.rem(n, 20) // MAIN
    r = lax.rem(n, MAIN)
    for k in range(4):
        v = wb[pl.ds(n * 4 + k, 8, stride=WROWS), :]
        base = ((ri * 8 + j) * MAIN + r) * 16 + k
        for i in range(2):
            wt[pl.ds(base + i * 4 * MAIN * 16, 4, stride=4), :] = v[4 * i : 4 * i + 4]


def mix_maps(pw):
    ones = jnp.where(
        lax.broadcasted_iota(jnp.int32, (C * 8, C), 0) // 8 == lax.broadcasted_iota(jnp.int32, (C * 8, C), 1), 1.0, 0.0
    ).astype(BF)
    shape = (C * 8, C * 8)
    same = lax.rem(lax.broadcasted_iota(jnp.int32, shape, 0), 8) == lax.rem(lax.broadcasted_iota(jnp.int32, shape, 1), 8)
    fwd, adj = [], []
    for part in halves(pw[...]):
        rows = nn(ones, part).astype(BF)
        fwd.append(jnp.where(same, nt(ones, rows), 0.0).astype(BF))
        adj.append(jnp.where(same, nt(rows, ones), 0.0).astype(BF))
    return jnp.concatenate(fwd, axis=0), jnp.concatenate(adj, axis=0)


def mix_step(maps, src, dst, b):
    rows = pl.ds(pl.multiple_of(b * 8, 8), 8)
    sh, sl = halves(src[:, rows, :].reshape(C * 8, NX))
    o = nn(maps[...], sh)
    o = o[: C * 8] + o[C * 8 :] + nn(maps[: C * 8], sl)
    dst[:, rows, :] = o.reshape(C, 8, NX)


def activate(mixed):
    cdf = 0.5 * (1.0 + lax.erf(mixed * (1.0 / math.sqrt(2.0))))
    density = jnp.exp(-0.5 * mixed * mixed) * (1.0 / math.sqrt(2.0 * math.pi))
    return mixed * cdf, cdf + mixed * density


def loop(first, last, fn, unroll=1):
    def body(i, carry):
        fn(i)
        return carry

    lax.fori_loop(first, last, body, 0, unroll=unroll)


def layer_kernel(
    act, cot, w, pw, bias, tf, ti, kf, ki, zf, zi, tw, g, gi, e_ref, pick,
    out, pg, rb_out,
    av, cv, pm, kfv, kiv, gv, giv, maps, sx, ey, cx, ex, wv, ws, wb, wt,
    sb1, rb1, sb2, rb2, sb3, rb3, sb4, rb4,
    act_sem, cot_sem, tab_sem, out_sem, pg_sem, end_sem, w_send, w_recv, send_sem, recv_sem,
):
    gz = lax.axis_index("gz")
    gy = lax.axis_index("gy")
    p, sign, h = owner_of(gz)
    q = group_of(p, h, gy)
    mine = q * 16 + p
    extra = p * q == 0
    variant = 2 * ((16 - p) // 16) + (8 - q) // 8

    def act_copy(c):
        return pltpu.make_async_copy(act.at[c], av.at[c], act_sem.at[c])

    def cot_copy(c):
        return pltpu.make_async_copy(cot.at[c], cv.at[c], cot_sem.at[c])

    table_copies = [
        pltpu.make_async_copy(kf.at[gy], kfv, tab_sem.at[0]),
        pltpu.make_async_copy(ki.at[gy], kiv, tab_sem.at[1]),
        pltpu.make_async_copy(g.at[variant], gv, tab_sem.at[2]),
        pltpu.make_async_copy(gi.at[variant], giv, tab_sem.at[3]),
        pltpu.make_async_copy(w, wv.at[pl.ds(0, WIN)], tab_sem.at[4]),
    ]
    table_copies[0].start()
    loop(0, 8, lambda c: act_copy(c).start())
    table_copies[4].start()
    loop(8, C, lambda c: act_copy(c).start())
    for copy in table_copies[1:4]:
        copy.start()
    loop(0, C, lambda c: cot_copy(c).start())

    for rb in (rb1, rb2, rb3, rb4):
        rb[MAIN:] = jnp.zeros((MAIN, ND, LANES), F32)

    next_y = [gy] + [lax.rem(gy + j, GY) for j in range(1, GY)]

    def each_peer(fn, per_z):
        own = per_z(gz)
        for j in range(1, GY):
            fn(gz, next_y[j], own)

        def body(_, z):
            z = z + 1
            z = jnp.where(z == GZ, 0, z)
            known = per_z(z)
            for j in range(GY):
                fn(z, next_y[j], known)
            return z

        lax.fori_loop(1, GZ, body, gz)

    barrier = pltpu.get_barrier_semaphore()
    each_peer(
        lambda z, y, _: pl.semaphore_signal(barrier, 1, device_id=(z, y), device_id_type=MESH), lambda z: None
    )

    def exchange_out(n, src, dst):
        def start(z, y, to, rows):
            pltpu.make_async_remote_copy(
                src_ref=src.at[pl.ds(0, rows), to],
                dst_ref=dst.at[pl.ds(0, rows), gz * GY + gy],
                send_sem=send_sem.at[n],
                recv_sem=recv_sem.at[n],
                device_id=(z, y),
                device_id_type=MESH,
            ).start()

        def send(z, y, known):
            tp, _, th = known
            tq = group_of(tp, th, y)
            to = tq * 16 + tp
            some = tp * tq
            pl.when(some == 0)(lambda: start(z, y, to, FULL))
            pl.when(some != 0)(lambda: start(z, y, to, MAIN))

        def keep(rows):
            pltpu.make_async_copy(
                src.at[pl.ds(0, rows), mine], dst.at[pl.ds(0, rows), gz * GY + gy], recv_sem.at[n]
            ).start()

        pl.when(extra)(lambda: keep(FULL))
        pl.when(p * q != 0)(lambda: keep(MAIN))
        each_peer(send, owner_of)

    def exchange_back(n, src, dst):
        def start_all(rows):
            def send(z, y, _):
                pltpu.make_async_remote_copy(
                    src_ref=src.at[pl.ds(0, rows), z],
                    dst_ref=dst.at[pl.ds(0, rows), mine],
                    send_sem=send_sem.at[n],
                    recv_sem=recv_sem.at[n],
                    device_id=(z, y),
                    device_id_type=MESH,
                ).start()

            pltpu.make_async_copy(src.at[pl.ds(0, rows), gz], dst.at[pl.ds(0, rows), mine], recv_sem.at[n]).start()
            each_peer(send, lambda z: None)

        pl.when(extra)(lambda: start_all(FULL))
        pl.when(p * q != 0)(lambda: start_all(MAIN))

    def await_rows(rows, sem):
        pltpu.make_async_copy(ws.at[pl.ds(0, rows)], wb.at[pl.ds(0, rows)], sem).wait()

    def received_out(n):
        pl.when(extra)(lambda: await_rows(ND * FULL, recv_sem.at[n]))
        pl.when(p * q != 0)(lambda: await_rows(ND * MAIN, recv_sem.at[n]))

    def received_back(n):
        await_rows(ND * MAIN + 23 * (FULL - MAIN), recv_sem.at[n])

    def sent_out(n):
        pl.when(extra)(lambda: await_rows((ND - 1) * MAIN + 22 * (FULL - MAIN), send_sem.at[n]))
        pl.when(p * q != 0)(lambda: await_rows((ND - 1) * MAIN + 23 * (FULL - MAIN), send_sem.at[n]))

    def sent_back(n):
        pl.when(extra)(lambda: await_rows((ND - 1) * FULL, send_sem.at[n]))
        pl.when(p * q != 0)(lambda: await_rows((ND - 1) * MAIN, send_sem.at[n]))

    wv[pl.ds(WIN, 64), :] = jnp.zeros((64, 32), F32)
    table_copies[0].wait()

    def first(n):
        act_copy(2 * n).wait()
        act_copy(2 * n + 1).wait()
        forward_pair([av[2 * n], av[2 * n + 1]], kfv, tf, sx, ey, n)

    loop(0, 4, first, 2)
    table_copies[4].wait()
    pickv = pick[...]
    loop(0, 4, lambda k: weight_step(wv, ws, pickv, k))
    pl.semaphore_wait(barrier, ND - 1)

    slot = (sign * 4 + gy) * WROWS

    def send_weights(to):
        z, y = owner_device(p, to)

        @pl.when(to == q)
        def _():
            pltpu.make_async_copy(ws.at[pl.ds(to * WROWS, WROWS)], wb.at[pl.ds(slot, WROWS)], w_recv).start()

        @pl.when(to != q)
        def _():
            pltpu.make_async_remote_copy(
                src_ref=ws.at[pl.ds(to * WROWS, WROWS)],
                dst_ref=wb.at[pl.ds(slot, WROWS)],
                send_sem=w_send,
                recv_sem=w_recv,
                device_id=(z, y),
                device_id_type=MESH,
            ).start()

    loop(0, 8, send_weights)
    loop(4, PAIRS, first, 2)
    pack(sx, ey, sb1)
    exchange_out(0, sb1, rb1)

    fwd, adj = mix_maps(pw)
    maps[0] = fwd
    maps[1] = adj
    steps = CELLS // 8
    loop(0, steps // 2, lambda b: mix_step(maps.at[0], av, pm, b), 2)
    for copy in table_copies[1:4]:
        copy.wait()
    clear_rest(cx)
    await_rows(8 * WROWS, w_recv)
    loop(0, 40, lambda n: weight_spread(wb, wt, n), 4)

    received_out(0)
    owner_step(rb1, sb2, wt, gv, giv, e_ref, zf, zi, tw, False)
    exchange_back(1, sb2, rb2)
    loop(steps // 2, steps, lambda b: mix_step(maps.at[0], av, pm, b), 2)
    received_back(1)
    unpack(rb2, cx, ex)

    def out_copy(o):
        return pltpu.make_async_copy(pm.at[o], out.at[o], out_sem.at[o])

    def middle(n):
        pair = inverse_pair(cx, ex, n, kiv, ti)
        grads = []
        for j in range(2):
            o = 2 * n + j
            cot_copy(o).wait()
            value, slope = activate(pm[o] + bias[o] + pair[j])
            pm[o] = value
            out_copy(o).start()
            grad = cv[o] * slope
            cv[o] = grad
            grads.append(grad)
        forward_pair(grads, kfv, tf, sx, ey, n)

    loop(0, PAIRS, middle, 2)
    pack(sx, ey, sb3)
    exchange_out(2, sb3, rb3)
    loop(0, steps // 2, lambda b: mix_step(maps.at[1], cv, av, b), 2)
    received_out(2)
    owner_step(rb3, sb4, wt, gv, giv, e_ref, zf, zi, tw, True)
    exchange_back(3, sb4, rb4)
    loop(steps // 2, steps, lambda b: mix_step(maps.at[1], cv, av, b), 2)

    def pg_copy(c):
        return pltpu.make_async_copy(av.at[c], pg.at[c], pg_sem.at[c])

    loop(0, C, lambda c: pg_copy(c).start())
    loop(0, C, lambda c: out_copy(c).wait())
    sent_out(0)
    sent_back(1)
    sent_out(2)
    await_rows(7 * WROWS, w_send)
    received_back(3)
    end = pltpu.make_async_copy(rb4, rb_out, end_sem)
    end.start()
    loop(0, C, lambda c: pg_copy(c).wait())
    end.wait()
    sent_back(3)


STEP = 4


def final_kernel(rb, pg, tmp, ti, ki, out, grad, cx, ex, kiv, held, sem, in_sem, out_sem):
    gy = lax.axis_index("gy")
    step = pl.program_id(0)

    def take(c):
        return pltpu.make_async_copy(tmp.at[c], held.at[c], in_sem.at[c])

    def give(c):
        return pltpu.make_async_copy(held.at[c], out.at[c], out_sem.at[c])

    @pl.when(step == 0)
    def _():
        table = pltpu.make_async_copy(ki.at[gy], kiv, sem)
        table.start()
        loop(0, C, lambda c: take(c).start())
        clear_rest(cx)
        unpack(rb, cx, ex)
        table.wait()

    for j in range(STEP):
        take(step * STEP + j).wait()
        give(step * STEP + j).start()
    for n in range(STEP // 2):
        pair = inverse_pair(cx, ex, step * (STEP // 2) + n, kiv, ti)
        for j in range(2):
            grad[2 * n + j] = pg[2 * n + j] + pair[j]

    @pl.when(step == pl.num_programs(0) - 1)
    def _():
        loop(0, C, lambda c: give(c).wait())


def local(activation, pointwise, bias_term, spectral_weight, cotangent):
    t = {name: jnp.asarray(value) for name, value in tables().items()}
    volume = (C, CELLS, NX)
    any_spec = pl.BlockSpec(memory_space=pl.ANY)
    vmem = pl.BlockSpec(memory_space=pltpu.VMEM)
    smem = pl.BlockSpec(memory_space=pltpu.SMEM)
    message = pltpu.VMEM((FULL, ND, LANES), F32)
    reply = pltpu.VMEM((FULL, GZ, LANES), F32)
    weights = pltpu.VMEM((8 * WROWS, LANES), F32)
    fields = pltpu.VMEM((PAIRS, LANES, LANES), F32)
    edges = pltpu.VMEM((PAIRS, 32, LANES), F32)
    dma = pltpu.SemaphoreType.DMA
    tmp, pg, rb = pl.pallas_call(
        layer_kernel,
        out_shape=[
            jax.ShapeDtypeStruct(volume, F32),
            jax.ShapeDtypeStruct(volume, F32),
            jax.ShapeDtypeStruct((FULL, ND, LANES), F32),
        ],
        in_specs=[
            any_spec, any_spec, any_spec, vmem, smem,
            vmem, vmem, any_spec, any_spec, vmem, vmem, vmem, any_spec, any_spec, vmem, vmem,
        ],
        out_specs=[any_spec, any_spec, any_spec],
        scratch_shapes=[
            pltpu.VMEM(volume, F32),
            pltpu.VMEM(volume, F32),
            pltpu.VMEM(volume, F32),
            pltpu.VMEM((288, CELLS), BF),
            pltpu.VMEM((CELLS, 512), BF),
            pltpu.VMEM((512, 256), BF),
            pltpu.VMEM((256, 512), BF),
            pltpu.VMEM((2, C * 16, C * 8), BF),
            fields,
            pltpu.VMEM((256, LANES), F32),
            fields,
            edges,
            pltpu.VMEM((WIN + 64, 32), F32),
            weights,
            weights,
            weights,
        ]
        + [message, message, reply, message] * 2
        + [dma((C,)), dma((C,)), dma((5,)), dma((C,)), dma((C,)), dma, dma, dma, dma((4,)), dma((4,))],
        compiler_params=pltpu.CompilerParams(
            collective_id=0, has_side_effects=True, vmem_limit_bytes=58 * 1024 * 1024
        ),
        name="layer",
    )(
        activation.reshape(volume), cotangent.reshape(volume),
        jnp.transpose(spectral_weight[0], (0, 2, 3, 1, 4)).reshape(WIN, 32), pointwise, bias_term,
        t["tf"], t["ti"], t["kf"], t["ki"], t["zf"], t["zi"], t["tw"], t["g"], t["gi"], t["e"], t["pick"],
    )
    block = pl.BlockSpec((STEP, CELLS, NX), lambda i: (i, 0, 0))
    out, grad = pl.pallas_call(
        final_kernel,
        grid=(C // STEP,),
        out_shape=[jax.ShapeDtypeStruct(volume, F32), jax.ShapeDtypeStruct(volume, F32)],
        in_specs=[vmem, block, any_spec, vmem, any_spec],
        out_specs=[any_spec, block],
        scratch_shapes=[fields, edges, pltpu.VMEM((CELLS, 512), BF), pltpu.VMEM(volume, F32), dma, dma((C,)), dma((C,))],
        compiler_params=pltpu.CompilerParams(vmem_limit_bytes=58 * 1024 * 1024),
        name="final",
    )(rb, pg, tmp, t["ti"], t["ki"])
    shape = (C, ZL, YL, NX)
    return out.reshape(shape), grad.reshape(shape)


def solution(mesh):
    return jax.shard_map(
        local,
        mesh=mesh,
        in_specs=(
            P(None, "gz", "gy", None),
            P(),
            P(),
            P("gz", "gy", None, None, None, None),
            P(None, "gz", "gy", None),
        ),
        out_specs=(P(None, "gz", "gy", None), P(None, "gz", "gy", None)),
        check_vma=False,
    )
```

```python
import functools
import math

import jax
import jax.numpy as jnp
import ml_dtypes
import numpy as np
from jax import lax
from jax.experimental import pallas as pl
from jax.experimental.pallas import tpu as pltpu
from jax.sharding import PartitionSpec as P

C = 20
M = 16
NX = 256
NY = 256
NZ = 128
GZ = 32
GY = 4
ND = GZ * GY
ZL = NZ // GZ
YL = NY // GY
CELLS = ZL * YL
LANES = 128
PAIRS = C // 2
MAIN = 5
EDGE = 8
FULL = 11
WROWS = 160
WIN = ZL * C * C * 2
MESH = pl.DeviceIdType.MESH
BF = jnp.bfloat16
F32 = jnp.float32


def _cos(k, n, length):
    return np.cos(2.0 * np.pi * ((k * n) % length) / length)


def _sin(k, n, length):
    return np.sin(2.0 * np.pi * ((k * n) % length) / length)


def _halves(table):
    high = table.astype(np.float32).astype(ml_dtypes.bfloat16)
    low = (table - high.astype(np.float64)).astype(ml_dtypes.bfloat16)
    return high, low


def _x_table():
    x = np.arange(NX)
    rows = np.zeros((64, NX))
    for p in range(M):
        rows[p] = _cos(p, x, NX)
        rows[16 + p] = _sin(p, x, NX) if p else _cos(16, x, NX)
    rows[32] = _sin(16, x, NX)
    return rows


def _y_table(gy):
    y = gy * YL + np.arange(YL)
    rows = np.zeros((144, ZL, YL))
    for q in range(8):
        basis = [
            _cos(q, y, NY),
            _sin(q, y, NY) if q else _cos(16, y, NY),
            _cos(q + 8, y, NY),
            _sin(q + 8, y, NY),
        ]
        for yb in range(4):
            for zl in range(ZL):
                rows[q * 16 + yb * 4 + zl, zl] = basis[yb]
    for s in range(4):
        for zl in range(ZL):
            rows[128 + s * 4 + zl, zl] = _sin(16, y, NY)
    return rows.reshape(144, CELLS)


def _mode_tables(p_zero, q_zero):
    xs = [([1, 0, 0], [0, 0, 0]), ([0, 1, 0], [0, 0, -1])] if p_zero else [([1, 0, 0], [0, 1, 0]), ([1, 0, 0], [0, -1, 0])]
    ys = [
        ([1, 0, 0, 0, 0], [0, 0, 0, 0, 0]),
        ([0, 1, 0, 0, 0], [0, 0, 0, 0, -1]),
    ] if q_zero else [([1, 0, 0, 0, 0], [0, 1, 0, 0, 0]), ([1, 0, 0, 0, 0], [0, -1, 0, 0, 0])]
    ys = ys + [([0, 0, 1, 0, 0], [0, 0, 0, 1, 0]), ([0, 0, 1, 0, 0], [0, 0, 0, -1, 0])]
    u = np.zeros((16, 8))
    v = np.zeros((16, 8))
    for i, (cx, sx) in enumerate(xs):
        for j, (cy, sy) in enumerate(ys):
            both_u = np.outer(cx, cy) - np.outer(sx, sy)
            both_v = np.outer(sx, cy) + np.outer(cx, sy)
            for xb in range(3):
                for yb in range(5):
                    if yb < 4:
                        slot = xb * 4 + yb
                    else:
                        slot = 12 + xb
                    u[slot, i * 4 + j] = both_u[xb, yb]
                    v[slot, i * 4 + j] = both_v[xb, yb]
    return u, v


def _mode_maps():
    g = np.zeros((4, 512, 256))
    gi = np.zeros((4, 256, 512))
    for variant in range(4):
        u, v = _mode_tables(variant // 2, variant % 2)
        gv = np.zeros((2, 2, 4, 8, 4, 2, 4, 8, 4))
        giv = np.zeros((2, 4, 8, 4, 2, 2, 4, 8, 4))
        for half in range(2):
            us = u[half * 8 : half * 8 + 8]
            vs = v[half * 8 : half * 8 + 8]
            for ch in range(4):
                for zl in range(4):
                    for rep in range(4):
                        gv[half, 0, ch, :, zl, 0, rep, :, ch] = us
                        gv[half, 1, ch, :, zl, 0, rep, :, ch] = -vs
                        gv[half, 0, ch, :, zl, 1, rep, :, ch] = -vs
                        gv[half, 1, ch, :, zl, 1, rep, :, ch] = -us
                        giv[0, rep, :, ch, half, 0, ch, :, zl] = us.T
                        giv[1, rep, :, ch, half, 0, ch, :, zl] = -vs.T
                        giv[0, rep, :, ch, half, 1, ch, :, zl] = -vs.T
                        giv[1, rep, :, ch, half, 1, ch, :, zl] = -us.T
        g[variant] = gv.reshape(512, 256)
        gi[variant] = giv.reshape(256, 512)
    return g.astype(ml_dtypes.bfloat16), gi.astype(ml_dtypes.bfloat16)


def _expand_maps():
    e = np.zeros((8, 4, 8, 4, 4, 32))
    for m in range(8):
        for ch in range(4):
            e[m, 0, m, ch, ch, :] = 1
    return e.reshape(8, 128, 128).astype(ml_dtypes.bfloat16)


def _pick_map():
    pick = np.zeros((32, 32))
    for q in range(8):
        for j, k in enumerate([q, (-q if q else -16), q + 8, -(q + 8)]):
            pick[j * 8 + q, k % 32] = 1
    return pick.astype(ml_dtypes.bfloat16)


@functools.cache
def tables():
    xh, xl = _halves(_x_table())
    tf = np.zeros((2, NX, 256), ml_dtypes.bfloat16)
    for j in range(2):
        tf[j, :, 64 * j : 64 * j + 64] = xh.T
        tf[j, :, 128 + 64 * j : 192 + 64 * j] = xl.T
    ti = np.concatenate([xh, xh, xl, np.zeros_like(xl)], axis=0)
    kf, ki = [], []
    for gy in range(GY):
        h, l = _halves(_y_table(gy))
        kf.append(np.concatenate([h, l], axis=0))
        ht, lt = h.T, l.T
        pad = np.zeros((CELLS, 80), ml_dtypes.bfloat16)
        ki.append(np.concatenate([ht[:, :128], lt[:, :128], ht[:, :128], ht[:, 128:], ht[:, 128:], lt[:, 128:], pad], axis=1))
    kz = np.arange(M)[:, None]
    far = 4 * (np.arange(ND)[None, :] // GY)
    h, l = _halves(np.concatenate([_cos(kz, far, NZ), _sin(kz, far, NZ)], axis=0))
    zf = np.concatenate([h, l], axis=0)
    far = 4 * np.arange(GZ)[None, :]
    factor = np.where(kz == 0, 1.0, 2.0) / float(NX * NY * NZ)
    h, l = _halves(np.concatenate([factor * _cos(kz, far, NZ), factor * _sin(kz, far, NZ)], axis=0).T)
    zi = np.concatenate([h, h, l], axis=1)
    near = np.arange(LANES)[None, :] % 4
    tw = np.stack([_cos(kz, near, NZ), _sin(kz, near, NZ)]).astype(np.float32)
    g, gi = _mode_maps()
    return dict(tf=tf, ti=ti, kf=np.stack(kf), ki=np.stack(ki), zf=zf, zi=zi, tw=tw, g=g, gi=gi, e=_expand_maps(), pick=_pick_map())


def nn(a, b):
    return lax.dot_general(a, b, (((1,), (0,)), ((), ())), preferred_element_type=F32)


def nt(a, b):
    return lax.dot_general(a, b, (((1,), (1,)), ((), ())), preferred_element_type=F32)


def halves(value):
    high = value.astype(BF)
    low = (value - high.astype(F32)).astype(BF)
    return high, low


def lanes_of(value):
    return lax.broadcasted_iota(jnp.int32, value.shape, 1)


def swap_blocks(tiles, width):
    tiles = list(tiles)
    block = lax.rem(lanes_of(tiles[0]) // width, 8)
    for bit in (1, 2, 4):
        upper = lax.rem(block // bit, 2) == 1
        shift = bit * width
        for i in range(8):
            if i & bit:
                continue
            a, b = tiles[i], tiles[i | bit]
            tiles[i] = jnp.where(upper, pltpu.roll(b, shift, 1), a)
            tiles[i | bit] = jnp.where(upper, b, pltpu.roll(a, LANES - shift, 1))
    return tiles


def forward_pair(pair, kf, tf, sx, ey, n):
    parts = []
    for volume in pair:
        ah, al = halves(volume)
        b = nn(kf[...], ah)
        parts.append(halves(b[:144] + b[144:] + nn(kf[:144], al)))
    (h0, l0), (h1, l1) = parts
    o = nn(h0, tf[0]) + nn(h1, tf[1])
    o = o[:, :LANES] + o[:, LANES:] + nn(l0, tf[0, :, :LANES]) + nn(l1, tf[1, :, :LANES])
    sx[n] = o[:LANES].T
    ey[pl.ds(pl.multiple_of(n * 16, 16), 16), :] = o[LANES:]


def pack(sx, ey, sb):
    for r in range(MAIN):
        tiles = swap_blocks([sx[2 * r + i // 4, pl.ds((i // 2 % 2) * 64 + (i % 2) * 16, 16), :] for i in range(8)], 16)
        for q in range(8):
            sb[r, 16 * q : 16 * q + 16, :] = tiles[q]
    turned = [ey[0:LANES, :].T, ey[LANES : 2 * LANES, :].T]
    slot = lax.rem(lax.broadcasted_iota(jnp.int32, (16, LANES), 1) // 4, 4)
    block = lax.broadcasted_iota(jnp.int32, (16, LANES), 1) // 16
    zero = jnp.zeros((16, LANES), F32)
    by_ch = [
        [
            sum((jnp.where(slot == h, t[64 * ch + 16 * h : 64 * ch + 16 * h + 16], zero) for h in range(3)), zero)
            for ch in range(2)
        ]
        for t in turned
    ]
    none = jnp.zeros((8, LANES), F32)
    top = lax.broadcasted_iota(jnp.int32, (16, LANES), 0) == 0
    for e in range(EDGE - MAIN):
        tiles = []
        edge = zero
        for c in range(4):
            for k in range(2):
                r = 2 * e + k
                if r == MAIN:
                    tiles.append(none)
                    continue
                n = 2 * r + c // 2
                tiles.append(sx[n, pl.ds((c % 2) * 64 + 32, 8), :])
                to = 2 * c + 1 - k
                moved = pltpu.roll(by_ch[n // 8][c % 2], (to - n % 8) % 8 * 16, 1)
                edge = edge + jnp.where(block == to, moved, zero)
        tiles = swap_blocks(tiles, 16)
        sb[MAIN + e, 0:8, :] = jnp.where(top[:8], tiles[0], edge[:8])
        sb[MAIN + e, 8:16, :] = edge[8:]
        sb[EDGE + e, 0:16, :] = edge
        for q in range(1, 8):
            sb[MAIN + e, 16 * q : 16 * q + 8, :] = tiles[q]


def unpack(rb, cx, ex):
    for r in range(MAIN):
        tiles = swap_blocks([rb[r, 16 * q : 16 * q + 16, :] for q in range(8)], 16)
        for i in range(8):
            cx[2 * r + i // 4, pl.ds((i // 2 % 2) * 64 + (i % 2) * 16, 16), :] = tiles[i]
    top = lax.broadcasted_iota(jnp.int32, (16, LANES), 0) == 0
    rows = []
    for e in range(EDGE - MAIN):
        tiles = swap_blocks([rb[MAIN + e, 16 * q : 16 * q + 8, :] for q in range(8)], 16)
        for c in range(4):
            for k in range(2):
                r = 2 * e + k
                if r < MAIN:
                    cx[2 * r + c // 2, pl.ds((c % 2) * 64 + 32, 8), :] = tiles[2 * c + k]
        rows.append(jnp.where(top, rb[EDGE + e, 0:16, :], rb[MAIN + e, 0:16, :]))
    turned = jnp.concatenate(rows + [jnp.zeros((80, LANES), F32)], axis=0).T
    row = lax.broadcasted_iota(jnp.int32, (16, LANES), 0)
    block = lax.broadcasted_iota(jnp.int32, (16, LANES), 1) // 16
    keep = lax.rem(block, 4) == row // 4
    zero = jnp.zeros((16, LANES), F32)
    for r in range(MAIN):
        for c in range(4):
            at = 32 * c + 16 * (1 - r % 2)
            e = jnp.where(block == r // 2, turned[at : at + 16], zero)
            for shift in (16, 32, 64):
                e = e + pltpu.roll(e, shift, 1)
            ex[2 * r + c // 2, pl.ds((c % 2) * 16, 16), :] = jnp.where(keep, e, zero)


def clear_rest(cx):
    for n in range(PAIRS):
        for ch in range(2):
            cx[n, pl.ds(64 * ch + 40, 24), :] = jnp.zeros((24, LANES), F32)


def inverse_pair(cx, ex, n, ki, ti):
    c = cx[n].T
    low = lanes_of(c) < 64
    other = pltpu.roll(c, 64, 1)
    d = jnp.concatenate([jnp.where(low, c, other), jnp.where(low, other, c)], axis=1)
    dh, dl = halves(d)
    e = ex[n]
    eh, el = halves(jnp.concatenate([e[:16], e[16:]], axis=1))
    one = jnp.concatenate([dh, dh], axis=0)
    two = jnp.concatenate([dl, eh, el, eh, jnp.zeros((80, 256), BF)], axis=0)
    h = nn(ki[:, :256], one) + nn(ki[:, 256:], two)
    hh, hl = halves(h)
    out = []
    for j in range(2):
        high = hh[:, LANES * j : LANES * j + LANES]
        rest = hl[:, LANES * j : LANES * j + LANES]
        mix = jnp.where(lanes_of(high) < 64, high.astype(F32), rest.astype(F32)).astype(BF)
        out.append(nn(jnp.concatenate([mix, high], axis=1), ti[...]))
    return out


def owner_step(rb, sb, wt, g, gi, e_ref, zf, zi, tw, corner, adjoint):
    d = jnp.concatenate([rb[r] for r in range(FULL)], axis=1)
    dh, dl = halves(d)
    zfv = zf[...]
    f = nn(zfv, dh)
    f = f[:32] + f[32:] + nn(zfv[:32], dl)
    cb = tw[0]
    sb_near = tw[1]

    first_half = lax.rem(lax.broadcasted_iota(jnp.int32, (32, LANES), 1) // 16, 2) == 0
    fields = [f[:, r * LANES : (r + 1) * LANES] for r in range(FULL)]
    extras = []
    for e in range(EDGE - MAIN):
        one = fields[MAIN + e]
        two = one * (1.0 - corner) + fields[EDGE + e] * corner
        extras.append(jnp.where(first_half, one, two))
        extras.append(jnp.where(first_half, pltpu.roll(one, LANES - 16, 1), pltpu.roll(two, 16, 1)))

    def turned(field):
        fc = field[:16]
        fs = field[16:]
        return jnp.concatenate([fc * cb - fs * sb_near, fs * cb + fc * sb_near], axis=1)

    z = jnp.concatenate(
        [jnp.concatenate([turned(fields[r]), turned(extras[r])], axis=1) for r in range(MAIN)], axis=0
    )
    zh, zlow = halves(z)
    x = nn(jnp.concatenate([zh, zlow], axis=0), g[...])
    x = x[:80] + x[80:]
    xre, xim = x[:, :LANES], x[:, LANES:]

    def weight(ri, m, r):
        return wt[pl.ds(((ri * 8 + m) * MAIN + r) * 16, 16), :]

    zero = jnp.zeros((16, LANES), F32)
    if not adjoint:
        pieces = jnp.concatenate(halves(xre) + halves(xim), axis=0)
        yre, yim = [], []
        for m in range(8):
            xm = nn(pieces, e_ref[m])
            xmr = xm[:80] + xm[80:160]
            xmi = xm[160:240] + xm[240:]
            sr, si = zero, zero
            for r in range(MAIN):
                wr, wi = weight(0, m, r), weight(1, m, r)
                ar, ai = xmr[16 * r : 16 * r + 16], xmi[16 * r : 16 * r + 16]
                sr = sr + wr * ar - wi * ai
                si = si + wr * ai + wi * ar
            yre.append(sr)
            yim.append(si)
        vre = swap_blocks(yre, 4)[:MAIN]
        vim = swap_blocks(yim, 4)[:MAIN]
        v = jnp.concatenate([jnp.concatenate([a, b], axis=1) for a, b in zip(vre, vim)], axis=0)
    else:
        gre = swap_blocks([xre[16 * t : 16 * t + 16] for t in range(MAIN)] + [zero] * 3, 4)
        gim = swap_blocks([xim[16 * t : 16 * t + 16] for t in range(MAIN)] + [zero] * 3, 4)
        total = None
        for m in range(8):
            yr, yi = [], []
            for r in range(MAIN):
                wr, wi = weight(0, m, r), weight(1, m, r)
                yr.append(wr * gre[m] + wi * gim[m])
                yi.append(wr * gim[m] - wi * gre[m])
            pieces = jnp.concatenate(
                halves(jnp.concatenate(yr, axis=0)) + halves(jnp.concatenate(yi, axis=0)), axis=0
            )
            part = nt(pieces, e_ref[m])
            total = part if total is None else total + part
        v = jnp.concatenate([total[:80] + total[80:160], total[160:240] + total[240:]], axis=1)
    vh, vl = halves(v)
    c = nn(jnp.concatenate([vh, vl], axis=0), gi[...])
    c = c[:80] + c[80:]

    def back(t, half):
        cc = c[16 * t : 16 * t + 16, half * 256 : half * 256 + LANES]
        cs = c[16 * t : 16 * t + 16, half * 256 + LANES : half * 256 + 256]
        return jnp.concatenate([cc * cb + cs * sb_near, cs * cb - cc * sb_near], axis=0)

    edges, corners = [], []
    none = jnp.zeros((32, LANES), F32)
    for e in range(EDGE - MAIN):
        one = back(2 * e, 1)
        two = back(2 * e + 1, 1) if 2 * e + 1 < MAIN else none
        low = jnp.where(first_half, one, pltpu.roll(two, 16, 1))
        high = jnp.where(first_half, pltpu.roll(two, LANES - 16, 1), one)
        edges.append(low + high * (1.0 - corner))
        corners.append(high)
    r = jnp.concatenate([back(t, 0) for t in range(MAIN)] + edges + corners, axis=1)
    rh, rl = halves(r)
    out = nn(zi[...], jnp.concatenate([rh, rl, rh], axis=0))
    for t in range(FULL):
        sb[t] = out[:, t * LANES : (t + 1) * LANES]


def owner_of(z):
    i = z // 16
    p = lax.rem(z * (1 - 2 * i) + 32 * i, 16)
    return p, i, lax.rem(i + p, 2)


def group_of(p, h, y):
    return 4 * h + lax.rem(y + 8 - p // 2, 4)


def owner_device(p, q):
    i = lax.rem(q // 4 + p, 2)
    first = (16 - p) // 16
    z = p + i * (32 - 2 * p - 16 * first)
    y = lax.rem(lax.rem(q, 4) + p // 2, 4)
    return z, y


def weight_step(wv, ws, pick, k):
    for ri in range(2):
        block = jnp.concatenate([wv[pl.ds(k * 800 + c * 40 + ri, 32, stride=2), :] for c in range(C)], axis=0)
        bh, bl = halves(block)
        rows = nt(pick, bh) + nt(pick, bl)
        for j in range(4):
            for r in range(MAIN):
                ws[pl.ds(ri * 80 + (j * MAIN + r) * 4 + k, 8, stride=WROWS), :] = rows[
                    8 * j : 8 * j + 8, r * LANES : (r + 1) * LANES
                ]


def weight_spread(wb, wt, n):
    ri = n // 20
    j = lax.rem(n, 20) // MAIN
    r = lax.rem(n, MAIN)
    for k in range(4):
        v = wb[pl.ds(n * 4 + k, 8, stride=WROWS), :]
        base = ((ri * 8 + j) * MAIN + r) * 16 + k
        for i in range(2):
            wt[pl.ds(base + i * 4 * MAIN * 16, 4, stride=4), :] = v[4 * i : 4 * i + 4]


def mix_maps(pw):
    ones = jnp.where(
        lax.broadcasted_iota(jnp.int32, (C * 8, C), 0) // 8 == lax.broadcasted_iota(jnp.int32, (C * 8, C), 1), 1.0, 0.0
    ).astype(BF)
    shape = (C * 8, C * 8)
    same = lax.rem(lax.broadcasted_iota(jnp.int32, shape, 0), 8) == lax.rem(lax.broadcasted_iota(jnp.int32, shape, 1), 8)
    fwd, adj = [], []
    for part in halves(pw[...]):
        rows = nn(ones, part).astype(BF)
        fwd.append(jnp.where(same, nt(ones, rows), 0.0).astype(BF))
        adj.append(jnp.where(same, nt(rows, ones), 0.0).astype(BF))
    return jnp.concatenate(fwd, axis=0), jnp.concatenate(adj, axis=0)


def mix_step(maps, src, dst, b):
    rows = pl.ds(pl.multiple_of(b * 8, 8), 8)
    sh, sl = halves(src[:, rows, :].reshape(C * 8, NX))
    o = nn(maps[...], sh)
    o = o[: C * 8] + o[C * 8 :] + nn(maps[: C * 8], sl)
    dst[:, rows, :] = o.reshape(C, 8, NX)


def activate(mixed):
    cdf = 0.5 * (1.0 + lax.erf(mixed * (1.0 / math.sqrt(2.0))))
    density = jnp.exp(-0.5 * mixed * mixed) * (1.0 / math.sqrt(2.0 * math.pi))
    return mixed * cdf, cdf + mixed * density


def loop(first, last, fn, unroll=1):
    def body(i, carry):
        fn(i)
        return carry

    lax.fori_loop(first, last, body, 0, unroll=unroll)


def layer_kernel(
    act, cot, w, pw, bias, tf, ti, kf, ki, zf, zi, tw, g, gi, e_ref, pick,
    out, pg, rb_out,
    av, cv, pm, kfv, kiv, gv, giv, maps, sx, ey, cx, ex, wv, ws, wb, wt, count,
    sb1, rb1, sb2, rb2, sb3, rb3, sb4, rb4,
    act_sem, cot_sem, tab_sem, out_sem, pg_sem, end_sem, w_send, w_recv, send_sem, recv_sem,
):
    gz = lax.axis_index("gz")
    gy = lax.axis_index("gy")
    p, sign, h = owner_of(gz)
    q = group_of(p, h, gy)
    mine = q * 16 + p
    corner = jnp.where(p + q == 0, 1.0, 0.0)

    def by_kind(fn):
        pl.when(p * q != 0)(lambda: fn(MAIN))
        pl.when((p * q == 0) & (p + q != 0))(lambda: fn(EDGE))
        pl.when(p + q == 0)(lambda: fn(FULL))

    variant = 2 * ((16 - p) // 16) + (8 - q) // 8

    def act_copy(c):
        return pltpu.make_async_copy(act.at[c], av.at[c], act_sem.at[c])

    def cot_copy(c):
        return pltpu.make_async_copy(cot.at[c], cv.at[c], cot_sem.at[c])

    table_copies = [
        pltpu.make_async_copy(kf.at[gy], kfv, tab_sem.at[0]),
        pltpu.make_async_copy(ki.at[gy], kiv, tab_sem.at[1]),
        pltpu.make_async_copy(g.at[variant], gv, tab_sem.at[2]),
        pltpu.make_async_copy(gi.at[variant], giv, tab_sem.at[3]),
        pltpu.make_async_copy(w, wv.at[pl.ds(0, WIN)], tab_sem.at[4]),
    ]
    table_copies[0].start()
    loop(0, 8, lambda c: act_copy(c).start())
    table_copies[4].start()
    loop(8, C, lambda c: act_copy(c).start())
    for rb in (rb1, rb2, rb3, rb4):
        rb[MAIN:] = jnp.zeros((FULL - MAIN, ND, LANES), F32)

    next_y = [gy] + [lax.rem(gy + j, GY) for j in range(1, GY)]

    def each_peer(fn, per_z):
        own = per_z(gz)
        for j in range(1, GY):
            fn(gz, next_y[j], own)

        def body(_, z):
            z = z + 1
            z = jnp.where(z == GZ, 0, z)
            known = per_z(z)
            for j in range(GY):
                fn(z, next_y[j], known)
            return z

        lax.fori_loop(1, GZ, body, gz)

    barrier = pltpu.get_barrier_semaphore()
    each_peer(
        lambda z, y, _: pl.semaphore_signal(barrier, 1, device_id=(z, y), device_id_type=MESH), lambda z: None
    )

    def exchange_out(n, src, dst):
        def start(z, y, to, at, rows):
            pltpu.make_async_remote_copy(
                src_ref=src.at[pl.ds(at, rows), to],
                dst_ref=dst.at[pl.ds(at, rows), gz * GY + gy],
                send_sem=send_sem.at[n],
                recv_sem=recv_sem.at[n],
                device_id=(z, y),
                device_id_type=MESH,
            ).start()

        def send(z, y, known):
            tp, _, th = known
            tq = group_of(tp, th, y)
            to = tq * 16 + tp
            some = tp * tq
            pl.when(some == 0)(lambda: start(z, y, to, 0, EDGE))
            pl.when(some != 0)(lambda: start(z, y, to, 0, MAIN))

        def keep(rows):
            pltpu.make_async_copy(
                src.at[pl.ds(0, rows), mine], dst.at[pl.ds(0, rows), gz * GY + gy], recv_sem.at[n]
            ).start()

        each_peer(send, owner_of)
        by_kind(keep)
        pl.when(p + q != 0)(lambda: start(0, 0, 0, EDGE, FULL - EDGE))

    def exchange_back(n, src, dst):
        def start_all(rows):
            def send(z, y, _):
                pltpu.make_async_remote_copy(
                    src_ref=src.at[pl.ds(0, rows), z],
                    dst_ref=dst.at[pl.ds(0, rows), mine],
                    send_sem=send_sem.at[n],
                    recv_sem=recv_sem.at[n],
                    device_id=(z, y),
                    device_id_type=MESH,
                ).start()

            pltpu.make_async_copy(src.at[pl.ds(0, rows), gz], dst.at[pl.ds(0, rows), mine], recv_sem.at[n]).start()
            each_peer(send, lambda z: None)

        by_kind(start_all)

    def await_rows(rows, sem):
        pltpu.make_async_copy(count.at[pl.ds(0, rows)], count.at[pl.ds(0, rows)], sem).wait()

    def received_out(n):
        by_kind(lambda rows: await_rows(ND * rows, recv_sem.at[n]))

    def received_back(n):
        await_rows(ND * MAIN + 23 * (EDGE - MAIN) + (FULL - EDGE), recv_sem.at[n])

    def sent_out(n):
        most = (ND - 1) * MAIN + (FULL - EDGE)
        others = {MAIN: most + 23 * (EDGE - MAIN), EDGE: most + 22 * (EDGE - MAIN), FULL: (ND - 1) * MAIN + 22 * (EDGE - MAIN)}
        by_kind(lambda rows: await_rows(others[rows], send_sem.at[n]))

    def sent_back(n):
        by_kind(lambda rows: await_rows((ND - 1) * rows, send_sem.at[n]))

    for copy in table_copies[1:4]:
        copy.start()
    loop(0, C, lambda c: cot_copy(c).start())

    wv[pl.ds(WIN, 64), :] = jnp.zeros((64, 32), F32)
    table_copies[0].wait()

    def first(n):
        act_copy(2 * n).wait()
        act_copy(2 * n + 1).wait()
        forward_pair([av[2 * n], av[2 * n + 1]], kfv, tf, sx, ey, n)

    loop(0, 4, first, 4)
    table_copies[4].wait()
    pickv = pick[...]
    loop(0, 4, lambda k: weight_step(wv, ws, pickv, k))
    pl.semaphore_wait(barrier, ND - 1)

    slot = (sign * 4 + gy) * WROWS

    def send_weights(to):
        z, y = owner_device(p, to)

        @pl.when(to == q)
        def _():
            pltpu.make_async_copy(ws.at[pl.ds(to * WROWS, WROWS)], wb.at[pl.ds(slot, WROWS)], w_recv).start()

        @pl.when(to != q)
        def _():
            pltpu.make_async_remote_copy(
                src_ref=ws.at[pl.ds(to * WROWS, WROWS)],
                dst_ref=wb.at[pl.ds(slot, WROWS)],
                send_sem=w_send,
                recv_sem=w_recv,
                device_id=(z, y),
                device_id_type=MESH,
            ).start()

    loop(0, 8, send_weights)
    loop(4, PAIRS, first, 6)
    pack(sx, ey, sb1)
    exchange_out(0, sb1, rb1)

    fwd, adj = mix_maps(pw)
    maps[0] = fwd
    maps[1] = adj
    steps = CELLS // 8
    loop(0, steps // 2, lambda b: mix_step(maps.at[0], av, pm, b), 2)
    for copy in table_copies[1:4]:
        copy.wait()
    clear_rest(cx)
    await_rows(8 * WROWS, w_recv)
    loop(0, 40, lambda n: weight_spread(wb, wt, n), 4)

    received_out(0)
    owner_step(rb1, sb2, wt, gv, giv, e_ref, zf, zi, tw, corner, False)
    exchange_back(1, sb2, rb2)
    loop(steps // 2, steps, lambda b: mix_step(maps.at[0], av, pm, b), 2)
    received_back(1)
    unpack(rb2, cx, ex)

    def out_copy(o):
        return pltpu.make_async_copy(pm.at[o], out.at[o], out_sem.at[o])

    def middle(n):
        pair = inverse_pair(cx, ex, n, kiv, ti)
        for j in range(2):
            o = 2 * n + j
            value, slope = activate(pm[o] + bias[o] + pair[j])
            pm[o] = value
            cv[o] = cv[o] * slope

    loop(0, C, lambda o: cot_copy(o).wait())
    loop(0, PAIRS, middle, PAIRS)
    loop(0, C, lambda o: out_copy(o).start())
    loop(0, PAIRS, lambda n: forward_pair([cv[2 * n], cv[2 * n + 1]], kfv, tf, sx, ey, n), PAIRS)
    pack(sx, ey, sb3)
    exchange_out(2, sb3, rb3)
    loop(0, steps // 2, lambda b: mix_step(maps.at[1], cv, av, b), 2)
    received_out(2)
    owner_step(rb3, sb4, wt, gv, giv, e_ref, zf, zi, tw, corner, True)
    exchange_back(3, sb4, rb4)
    loop(steps // 2, steps, lambda b: mix_step(maps.at[1], cv, av, b), 2)

    def pg_copy(c):
        return pltpu.make_async_copy(av.at[c], pg.at[c], pg_sem.at[c])

    loop(0, C, lambda c: pg_copy(c).start())
    loop(0, C, lambda c: out_copy(c).wait())
    sent_out(0)
    sent_back(1)
    sent_out(2)
    await_rows(7 * WROWS, w_send)
    received_back(3)
    end = pltpu.make_async_copy(rb4, rb_out, end_sem)
    end.start()
    loop(0, C, lambda c: pg_copy(c).wait())
    end.wait()
    sent_back(3)


def final_kernel(rb, pg, tmp, ti, ki, out, grad, rbv, cx, ex, kiv, held, gv, sem, in_sem, out_sem, pg_sem, grad_sem):
    gy = lax.axis_index("gy")

    def take(c):
        return pltpu.make_async_copy(tmp.at[c], held.at[c], in_sem.at[c])

    def give(c):
        return pltpu.make_async_copy(held.at[c], out.at[c], out_sem.at[c])

    def pg_copy(c):
        return pltpu.make_async_copy(pg.at[c], gv.at[c], pg_sem.at[c])

    def grad_copy(c):
        return pltpu.make_async_copy(gv.at[c], grad.at[c], grad_sem.at[c])

    fields = pltpu.make_async_copy(rb, rbv, sem.at[0])
    table = pltpu.make_async_copy(ki.at[gy], kiv, sem.at[1])
    fields.start()
    table.start()
    half = C // 2
    loop(0, half, lambda c: take(c).start())
    loop(0, C, lambda c: pg_copy(c).start())
    loop(half, C, lambda c: take(c).start())

    def pass_on(c):
        take(c).wait()
        give(c).start()

    clear_rest(cx)
    fields.wait()
    unpack(rbv, cx, ex)
    loop(0, half, pass_on)
    table.wait()

    def finish(n):
        pair = inverse_pair(cx, ex, n, kiv, ti)
        for j in range(2):
            gv[2 * n + j] = gv[2 * n + j] + pair[j]

    for first in (0, half):
        loop(first, first + half, lambda c: pg_copy(c).wait())
        loop(first // 2, (first + half) // 2, finish, half // 2)
        loop(first, first + half, lambda c: grad_copy(c).start())
        if first == 0:
            loop(half, C, pass_on)
    loop(0, C, lambda c: give(c).wait())
    loop(0, C, lambda c: grad_copy(c).wait())


def local(activation, pointwise, bias_term, spectral_weight, cotangent):
    t = {name: jnp.asarray(value) for name, value in tables().items()}
    volume = (C, CELLS, NX)
    any_spec = pl.BlockSpec(memory_space=pl.ANY)
    vmem = pl.BlockSpec(memory_space=pltpu.VMEM)
    smem = pl.BlockSpec(memory_space=pltpu.SMEM)
    message = pltpu.VMEM((FULL, ND, LANES), F32)
    reply = pltpu.VMEM((FULL, GZ, LANES), F32)
    weights = pltpu.VMEM((8 * WROWS, LANES), F32)
    fields = pltpu.VMEM((PAIRS, LANES, LANES), F32)
    edges = pltpu.VMEM((PAIRS, 32, LANES), F32)
    dma = pltpu.SemaphoreType.DMA
    tmp, pg, rb = pl.pallas_call(
        layer_kernel,
        out_shape=[
            jax.ShapeDtypeStruct(volume, F32),
            jax.ShapeDtypeStruct(volume, F32),
            jax.ShapeDtypeStruct((FULL, ND, LANES), F32),
        ],
        in_specs=[
            any_spec, any_spec, any_spec, vmem, smem,
            vmem, vmem, any_spec, any_spec, vmem, vmem, vmem, any_spec, any_spec, vmem, vmem,
        ],
        out_specs=[any_spec, any_spec, any_spec],
        scratch_shapes=[
            pltpu.VMEM(volume, F32),
            pltpu.VMEM(volume, F32),
            pltpu.VMEM(volume, F32),
            pltpu.VMEM((288, CELLS), BF),
            pltpu.VMEM((CELLS, 512), BF),
            pltpu.VMEM((512, 256), BF),
            pltpu.VMEM((256, 512), BF),
            pltpu.VMEM((2, C * 16, C * 8), BF),
            fields,
            pltpu.VMEM((256, LANES), F32),
            fields,
            edges,
            pltpu.VMEM((WIN + 64, 32), F32),
            weights,
            weights,
            weights,
            pltpu.VMEM((ND * FULL, LANES), F32),
        ]
        + [message, message, reply, message] * 2
        + [dma((C,)), dma((C,)), dma((5,)), dma((C,)), dma((C,)), dma, dma, dma, dma((4,)), dma((4,))],
        compiler_params=pltpu.CompilerParams(
            collective_id=0, has_side_effects=True, vmem_limit_bytes=58 * 1024 * 1024
        ),
        name="layer",
    )(
        activation.reshape(volume), cotangent.reshape(volume),
        jnp.transpose(spectral_weight[0], (0, 2, 3, 1, 4)).reshape(WIN, 32), pointwise, bias_term,
        t["tf"], t["ti"], t["kf"], t["ki"], t["zf"], t["zi"], t["tw"], t["g"], t["gi"], t["e"], t["pick"],
    )
    out, grad = pl.pallas_call(
        final_kernel,
        out_shape=[jax.ShapeDtypeStruct(volume, F32), jax.ShapeDtypeStruct(volume, F32)],
        in_specs=[any_spec, any_spec, any_spec, vmem, any_spec],
        out_specs=[any_spec, any_spec],
        scratch_shapes=[
            message, fields, edges, pltpu.VMEM((CELLS, 512), BF), pltpu.VMEM(volume, F32), pltpu.VMEM(volume, F32),
            dma((2,)), dma((C,)), dma((C,)), dma((C,)), dma((C,)),
        ],
        compiler_params=pltpu.CompilerParams(vmem_limit_bytes=58 * 1024 * 1024),
        name="final",
    )(rb, pg, tmp, t["ti"], t["ki"])
    shape = (C, ZL, YL, NX)
    return out.reshape(shape), grad.reshape(shape)


def solution(mesh):
    return jax.shard_map(
        local,
        mesh=mesh,
        in_specs=(
            P(None, "gz", "gy", None),
            P(),
            P(),
            P("gz", "gy", None, None, None, None),
            P(None, "gz", "gy", None),
        ),
        out_specs=(P(None, "gz", "gy", None), P(None, "gz", "gy", None)),
        check_vma=False,
    )
```

```python
import functools
import math

import jax
import jax.numpy as jnp
import ml_dtypes
import numpy as np
from jax import lax
from jax.experimental import pallas as pl
from jax.experimental.pallas import tpu as pltpu
from jax.sharding import PartitionSpec as P

C = 20
M = 16
NX = 256
NY = 256
NZ = 128
GZ = 32
GY = 4
ND = GZ * GY
ZL = NZ // GZ
YL = NY // GY
CELLS = ZL * YL
LANES = 128
PAIRS = C // 2
MAIN = 5
EDGE = 8
FULL = 11
WROWS = 128
WIN = ZL * C * C * 2
MESH = pl.DeviceIdType.MESH
BF = jnp.bfloat16
F32 = jnp.float32


def _cos(k, n, length):
    return np.cos(2.0 * np.pi * ((k * n) % length) / length)


def _sin(k, n, length):
    return np.sin(2.0 * np.pi * ((k * n) % length) / length)


def _halves(table):
    high = table.astype(np.float32).astype(ml_dtypes.bfloat16)
    low = (table - high.astype(np.float64)).astype(ml_dtypes.bfloat16)
    return high, low


def _x_table():
    x = np.arange(NX)
    rows = np.zeros((64, NX))
    for p in range(M):
        rows[p] = _cos(p, x, NX)
        rows[16 + p] = _sin(p, x, NX) if p else _cos(16, x, NX)
    rows[32] = _sin(16, x, NX)
    return rows


def _y_table(gy):
    y = gy * YL + np.arange(YL)
    rows = np.zeros((144, ZL, YL))
    for q in range(8):
        basis = [
            _cos(q, y, NY),
            _sin(q, y, NY) if q else _cos(16, y, NY),
            _cos(q + 8, y, NY),
            _sin(q + 8, y, NY),
        ]
        for yb in range(4):
            for zl in range(ZL):
                rows[q * 16 + yb * 4 + zl, zl] = basis[yb]
    for s in range(4):
        for zl in range(ZL):
            rows[128 + s * 4 + zl, zl] = _sin(16, y, NY)
    return rows.reshape(144, CELLS)


def _mode_tables(p_zero, q_zero):
    xs = [([1, 0, 0], [0, 0, 0]), ([0, 1, 0], [0, 0, -1])] if p_zero else [([1, 0, 0], [0, 1, 0]), ([1, 0, 0], [0, -1, 0])]
    ys = [
        ([1, 0, 0, 0, 0], [0, 0, 0, 0, 0]),
        ([0, 1, 0, 0, 0], [0, 0, 0, 0, -1]),
    ] if q_zero else [([1, 0, 0, 0, 0], [0, 1, 0, 0, 0]), ([1, 0, 0, 0, 0], [0, -1, 0, 0, 0])]
    ys = ys + [([0, 0, 1, 0, 0], [0, 0, 0, 1, 0]), ([0, 0, 1, 0, 0], [0, 0, 0, -1, 0])]
    u = np.zeros((16, 8))
    v = np.zeros((16, 8))
    for i, (cx, sx) in enumerate(xs):
        for j, (cy, sy) in enumerate(ys):
            both_u = np.outer(cx, cy) - np.outer(sx, sy)
            both_v = np.outer(sx, cy) + np.outer(cx, sy)
            for xb in range(3):
                for yb in range(5):
                    if yb < 4:
                        slot = xb * 4 + yb
                    else:
                        slot = 12 + xb
                    u[slot, i * 4 + j] = both_u[xb, yb]
                    v[slot, i * 4 + j] = both_v[xb, yb]
    return u, v


def _mode_maps():
    g = np.zeros((4, 512, 256))
    gi = np.zeros((4, 256, 512))
    for variant in range(4):
        u, v = _mode_tables(variant // 2, variant % 2)
        gv = np.zeros((2, 2, 4, 8, 4, 2, 4, 8, 4))
        giv = np.zeros((2, 4, 8, 4, 2, 2, 4, 8, 4))
        for half in range(2):
            us = u[half * 8 : half * 8 + 8]
            vs = v[half * 8 : half * 8 + 8]
            for ch in range(4):
                for zl in range(4):
                    for rep in range(4):
                        gv[half, 0, ch, :, zl, 0, rep, :, ch] = us
                        gv[half, 1, ch, :, zl, 0, rep, :, ch] = -vs
                        gv[half, 0, ch, :, zl, 1, rep, :, ch] = -vs
                        gv[half, 1, ch, :, zl, 1, rep, :, ch] = -us
                        giv[0, rep, :, ch, half, 0, ch, :, zl] = us.T
                        giv[1, rep, :, ch, half, 0, ch, :, zl] = -vs.T
                        giv[0, rep, :, ch, half, 1, ch, :, zl] = -vs.T
                        giv[1, rep, :, ch, half, 1, ch, :, zl] = -us.T
        g[variant] = gv.reshape(512, 256)
        gi[variant] = giv.reshape(256, 512)
    return g.astype(ml_dtypes.bfloat16), gi.astype(ml_dtypes.bfloat16)


def _expand_maps():
    e = np.zeros((8, 4, 8, 4, 4, 32))
    for m in range(8):
        for ch in range(4):
            e[m, 0, m, ch, ch, :] = 1
    return e.reshape(8, 128, 128).astype(ml_dtypes.bfloat16)


def _pick_map():
    pick = np.zeros((32, 32))
    for q in range(8):
        for j, k in enumerate([q, (-q if q else -16), q + 8, -(q + 8)]):
            pick[j * 8 + q, k % 32] = 1
    return pick.astype(ml_dtypes.bfloat16)


@functools.cache
def tables():
    xh, xl = _halves(_x_table())
    tf = np.zeros((2, NX, 256), ml_dtypes.bfloat16)
    for j in range(2):
        tf[j, :, 64 * j : 64 * j + 64] = xh.T
        tf[j, :, 128 + 64 * j : 192 + 64 * j] = xl.T
    ti = np.concatenate([xh, xh, xl, np.zeros_like(xl)], axis=0)
    kf, ki = [], []
    for gy in range(GY):
        h, l = _halves(_y_table(gy))
        kf.append(np.concatenate([h, l], axis=0))
        ht, lt = h.T, l.T
        pad = np.zeros((CELLS, 80), ml_dtypes.bfloat16)
        ki.append(np.concatenate([ht[:, :128], lt[:, :128], ht[:, :128], ht[:, 128:], ht[:, 128:], lt[:, 128:], pad], axis=1))
    kz = np.arange(M)[:, None]
    far = 4 * (np.arange(ND)[None, :] // GY)
    h, l = _halves(np.concatenate([_cos(kz, far, NZ), _sin(kz, far, NZ)], axis=0))
    zf = np.concatenate([h, l], axis=0)
    far = 4 * np.arange(GZ)[None, :]
    factor = np.where(kz == 0, 1.0, 2.0) / float(NX * NY * NZ)
    h, l = _halves(np.concatenate([factor * _cos(kz, far, NZ), factor * _sin(kz, far, NZ)], axis=0).T)
    zi = np.concatenate([h, h, l], axis=1)
    near = np.arange(LANES)[None, :] % 4
    tw = np.stack([_cos(kz, near, NZ), _sin(kz, near, NZ)]).astype(np.float32)
    g, gi = _mode_maps()
    return dict(tf=tf, ti=ti, kf=np.stack(kf), ki=np.stack(ki), zf=zf, zi=zi, tw=tw, g=g, gi=gi, e=_expand_maps(), pick=_pick_map())


def nn(a, b):
    return lax.dot_general(a, b, (((1,), (0,)), ((), ())), preferred_element_type=F32)


def nt(a, b):
    return lax.dot_general(a, b, (((1,), (1,)), ((), ())), preferred_element_type=F32)


def halves(value):
    high = value.astype(BF)
    low = (value - high.astype(F32)).astype(BF)
    return high, low


def lanes_of(value):
    return lax.broadcasted_iota(jnp.int32, value.shape, 1)


def swap_blocks(tiles, width):
    tiles = list(tiles)
    block = lax.rem(lanes_of(tiles[0]) // width, 8)
    for bit in (1, 2, 4):
        upper = lax.rem(block // bit, 2) == 1
        shift = bit * width
        for i in range(8):
            if i & bit:
                continue
            a, b = tiles[i], tiles[i | bit]
            tiles[i] = jnp.where(upper, pltpu.roll(b, shift, 1), a)
            tiles[i | bit] = jnp.where(upper, b, pltpu.roll(a, LANES - shift, 1))
    return tiles


def forward_pair(pair, kf, tf, sx, ey, n):
    parts = []
    for volume in pair:
        ah, al = halves(volume)
        b = nn(kf[...], ah)
        parts.append(halves(b[:144] + b[144:] + nn(kf[:144], al)))
    (h0, l0), (h1, l1) = parts
    o = nn(h0, tf[0]) + nn(h1, tf[1])
    o = o[:, :LANES] + o[:, LANES:] + nn(l0, tf[0, :, :LANES]) + nn(l1, tf[1, :, :LANES])
    sx[n] = o[:LANES].T
    ey[pl.ds(pl.multiple_of(n * 16, 16), 16), :] = o[LANES:]


def pack(sx, ey, sb):
    for r in range(MAIN):
        tiles = swap_blocks([sx[2 * r + i // 4, pl.ds((i // 2 % 2) * 64 + (i % 2) * 16, 16), :] for i in range(8)], 16)
        for q in range(8):
            sb[r, 16 * q : 16 * q + 16, :] = tiles[q]
    turned = [ey[0:LANES, :].T, ey[LANES : 2 * LANES, :].T]
    slot = lax.rem(lax.broadcasted_iota(jnp.int32, (16, LANES), 1) // 4, 4)
    block = lax.broadcasted_iota(jnp.int32, (16, LANES), 1) // 16
    zero = jnp.zeros((16, LANES), F32)
    by_ch = [
        [
            sum((jnp.where(slot == h, t[64 * ch + 16 * h : 64 * ch + 16 * h + 16], zero) for h in range(3)), zero)
            for ch in range(2)
        ]
        for t in turned
    ]
    none = jnp.zeros((8, LANES), F32)
    top = lax.broadcasted_iota(jnp.int32, (16, LANES), 0) == 0
    for e in range(EDGE - MAIN):
        tiles = []
        edge = zero
        for c in range(4):
            for k in range(2):
                r = 2 * e + k
                if r == MAIN:
                    tiles.append(none)
                    continue
                n = 2 * r + c // 2
                tiles.append(sx[n, pl.ds((c % 2) * 64 + 32, 8), :])
                to = 2 * c + 1 - k
                moved = pltpu.roll(by_ch[n // 8][c % 2], (to - n % 8) % 8 * 16, 1)
                edge = edge + jnp.where(block == to, moved, zero)
        tiles = swap_blocks(tiles, 16)
        sb[MAIN + e, 0:8, :] = jnp.where(top[:8], tiles[0], edge[:8])
        sb[MAIN + e, 8:16, :] = edge[8:]
        sb[EDGE + e, 0:16, :] = edge
        for q in range(1, 8):
            sb[MAIN + e, 16 * q : 16 * q + 8, :] = tiles[q]


def unpack(rb, cx, ex):
    for r in range(MAIN):
        tiles = swap_blocks([rb[r, 16 * q : 16 * q + 16, :] for q in range(8)], 16)
        for i in range(8):
            cx[2 * r + i // 4, pl.ds((i // 2 % 2) * 64 + (i % 2) * 16, 16), :] = tiles[i]
    top = lax.broadcasted_iota(jnp.int32, (16, LANES), 0) == 0
    rows = []
    for e in range(EDGE - MAIN):
        tiles = [rb[MAIN + e, 0:8, :]]
        tiles += [jnp.where(top[:8], rb[MAIN + e, 16 * q : 16 * q + 8, :], 0.0) for q in range(1, 8)]
        tiles = swap_blocks(tiles, 16)
        for c in range(4):
            for k in range(2):
                r = 2 * e + k
                if r < MAIN:
                    cx[2 * r + c // 2, pl.ds((c % 2) * 64 + 32, 8), :] = tiles[2 * c + k]
        rows.append(jnp.where(top, rb[EDGE + e, 0:16, :], rb[MAIN + e, 0:16, :]))
    turned = jnp.concatenate(rows + [jnp.zeros((80, LANES), F32)], axis=0).T
    row = lax.broadcasted_iota(jnp.int32, (16, LANES), 0)
    block = lax.broadcasted_iota(jnp.int32, (16, LANES), 1) // 16
    keep = lax.rem(block, 4) == row // 4
    zero = jnp.zeros((16, LANES), F32)
    for r in range(MAIN):
        for c in range(4):
            at = 32 * c + 16 * (1 - r % 2)
            e = jnp.where(block == r // 2, turned[at : at + 16], zero)
            for shift in (16, 32, 64):
                e = e + pltpu.roll(e, shift, 1)
            ex[2 * r + c // 2, pl.ds((c % 2) * 16, 16), :] = jnp.where(keep, e, zero)


def clear_rest(cx):
    for n in range(PAIRS):
        for ch in range(2):
            cx[n, pl.ds(64 * ch + 40, 24), :] = jnp.zeros((24, LANES), F32)


def inverse_pair(cx, ex, n, ki, ti):
    c = cx[n].T
    low = lanes_of(c) < 64
    other = pltpu.roll(c, 64, 1)
    d = jnp.concatenate([jnp.where(low, c, other), jnp.where(low, other, c)], axis=1)
    dh, dl = halves(d)
    e = ex[n]
    eh, el = halves(jnp.concatenate([e[:16], e[16:]], axis=1))
    one = jnp.concatenate([dh, dh], axis=0)
    two = jnp.concatenate([dl, eh, el, eh, jnp.zeros((80, 256), BF)], axis=0)
    h = nn(ki[:, :256], one) + nn(ki[:, 256:], two)
    hh, hl = halves(h)
    out = []
    for j in range(2):
        high = hh[:, LANES * j : LANES * j + LANES]
        rest = hl[:, LANES * j : LANES * j + LANES]
        mix = jnp.where(lanes_of(high) < 64, high.astype(F32), rest.astype(F32)).astype(BF)
        out.append(nn(jnp.concatenate([mix, high], axis=1), ti[...]))
    return out


def owner_step(rb, sb, wt, g, gi, e_ref, zf, zi, tw, edge, corner, adjoint):
    d = jnp.concatenate([rb[r] for r in range(FULL)], axis=1)
    dh, dl = halves(d)
    zfv = zf[...]
    f = nn(zfv, dh)
    f = f[:32] + f[32:] + nn(zfv[:32], dl)
    cb = tw[0]
    sb_near = tw[1]

    first_half = lax.rem(lax.broadcasted_iota(jnp.int32, (32, LANES), 1) // 16, 2) == 0
    fields = [f[:, r * LANES : (r + 1) * LANES] for r in range(FULL)]
    extras = []
    for e in range(EDGE - MAIN):
        one = jnp.where(edge, fields[MAIN + e], 0.0)
        two = jnp.where(corner, fields[EDGE + e], one)
        extras.append(jnp.where(first_half, one, two))
        extras.append(jnp.where(first_half, pltpu.roll(one, LANES - 16, 1), pltpu.roll(two, 16, 1)))

    def turned(field):
        fc = field[:16]
        fs = field[16:]
        return jnp.concatenate([fc * cb - fs * sb_near, fs * cb + fc * sb_near], axis=1)

    z = jnp.concatenate(
        [jnp.concatenate([turned(fields[r]), turned(extras[r])], axis=1) for r in range(MAIN)], axis=0
    )
    zh, zlow = halves(z)
    x = nn(jnp.concatenate([zh, zlow], axis=0), g[...])
    x = x[:80] + x[80:]
    xre, xim = x[:, :LANES], x[:, LANES:]

    def weight(ri, m, r):
        return wt[pl.ds(((ri * 8 + m) * MAIN + r) * 16, 16), :]

    zero = jnp.zeros((16, LANES), F32)
    if not adjoint:
        pieces = jnp.concatenate(halves(xre) + halves(xim), axis=0)
        yre, yim = [], []
        for m in range(8):
            xm = nn(pieces, e_ref[m])
            xmr = xm[:80] + xm[80:160]
            xmi = xm[160:240] + xm[240:]
            sr, si = zero, zero
            for r in range(MAIN):
                wr, wi = weight(0, m, r), weight(1, m, r)
                ar, ai = xmr[16 * r : 16 * r + 16], xmi[16 * r : 16 * r + 16]
                sr = sr + wr * ar - wi * ai
                si = si + wr * ai + wi * ar
            yre.append(sr)
            yim.append(si)
        vre = swap_blocks(yre, 4)[:MAIN]
        vim = swap_blocks(yim, 4)[:MAIN]
        v = jnp.concatenate([jnp.concatenate([a, b], axis=1) for a, b in zip(vre, vim)], axis=0)
    else:
        gre = swap_blocks([xre[16 * t : 16 * t + 16] for t in range(MAIN)] + [zero] * 3, 4)
        gim = swap_blocks([xim[16 * t : 16 * t + 16] for t in range(MAIN)] + [zero] * 3, 4)
        total = None
        for m in range(8):
            yr, yi = [], []
            for r in range(MAIN):
                wr, wi = weight(0, m, r), weight(1, m, r)
                yr.append(wr * gre[m] + wi * gim[m])
                yi.append(wr * gim[m] - wi * gre[m])
            pieces = jnp.concatenate(
                halves(jnp.concatenate(yr, axis=0)) + halves(jnp.concatenate(yi, axis=0)), axis=0
            )
            part = nt(pieces, e_ref[m])
            total = part if total is None else total + part
        v = jnp.concatenate([total[:80] + total[80:160], total[160:240] + total[240:]], axis=1)
    vh, vl = halves(v)
    c = nn(jnp.concatenate([vh, vl], axis=0), gi[...])
    c = c[:80] + c[80:]

    def back(t, half):
        cc = c[16 * t : 16 * t + 16, half * 256 : half * 256 + LANES]
        cs = c[16 * t : 16 * t + 16, half * 256 + LANES : half * 256 + 256]
        return jnp.concatenate([cc * cb + cs * sb_near, cs * cb - cc * sb_near], axis=0)

    edges, corners = [], []
    none = jnp.zeros((32, LANES), F32)
    for e in range(EDGE - MAIN):
        one = back(2 * e, 1)
        two = back(2 * e + 1, 1) if 2 * e + 1 < MAIN else none
        low = jnp.where(first_half, one, pltpu.roll(two, 16, 1))
        high = jnp.where(first_half, pltpu.roll(two, LANES - 16, 1), one)
        edges.append(low + jnp.where(corner, 0.0, high))
        corners.append(high)
    r = jnp.concatenate([back(t, 0) for t in range(MAIN)] + edges + corners, axis=1)
    rh, rl = halves(r)
    out = nn(zi[...], jnp.concatenate([rh, rl, rh], axis=0))
    for t in range(FULL):
        sb[t] = out[:, t * LANES : (t + 1) * LANES]


def owner_of(z):
    i = z // 16
    p = lax.rem(z * (1 - 2 * i) + 32 * i, 16)
    return p, i, lax.rem(i + p, 2)


def group_of(p, h, y):
    return 4 * h + lax.rem(y + 8 - p // 2, 4)


def owner_device(p, q):
    i = lax.rem(q // 4 + p, 2)
    first = (16 - p) // 16
    z = p + i * (32 - 2 * p - 16 * first)
    y = lax.rem(lax.rem(q, 4) + p // 2, 4)
    return z, y


def weight_step(wv, ws, pick, k):
    for ri in range(2):
        block = jnp.concatenate([wv[pl.ds(k * 800 + c * 40 + ri, 32, stride=2), :] for c in range(C)], axis=0)
        bh, bl = halves(block)
        rows = nt(pick, bh) + nt(pick, bl)
        for j in range(4):
            tiles = [rows[8 * j : 8 * j + 8, r * LANES : (r + 1) * LANES] for r in range(MAIN)]
            lane = lanes_of(tiles[0])
            for r in range(4):
                one = pltpu.roll(tiles[4], (20 - 32 * r) % LANES, 1)
                two = pltpu.roll(tiles[4], (40 - 32 * r) % LANES, 1)
                tile = jnp.where((lane >= 20) & (lane < 32), one, tiles[r])
                tile = jnp.where((lane >= 52) & (lane < 60), two, tile)
                ws[pl.ds(((ri * 4 + j) * 4 + r) * 4 + k, 8, stride=WROWS), :] = tile


def weight_spread(wb, wt, n):
    ri = n // 4
    j = lax.rem(n, 4)
    for k in range(4):
        tiles = [wb[pl.ds((n * 4 + r) * 4 + k, 8, stride=WROWS), :] for r in range(4)]
        lane = lanes_of(tiles[0])
        last = jnp.zeros_like(tiles[0])
        for r in range(4):
            one = pltpu.roll(tiles[r], (32 * r - 20) % LANES, 1)
            two = pltpu.roll(tiles[r], (32 * r - 40) % LANES, 1)
            last = jnp.where((lane >= 32 * r) & (lane < 32 * r + 12), one, last)
            last = jnp.where((lane >= 32 * r + 12) & (lane < 32 * r + 20), two, last)
        for r, v in enumerate(tiles + [last]):
            base = ((ri * 8 + j) * MAIN + r) * 16 + k
            for i in range(2):
                wt[pl.ds(base + i * 4 * MAIN * 16, 4, stride=4), :] = v[4 * i : 4 * i + 4]


def mix_maps(pw):
    ones = jnp.where(
        lax.broadcasted_iota(jnp.int32, (C * 8, C), 0) // 8 == lax.broadcasted_iota(jnp.int32, (C * 8, C), 1), 1.0, 0.0
    ).astype(BF)
    shape = (C * 8, C * 8)
    same = lax.rem(lax.broadcasted_iota(jnp.int32, shape, 0), 8) == lax.rem(lax.broadcasted_iota(jnp.int32, shape, 1), 8)
    fwd, adj = [], []
    for part in halves(pw[...]):
        rows = nn(ones, part).astype(BF)
        fwd.append(jnp.where(same, nt(ones, rows), 0.0).astype(BF))
        adj.append(jnp.where(same, nt(rows, ones), 0.0).astype(BF))
    return jnp.concatenate(fwd, axis=0), jnp.concatenate(adj, axis=0)


def mix_step(maps, src, dst, b):
    rows = pl.ds(pl.multiple_of(b * 8, 8), 8)
    sh, sl = halves(src[:, rows, :].reshape(C * 8, NX))
    o = nn(maps[...], sh)
    o = o[: C * 8] + o[C * 8 :] + nn(maps[: C * 8], sl)
    dst[:, rows, :] = o.reshape(C, 8, NX)


def activate(mixed):
    cdf = 0.5 * (1.0 + lax.erf(mixed * (1.0 / math.sqrt(2.0))))
    density = jnp.exp(-0.5 * mixed * mixed) * (1.0 / math.sqrt(2.0 * math.pi))
    return mixed * cdf, cdf + mixed * density


def loop(first, last, fn, unroll=1):
    def body(i, carry):
        fn(i)
        return carry

    lax.fori_loop(first, last, body, 0, unroll=unroll)


def layer_kernel(
    act, cot, w, pw_in, bias, tf_in, ti_in, kf, ki, zf_in, zi_in, tw_in, g, gi, e_in, pick_in,
    pm, pg, rb4,
    tf, ti, zf, zi, tw, e_ref, pick, pw, av, cv, kfv, kiv, gv, giv, maps, sx, ey, cx, ex, wv, ws, wb, wt, count,
    sb1, rb1, sb2, rb2, sb3, rb3, sb4,
    act_sem, cot_sem, tab_sem, w_send, w_recv, send_sem, recv_sem,
):
    gz = lax.axis_index("gz")
    gy = lax.axis_index("gy")
    p, sign, h = owner_of(gz)
    q = group_of(p, h, gy)
    mine = q * 16 + p
    edge = p * q == 0
    corner = p + q == 0

    def by_kind(fn):
        pl.when(p * q != 0)(lambda: fn(MAIN))
        pl.when((p * q == 0) & (p + q != 0))(lambda: fn(EDGE))
        pl.when(p + q == 0)(lambda: fn(FULL))

    variant = 2 * ((16 - p) // 16) + (8 - q) // 8

    def act_copy(c):
        return pltpu.make_async_copy(act.at[c], av.at[c], act_sem.at[c])

    def cot_copy(c):
        return pltpu.make_async_copy(cot.at[c], cv.at[c], cot_sem.at[c])

    table_copies = [
        pltpu.make_async_copy(kf.at[gy], kfv, tab_sem.at[0]),
        pltpu.make_async_copy(ki.at[gy], kiv, tab_sem.at[1]),
        pltpu.make_async_copy(g.at[variant], gv, tab_sem.at[2]),
        pltpu.make_async_copy(gi.at[variant], giv, tab_sem.at[3]),
        pltpu.make_async_copy(w, wv.at[pl.ds(0, WIN)], tab_sem.at[4]),
    ]
    early = [pltpu.make_async_copy(*pair, tab_sem.at[5 + i]) for i, pair in enumerate([(tf_in, tf), (pick_in, pick)])]
    late = [
        pltpu.make_async_copy(*pair, tab_sem.at[7 + i])
        for i, pair in enumerate([(pw_in, pw), (zf_in, zf), (zi_in, zi), (tw_in, tw), (e_in, e_ref), (ti_in, ti)])
    ]
    late += table_copies[1:4]
    table_copies[0].start()
    early[0].start()
    loop(0, 4, lambda c: act_copy(c).start())

    next_y = [gy] + [lax.rem(gy + j, GY) for j in range(1, GY)]

    def each_peer(fn, per_z):
        own = per_z(gz)
        for j in range(1, GY):
            fn(gz, next_y[j], own)

        def body(_, z):
            z = z + 1
            z = jnp.where(z == GZ, 0, z)
            known = per_z(z)
            for j in range(GY):
                fn(z, next_y[j], known)
            return z

        lax.fori_loop(1, GZ, body, gz)

    barrier = pltpu.get_barrier_semaphore()
    each_peer(
        lambda z, y, _: pl.semaphore_signal(barrier, 1, device_id=(z, y), device_id_type=MESH), lambda z: None
    )

    def exchange_out(n, src, dst):
        def start(z, y, to, at, rows):
            pltpu.make_async_remote_copy(
                src_ref=src.at[pl.ds(at, rows), to],
                dst_ref=dst.at[pl.ds(at, rows), gz * GY + gy],
                send_sem=send_sem.at[n],
                recv_sem=recv_sem.at[n],
                device_id=(z, y),
                device_id_type=MESH,
            ).start()

        def send(z, y, known):
            tp, _, th = known
            tq = group_of(tp, th, y)
            to = tq * 16 + tp
            some = tp * tq
            pl.when(some == 0)(lambda: start(z, y, to, 0, EDGE))
            pl.when(some != 0)(lambda: start(z, y, to, 0, MAIN))

        def keep(rows):
            pltpu.make_async_copy(
                src.at[pl.ds(0, rows), mine], dst.at[pl.ds(0, rows), gz * GY + gy], recv_sem.at[n]
            ).start()

        each_peer(send, owner_of)
        by_kind(keep)
        pl.when(p + q != 0)(lambda: start(0, 0, 0, EDGE, FULL - EDGE))

    def exchange_back(n, src, dst):
        def start_all(rows):
            def send(z, y, _):
                pltpu.make_async_remote_copy(
                    src_ref=src.at[pl.ds(0, rows), z],
                    dst_ref=dst.at[pl.ds(0, rows), mine],
                    send_sem=send_sem.at[n],
                    recv_sem=recv_sem.at[n],
                    device_id=(z, y),
                    device_id_type=MESH,
                ).start()

            pltpu.make_async_copy(src.at[pl.ds(0, rows), gz], dst.at[pl.ds(0, rows), mine], recv_sem.at[n]).start()
            each_peer(send, lambda z: None)

        by_kind(start_all)

    def await_rows(rows, sem):
        pltpu.make_async_copy(count.at[pl.ds(0, rows)], count.at[pl.ds(0, rows)], sem).wait()

    def received_out(n):
        by_kind(lambda rows: await_rows(ND * rows, recv_sem.at[n]))

    def received_back(n):
        await_rows(ND * MAIN + 23 * (EDGE - MAIN) + (FULL - EDGE), recv_sem.at[n])

    def sent_out(n):
        most = (ND - 1) * MAIN + (FULL - EDGE)
        others = {MAIN: most + 23 * (EDGE - MAIN), EDGE: most + 22 * (EDGE - MAIN), FULL: (ND - 1) * MAIN + 22 * (EDGE - MAIN)}
        by_kind(lambda rows: await_rows(others[rows], send_sem.at[n]))

    def sent_back(n):
        by_kind(lambda rows: await_rows((ND - 1) * rows, send_sem.at[n]))

    loop(4, C, lambda c: act_copy(c).start())
    table_copies[4].start()
    early[1].start()
    for copy in late:
        copy.start()
    loop(0, C, lambda c: cot_copy(c).start())

    wv[pl.ds(WIN, 64), :] = jnp.zeros((64, 32), F32)
    table_copies[0].wait()
    early[0].wait()

    def first(n):
        act_copy(2 * n).wait()
        act_copy(2 * n + 1).wait()
        forward_pair([av[2 * n], av[2 * n + 1]], kfv, tf, sx, ey, n)

    loop(0, 5, first, 5)
    table_copies[4].wait()
    early[1].wait()
    pickv = pick[...]
    loop(0, 4, lambda k: weight_step(wv, ws, pickv, k))
    pl.semaphore_wait(barrier, ND - 1)
    slot = (sign * 4 + gy) * WROWS

    def send_weights(to):
        z, y = owner_device(p, to)

        @pl.when(to == q)
        def _():
            pltpu.make_async_copy(ws.at[pl.ds(to * WROWS, WROWS)], wb.at[pl.ds(slot, WROWS)], w_recv).start()

        @pl.when(to != q)
        def _():
            pltpu.make_async_remote_copy(
                src_ref=ws.at[pl.ds(to * WROWS, WROWS)],
                dst_ref=wb.at[pl.ds(slot, WROWS)],
                send_sem=w_send,
                recv_sem=w_recv,
                device_id=(z, y),
                device_id_type=MESH,
            ).start()

    loop(0, 8, send_weights)
    loop(5, PAIRS, first, 5)
    pack(sx, ey, sb1)
    exchange_out(0, sb1, rb1)

    for copy in late:
        copy.wait()
    fwd, adj = mix_maps(pw)
    maps[0] = fwd
    maps[1] = adj
    steps = CELLS // 8
    loop(0, steps // 2, lambda b: mix_step(maps.at[0], av, pm, b), 2)
    clear_rest(cx)
    await_rows(8 * WROWS, w_recv)
    loop(0, 8, lambda n: weight_spread(wb, wt, n), 2)

    received_out(0)
    owner_step(rb1, sb2, wt, gv, giv, e_ref, zf, zi, tw, edge, corner, False)
    exchange_back(1, sb2, rb2)
    loop(steps // 2, steps, lambda b: mix_step(maps.at[0], av, pm, b), 2)
    received_back(1)
    unpack(rb2, cx, ex)

    def middle(n):
        pair = inverse_pair(cx, ex, n, kiv, ti)
        for j in range(2):
            o = 2 * n + j
            value, slope = activate(pm[o] + bias[o] + pair[j])
            pm[o] = value
            cv[o] = cv[o] * slope

    loop(0, C, lambda o: cot_copy(o).wait())
    loop(0, PAIRS, middle, PAIRS)
    loop(0, PAIRS, lambda n: forward_pair([cv[2 * n], cv[2 * n + 1]], kfv, tf, sx, ey, n), PAIRS)
    pack(sx, ey, sb3)
    exchange_out(2, sb3, rb3)
    loop(0, steps // 2, lambda b: mix_step(maps.at[1], cv, pg, b), 2)
    received_out(2)
    owner_step(rb3, sb4, wt, gv, giv, e_ref, zf, zi, tw, edge, corner, True)
    exchange_back(3, sb4, rb4)
    loop(steps // 2, steps, lambda b: mix_step(maps.at[1], cv, pg, b), 2)
    sent_out(0)
    sent_back(1)
    sent_out(2)
    await_rows(7 * WROWS, w_send)
    sent_back(3)
    received_back(3)


def final_kernel(rb, pg, tmp, ti_in, ki, out, grad, ti, cx, ex, kiv, gv, sem, out_sem, grad_sem):
    gy = lax.axis_index("gy")

    def give(c):
        return pltpu.make_async_copy(tmp.at[c], out.at[c], out_sem.at[c])

    def grad_copy(c):
        return pltpu.make_async_copy(gv.at[c], grad.at[c], grad_sem.at[c])

    table_copies = [
        pltpu.make_async_copy(ki.at[gy], kiv, sem.at[0]),
        pltpu.make_async_copy(ti_in, ti, sem.at[1]),
    ]
    for copy in table_copies:
        copy.start()
    loop(0, C, lambda c: give(c).start())
    clear_rest(cx)
    unpack(rb, cx, ex)
    for copy in table_copies:
        copy.wait()

    def finish(n):
        pair = inverse_pair(cx, ex, n, kiv, ti)
        for j in range(2):
            gv[2 * n + j] = pg[2 * n + j] + pair[j]

    half = C // 2
    for first in (0, half):
        loop(first // 2, (first + half) // 2, finish, half // 2)
        loop(first, first + half, lambda c: grad_copy(c).start())
    loop(0, C, lambda c: give(c).wait())
    loop(0, C, lambda c: grad_copy(c).wait())


def local(activation, pointwise, bias_term, spectral_weight, cotangent):
    t = {name: jnp.asarray(value) for name, value in tables().items()}
    volume = (C, CELLS, NX)
    any_spec = pl.BlockSpec(memory_space=pl.ANY)
    vmem = pl.BlockSpec(memory_space=pltpu.VMEM)
    smem = pl.BlockSpec(memory_space=pltpu.SMEM)
    message = pltpu.VMEM((FULL, ND, LANES), F32)
    reply = pltpu.VMEM((FULL, GZ, LANES), F32)
    weights = pltpu.VMEM((8 * WROWS, LANES), F32)
    fields = pltpu.VMEM((PAIRS, LANES, LANES), F32)
    edges = pltpu.VMEM((PAIRS, 32, LANES), F32)
    dma = pltpu.SemaphoreType.DMA

    def hbm(x):
        return pltpu.with_memory_space_constraint(x, pltpu.HBM)

    def kept(x):
        return pltpu.with_memory_space_constraint(x, pltpu.VMEM)

    tmp, pg, rb = pl.pallas_call(
        layer_kernel,
        out_shape=[pltpu.VMEM(volume, F32), pltpu.VMEM(volume, F32), message],
        in_specs=[
            any_spec, any_spec, any_spec, any_spec, smem,
            any_spec, any_spec, any_spec, any_spec, any_spec, any_spec, any_spec, any_spec, any_spec, any_spec, any_spec,
        ],
        out_specs=[vmem, vmem, vmem],
        scratch_shapes=[
            pltpu.VMEM((2, NX, 256), BF),
            pltpu.VMEM((256, NX), BF),
            pltpu.VMEM((64, ND), BF),
            pltpu.VMEM((GZ, 96), BF),
            pltpu.VMEM((2, 16, LANES), F32),
            pltpu.VMEM((8, LANES, LANES), BF),
            pltpu.VMEM((32, 32), BF),
            pltpu.VMEM((C, C), F32),
            pltpu.VMEM(volume, F32),
            pltpu.VMEM(volume, F32),
            pltpu.VMEM((288, CELLS), BF),
            pltpu.VMEM((CELLS, 512), BF),
            pltpu.VMEM((512, 256), BF),
            pltpu.VMEM((256, 512), BF),
            pltpu.VMEM((2, C * 16, C * 8), BF),
            fields,
            pltpu.VMEM((256, LANES), F32),
            fields,
            edges,
            pltpu.VMEM((WIN + 64, 32), F32),
            weights,
            weights,
            pltpu.VMEM((16 * MAIN * 16, LANES), F32),
            pltpu.VMEM((ND * FULL, LANES), F32),
        ]
        + [message, message, reply, message, message, message, reply]
        + [dma((C,)), dma((C,)), dma((13,)), dma, dma, dma((4,)), dma((4,))],
        compiler_params=pltpu.CompilerParams(
            collective_id=0, has_side_effects=True, vmem_limit_bytes=36 * 1024 * 1024
        ),
        name="layer",
    )(
        hbm(activation.reshape(volume)), hbm(cotangent.reshape(volume)),
        hbm(jnp.transpose(spectral_weight[0], (0, 2, 3, 1, 4)).reshape(WIN, 32)), hbm(pointwise), bias_term,
        *(hbm(t[name]) for name in ("tf", "ti", "kf", "ki", "zf", "zi", "tw", "g", "gi", "e", "pick")),
    )
    out, grad = pl.pallas_call(
        final_kernel,
        out_shape=[jax.ShapeDtypeStruct(volume, F32), jax.ShapeDtypeStruct(volume, F32)],
        in_specs=[vmem, vmem, vmem, any_spec, any_spec],
        out_specs=[any_spec, any_spec],
        scratch_shapes=[
            pltpu.VMEM((256, NX), BF), fields, edges, pltpu.VMEM((CELLS, 512), BF), pltpu.VMEM(volume, F32),
            dma((2,)), dma((C,)), dma((C,)),
        ],
        compiler_params=pltpu.CompilerParams(vmem_limit_bytes=24 * 1024 * 1024),
        name="final",
    )(kept(rb), kept(pg), kept(tmp), hbm(t["ti"]), hbm(t["ki"]))
    shape = (C, ZL, YL, NX)
    return out.reshape(shape), grad.reshape(shape)


def solution(mesh):
    return jax.shard_map(
        local,
        mesh=mesh,
        in_specs=(
            P(None, "gz", "gy", None),
            P(),
            P(),
            P("gz", "gy", None, None, None, None),
            P(None, "gz", "gy", None),
        ),
        out_specs=(P(None, "gz", "gy", None), P(None, "gz", "gy", None)),
        check_vma=False,
    )
```

```python
import functools
import math

import jax
import jax.numpy as jnp
import ml_dtypes
import numpy as np
from jax import lax
from jax.experimental import pallas as pl
from jax.experimental.pallas import tpu as pltpu
from jax.sharding import PartitionSpec as P

C = 20
M = 16
NX = 256
NY = 256
NZ = 128
GZ = 32
GY = 4
ND = GZ * GY
ZL = NZ // GZ
YL = NY // GY
CELLS = ZL * YL
LANES = 128
PAIRS = C // 2
MAIN = 5
EDGE = 8
FULL = 11
WROWS = 128
WIN = ZL * C * C * 2
MESH = pl.DeviceIdType.MESH
BF = jnp.bfloat16
F32 = jnp.float32


def _cos(k, n, length):
    return np.cos(2.0 * np.pi * ((k * n) % length) / length)


def _sin(k, n, length):
    return np.sin(2.0 * np.pi * ((k * n) % length) / length)


def _halves(table):
    high = table.astype(np.float32).astype(ml_dtypes.bfloat16)
    low = (table - high.astype(np.float64)).astype(ml_dtypes.bfloat16)
    return high, low


def _x_table():
    x = np.arange(NX)
    rows = np.zeros((64, NX))
    for p in range(M):
        rows[p] = _cos(p, x, NX)
        rows[16 + p] = _sin(p, x, NX) if p else _cos(16, x, NX)
    rows[32] = _sin(16, x, NX)
    return rows


def _y_table(gy):
    y = gy * YL + np.arange(YL)
    rows = np.zeros((144, ZL, YL))
    for q in range(8):
        basis = [
            _cos(q, y, NY),
            _sin(q, y, NY) if q else _cos(16, y, NY),
            _cos(q + 8, y, NY),
            _sin(q + 8, y, NY),
        ]
        for yb in range(4):
            for zl in range(ZL):
                rows[q * 16 + yb * 4 + zl, zl] = basis[yb]
    for s in range(4):
        for zl in range(ZL):
            rows[128 + s * 4 + zl, zl] = _sin(16, y, NY)
    return rows.reshape(144, CELLS)


def _mode_tables(p_zero, q_zero):
    xs = [([1, 0, 0], [0, 0, 0]), ([0, 1, 0], [0, 0, -1])] if p_zero else [([1, 0, 0], [0, 1, 0]), ([1, 0, 0], [0, -1, 0])]
    ys = [
        ([1, 0, 0, 0, 0], [0, 0, 0, 0, 0]),
        ([0, 1, 0, 0, 0], [0, 0, 0, 0, -1]),
    ] if q_zero else [([1, 0, 0, 0, 0], [0, 1, 0, 0, 0]), ([1, 0, 0, 0, 0], [0, -1, 0, 0, 0])]
    ys = ys + [([0, 0, 1, 0, 0], [0, 0, 0, 1, 0]), ([0, 0, 1, 0, 0], [0, 0, 0, -1, 0])]
    u = np.zeros((16, 8))
    v = np.zeros((16, 8))
    for i, (cx, sx) in enumerate(xs):
        for j, (cy, sy) in enumerate(ys):
            both_u = np.outer(cx, cy) - np.outer(sx, sy)
            both_v = np.outer(sx, cy) + np.outer(cx, sy)
            for xb in range(3):
                for yb in range(5):
                    if yb < 4:
                        slot = xb * 4 + yb
                    else:
                        slot = 12 + xb
                    u[slot, i * 4 + j] = both_u[xb, yb]
                    v[slot, i * 4 + j] = both_v[xb, yb]
    return u, v


def _mode_maps():
    g = np.zeros((4, 512, 256))
    gi = np.zeros((4, 256, 512))
    for variant in range(4):
        u, v = _mode_tables(variant // 2, variant % 2)
        gv = np.zeros((2, 2, 4, 8, 4, 2, 4, 8, 4))
        giv = np.zeros((2, 4, 8, 4, 2, 2, 4, 8, 4))
        for half in range(2):
            us = u[half * 8 : half * 8 + 8]
            vs = v[half * 8 : half * 8 + 8]
            for ch in range(4):
                for zl in range(4):
                    for rep in range(4):
                        gv[half, 0, ch, :, zl, 0, rep, :, ch] = us
                        gv[half, 1, ch, :, zl, 0, rep, :, ch] = -vs
                        gv[half, 0, ch, :, zl, 1, rep, :, ch] = -vs
                        gv[half, 1, ch, :, zl, 1, rep, :, ch] = -us
                        giv[0, rep, :, ch, half, 0, ch, :, zl] = us.T
                        giv[1, rep, :, ch, half, 0, ch, :, zl] = -vs.T
                        giv[0, rep, :, ch, half, 1, ch, :, zl] = -vs.T
                        giv[1, rep, :, ch, half, 1, ch, :, zl] = -us.T
        g[variant] = gv.reshape(512, 256)
        gi[variant] = giv.reshape(256, 512)
    return g.astype(ml_dtypes.bfloat16), gi.astype(ml_dtypes.bfloat16)


def _expand_maps():
    e = np.zeros((8, 4, 8, 4, 4, 32))
    for m in range(8):
        for ch in range(4):
            e[m, 0, m, ch, ch, :] = 1
    return e.reshape(8, 128, 128).astype(ml_dtypes.bfloat16)


def _pick_map():
    pick = np.zeros((32, 32))
    for q in range(8):
        for j, k in enumerate([q, (-q if q else -16), q + 8, -(q + 8)]):
            pick[j * 8 + q, k % 32] = 1
    return pick.astype(ml_dtypes.bfloat16)


@functools.cache
def tables():
    xh, xl = _halves(_x_table())
    tf = np.zeros((2, NX, 256), ml_dtypes.bfloat16)
    for j in range(2):
        tf[j, :, 64 * j : 64 * j + 64] = xh.T
        tf[j, :, 128 + 64 * j : 192 + 64 * j] = xl.T
    ti = np.concatenate([xh, xh, xl, np.zeros_like(xl)], axis=0)
    kf, ki = [], []
    for gy in range(GY):
        h, l = _halves(_y_table(gy))
        kf.append(np.concatenate([h, l], axis=0))
        ht, lt = h.T, l.T
        pad = np.zeros((CELLS, 80), ml_dtypes.bfloat16)
        ki.append(np.concatenate([ht[:, :128], lt[:, :128], ht[:, :128], ht[:, 128:], ht[:, 128:], lt[:, 128:], pad], axis=1))
    kz = np.arange(M)[:, None]
    far = 4 * (np.arange(ND)[None, :] // GY)
    h, l = _halves(np.concatenate([_cos(kz, far, NZ), _sin(kz, far, NZ)], axis=0))
    zf = np.concatenate([h, l], axis=0)
    far = 4 * np.arange(GZ)[None, :]
    factor = np.where(kz == 0, 1.0, 2.0) / float(NX * NY * NZ)
    h, l = _halves(np.concatenate([factor * _cos(kz, far, NZ), factor * _sin(kz, far, NZ)], axis=0).T)
    zi = np.concatenate([h, h, l], axis=1)
    near = np.arange(LANES)[None, :] % 4
    tw = np.stack([_cos(kz, near, NZ), _sin(kz, near, NZ)]).astype(np.float32)
    g, gi = _mode_maps()
    return dict(tf=tf, ti=ti, kf=np.stack(kf), ki=np.stack(ki), zf=zf, zi=zi, tw=tw, g=g, gi=gi, e=_expand_maps(), pick=_pick_map())


def nn(a, b):
    return lax.dot_general(a, b, (((1,), (0,)), ((), ())), preferred_element_type=F32)


def nt(a, b):
    return lax.dot_general(a, b, (((1,), (1,)), ((), ())), preferred_element_type=F32)


def halves(value):
    high = value.astype(BF)
    low = (value - high.astype(F32)).astype(BF)
    return high, low


def lanes_of(value):
    return lax.broadcasted_iota(jnp.int32, value.shape, 1)


def swap_blocks(tiles, width):
    tiles = list(tiles)
    block = lax.rem(lanes_of(tiles[0]) // width, 8)
    for bit in (1, 2, 4):
        upper = lax.rem(block // bit, 2) == 1
        shift = bit * width
        for i in range(8):
            if i & bit:
                continue
            a, b = tiles[i], tiles[i | bit]
            tiles[i] = jnp.where(upper, pltpu.roll(b, shift, 1), a)
            tiles[i | bit] = jnp.where(upper, b, pltpu.roll(a, LANES - shift, 1))
    return tiles


def forward_pair(pair, kf, tf, sx, ey, n):
    parts = []
    for volume in pair:
        ah, al = halves(volume)
        b = nn(kf[...], ah)
        parts.append(halves(b[:144] + b[144:] + nn(kf[:144], al)))
    (h0, l0), (h1, l1) = parts
    o = nn(h0, tf[0]) + nn(h1, tf[1])
    o = o[:, :LANES] + o[:, LANES:] + nn(l0, tf[0, :, :LANES]) + nn(l1, tf[1, :, :LANES])
    sx[n] = o[:LANES].T
    ey[pl.ds(pl.multiple_of(n * 16, 16), 16), :] = o[LANES:]


def pack(sx, ey, sb):
    for r in range(MAIN):
        tiles = swap_blocks([sx[2 * r + i // 4, pl.ds((i // 2 % 2) * 64 + (i % 2) * 16, 16), :] for i in range(8)], 16)
        for q in range(8):
            sb[r, 16 * q : 16 * q + 16, :] = tiles[q]
    turned = [ey[0:LANES, :].T, ey[LANES : 2 * LANES, :].T]
    slot = lax.rem(lax.broadcasted_iota(jnp.int32, (16, LANES), 1) // 4, 4)
    block = lax.broadcasted_iota(jnp.int32, (16, LANES), 1) // 16
    zero = jnp.zeros((16, LANES), F32)
    by_ch = [
        [
            sum((jnp.where(slot == h, t[64 * ch + 16 * h : 64 * ch + 16 * h + 16], zero) for h in range(3)), zero)
            for ch in range(2)
        ]
        for t in turned
    ]
    none = jnp.zeros((8, LANES), F32)
    top = lax.broadcasted_iota(jnp.int32, (16, LANES), 0) == 0
    for e in range(EDGE - MAIN):
        tiles = []
        edge = zero
        for c in range(4):
            for k in range(2):
                r = 2 * e + k
                if r == MAIN:
                    tiles.append(none)
                    continue
                n = 2 * r + c // 2
                tiles.append(sx[n, pl.ds((c % 2) * 64 + 32, 8), :])
                to = 2 * c + 1 - k
                moved = pltpu.roll(by_ch[n // 8][c % 2], (to - n % 8) % 8 * 16, 1)
                edge = edge + jnp.where(block == to, moved, zero)
        tiles = swap_blocks(tiles, 16)
        sb[MAIN + e, 0:8, :] = jnp.where(top[:8], tiles[0], edge[:8])
        sb[MAIN + e, 8:16, :] = edge[8:]
        sb[EDGE + e, 0:16, :] = edge
        for q in range(1, 8):
            sb[MAIN + e, 16 * q : 16 * q + 8, :] = tiles[q]


def unpack(rb, cx, ex):
    for r in range(MAIN):
        tiles = swap_blocks([rb[r, 16 * q : 16 * q + 16, :] for q in range(8)], 16)
        for i in range(8):
            cx[2 * r + i // 4, pl.ds((i // 2 % 2) * 64 + (i % 2) * 16, 16), :] = tiles[i]
    top = lax.broadcasted_iota(jnp.int32, (16, LANES), 0) == 0
    rows = []
    for e in range(EDGE - MAIN):
        tiles = [rb[MAIN + e, 0:8, :]]
        tiles += [jnp.where(top[:8], rb[MAIN + e, 16 * q : 16 * q + 8, :], 0.0) for q in range(1, 8)]
        tiles = swap_blocks(tiles, 16)
        for c in range(4):
            for k in range(2):
                r = 2 * e + k
                if r < MAIN:
                    cx[2 * r + c // 2, pl.ds((c % 2) * 64 + 32, 8), :] = tiles[2 * c + k]
        rows.append(jnp.where(top, rb[EDGE + e, 0:16, :], rb[MAIN + e, 0:16, :]))
    turned = jnp.concatenate(rows + [jnp.zeros((80, LANES), F32)], axis=0).T
    row = lax.broadcasted_iota(jnp.int32, (16, LANES), 0)
    block = lax.broadcasted_iota(jnp.int32, (16, LANES), 1) // 16
    keep = lax.rem(block, 4) == row // 4
    zero = jnp.zeros((16, LANES), F32)
    for r in range(MAIN):
        for c in range(4):
            at = 32 * c + 16 * (1 - r % 2)
            e = jnp.where(block == r // 2, turned[at : at + 16], zero)
            for shift in (16, 32, 64):
                e = e + pltpu.roll(e, shift, 1)
            ex[2 * r + c // 2, pl.ds((c % 2) * 16, 16), :] = jnp.where(keep, e, zero)


def clear_rest(cx):
    for n in range(PAIRS):
        for ch in range(2):
            cx[n, pl.ds(64 * ch + 40, 24), :] = jnp.zeros((24, LANES), F32)


def inverse_pair(cx, ex, n, ki, ti):
    c = cx[n].T
    low = lanes_of(c) < 64
    other = pltpu.roll(c, 64, 1)
    d = jnp.concatenate([jnp.where(low, c, other), jnp.where(low, other, c)], axis=1)
    dh, dl = halves(d)
    e = ex[n]
    eh, el = halves(jnp.concatenate([e[:16], e[16:]], axis=1))
    one = jnp.concatenate([dh, dh], axis=0)
    two = jnp.concatenate([dl, eh, el, eh, jnp.zeros((80, 256), BF)], axis=0)
    h = nn(ki[:, :256], one) + nn(ki[:, 256:], two)
    hh, hl = halves(h)
    out = []
    for j in range(2):
        high = hh[:, LANES * j : LANES * j + LANES]
        rest = hl[:, LANES * j : LANES * j + LANES]
        mix = jnp.where(lanes_of(high) < 64, high.astype(F32), rest.astype(F32)).astype(BF)
        out.append(nn(jnp.concatenate([mix, high], axis=1), ti[...]))
    return out


def owner_step(rb, sb, wt, g, gi, e_ref, zf, zi, tw, edge, corner, adjoint, ready):
    d = jnp.concatenate([rb[r] for r in range(FULL)], axis=1)
    dh, dl = halves(d)
    zfv = zf[...]
    f = nn(zfv, dh)
    f = f[:32] + f[32:] + nn(zfv[:32], dl)
    cb = tw[0]
    sb_near = tw[1]

    first_half = lax.rem(lax.broadcasted_iota(jnp.int32, (32, LANES), 1) // 16, 2) == 0
    fields = [f[:, r * LANES : (r + 1) * LANES] for r in range(FULL)]
    extras = []
    for e in range(EDGE - MAIN):
        one = jnp.where(edge, fields[MAIN + e], 0.0)
        two = jnp.where(corner, fields[EDGE + e], one)
        extras.append(jnp.where(first_half, one, two))
        extras.append(jnp.where(first_half, pltpu.roll(one, LANES - 16, 1), pltpu.roll(two, 16, 1)))

    def turned(field):
        fc = field[:16]
        fs = field[16:]
        return jnp.concatenate([fc * cb - fs * sb_near, fs * cb + fc * sb_near], axis=1)

    z = jnp.concatenate(
        [jnp.concatenate([turned(fields[r]), turned(extras[r])], axis=1) for r in range(MAIN)], axis=0
    )
    zh, zlow = halves(z)
    x = nn(jnp.concatenate([zh, zlow], axis=0), g[...])
    x = x[:80] + x[80:]
    xre, xim = x[:, :LANES], x[:, LANES:]

    ready()

    def weight(ri, m, r):
        return wt[pl.ds(((ri * 8 + m) * MAIN + r) * 16, 16), :]

    zero = jnp.zeros((16, LANES), F32)
    if not adjoint:
        pieces = jnp.concatenate(halves(xre) + halves(xim), axis=0)
        yre, yim = [], []
        for m in range(8):
            xm = nn(pieces, e_ref[m])
            xmr = xm[:80] + xm[80:160]
            xmi = xm[160:240] + xm[240:]
            sr, si = zero, zero
            for r in range(MAIN):
                wr, wi = weight(0, m, r), weight(1, m, r)
                ar, ai = xmr[16 * r : 16 * r + 16], xmi[16 * r : 16 * r + 16]
                sr = sr + wr * ar - wi * ai
                si = si + wr * ai + wi * ar
            yre.append(sr)
            yim.append(si)
        vre = swap_blocks(yre, 4)[:MAIN]
        vim = swap_blocks(yim, 4)[:MAIN]
        v = jnp.concatenate([jnp.concatenate([a, b], axis=1) for a, b in zip(vre, vim)], axis=0)
    else:
        gre = swap_blocks([xre[16 * t : 16 * t + 16] for t in range(MAIN)] + [zero] * 3, 4)
        gim = swap_blocks([xim[16 * t : 16 * t + 16] for t in range(MAIN)] + [zero] * 3, 4)
        total = None
        for m in range(8):
            yr, yi = [], []
            for r in range(MAIN):
                wr, wi = weight(0, m, r), weight(1, m, r)
                yr.append(wr * gre[m] + wi * gim[m])
                yi.append(wr * gim[m] - wi * gre[m])
            pieces = jnp.concatenate(
                halves(jnp.concatenate(yr, axis=0)) + halves(jnp.concatenate(yi, axis=0)), axis=0
            )
            part = nt(pieces, e_ref[m])
            total = part if total is None else total + part
        v = jnp.concatenate([total[:80] + total[80:160], total[160:240] + total[240:]], axis=1)
    vh, vl = halves(v)
    c = nn(jnp.concatenate([vh, vl], axis=0), gi[...])
    c = c[:80] + c[80:]

    def back(t, half):
        cc = c[16 * t : 16 * t + 16, half * 256 : half * 256 + LANES]
        cs = c[16 * t : 16 * t + 16, half * 256 + LANES : half * 256 + 256]
        return jnp.concatenate([cc * cb + cs * sb_near, cs * cb - cc * sb_near], axis=0)

    edges, corners = [], []
    none = jnp.zeros((32, LANES), F32)
    for e in range(EDGE - MAIN):
        one = back(2 * e, 1)
        two = back(2 * e + 1, 1) if 2 * e + 1 < MAIN else none
        low = jnp.where(first_half, one, pltpu.roll(two, 16, 1))
        high = jnp.where(first_half, pltpu.roll(two, LANES - 16, 1), one)
        edges.append(low + jnp.where(corner, 0.0, high))
        corners.append(high)
    r = jnp.concatenate([back(t, 0) for t in range(MAIN)] + edges + corners, axis=1)
    rh, rl = halves(r)
    out = nn(zi[...], jnp.concatenate([rh, rl, rh], axis=0))
    for t in range(FULL):
        sb[t] = out[:, t * LANES : (t + 1) * LANES]


def owner_of(z):
    i = z // 16
    p = lax.rem(z * (1 - 2 * i) + 32 * i, 16)
    return p, i, lax.rem(i + p, 2)


def group_of(p, h, y):
    return 4 * h + lax.rem(y + 8 - p // 2, 4)


def owner_device(p, q):
    i = lax.rem(q // 4 + p, 2)
    first = (16 - p) // 16
    z = p + i * (32 - 2 * p - 16 * first)
    y = lax.rem(lax.rem(q, 4) + p // 2, 4)
    return z, y


def weight_step(wv, ws, pick, k):
    for ri in range(2):
        block = jnp.concatenate([wv[pl.ds(k * 800 + c * 40 + ri, 32, stride=2), :] for c in range(C)], axis=0)
        bh, bl = halves(block)
        rows = nt(pick, bh) + nt(pick, bl)
        for j in range(4):
            tiles = [rows[8 * j : 8 * j + 8, r * LANES : (r + 1) * LANES] for r in range(MAIN)]
            lane = lanes_of(tiles[0])
            for r in range(4):
                one = pltpu.roll(tiles[4], (20 - 32 * r) % LANES, 1)
                two = pltpu.roll(tiles[4], (40 - 32 * r) % LANES, 1)
                tile = jnp.where((lane >= 20) & (lane < 32), one, tiles[r])
                tile = jnp.where((lane >= 52) & (lane < 60), two, tile)
                ws[pl.ds(((ri * 4 + j) * 4 + r) * 4 + k, 8, stride=WROWS), :] = tile


def weight_spread(wb, wt, n):
    ri = n // 4
    j = lax.rem(n, 4)
    for k in range(4):
        tiles = [wb[pl.ds((n * 4 + r) * 4 + k, 8, stride=WROWS), :] for r in range(4)]
        lane = lanes_of(tiles[0])
        last = jnp.zeros_like(tiles[0])
        for r in range(4):
            one = pltpu.roll(tiles[r], (32 * r - 20) % LANES, 1)
            two = pltpu.roll(tiles[r], (32 * r - 40) % LANES, 1)
            last = jnp.where((lane >= 32 * r) & (lane < 32 * r + 12), one, last)
            last = jnp.where((lane >= 32 * r + 12) & (lane < 32 * r + 20), two, last)
        for r, v in enumerate(tiles + [last]):
            base = ((ri * 8 + j) * MAIN + r) * 16 + k
            for i in range(2):
                wt[pl.ds(base + i * 4 * MAIN * 16, 4, stride=4), :] = v[4 * i : 4 * i + 4]


def mix_maps(pw):
    ones = jnp.where(
        lax.broadcasted_iota(jnp.int32, (C * 8, C), 0) // 8 == lax.broadcasted_iota(jnp.int32, (C * 8, C), 1), 1.0, 0.0
    ).astype(BF)
    shape = (C * 8, C * 8)
    same = lax.rem(lax.broadcasted_iota(jnp.int32, shape, 0), 8) == lax.rem(lax.broadcasted_iota(jnp.int32, shape, 1), 8)
    fwd, adj = [], []
    for part in halves(pw[...]):
        rows = nn(ones, part).astype(BF)
        fwd.append(jnp.where(same, nt(ones, rows), 0.0).astype(BF))
        adj.append(jnp.where(same, nt(rows, ones), 0.0).astype(BF))
    return jnp.concatenate(fwd, axis=0), jnp.concatenate(adj, axis=0)


def mix_step(maps, src, dst, b):
    rows = pl.ds(pl.multiple_of(b * 8, 8), 8)
    sh, sl = halves(src[:, rows, :].reshape(C * 8, NX))
    o = nn(maps[...], sh)
    o = o[: C * 8] + o[C * 8 :] + nn(maps[: C * 8], sl)
    dst[:, rows, :] = o.reshape(C, 8, NX)


def activate(mixed):
    cdf = 0.5 * (1.0 + lax.erf(mixed * (1.0 / math.sqrt(2.0))))
    density = jnp.exp(-0.5 * mixed * mixed) * (1.0 / math.sqrt(2.0 * math.pi))
    return mixed * cdf, cdf + mixed * density


def loop(first, last, fn, unroll=1):
    def body(i, carry):
        fn(i)
        return carry

    lax.fori_loop(first, last, body, 0, unroll=unroll)


def layer_kernel(
    act, cot, w, pw_in, bias_in, tf_in, ti_in, kf, ki, zf_in, zi_in, tw_in, g, gi, e_in, pick_in,
    pm, pg, rb4, kiv, ti,
    tf, zf, zi, tw, e_ref, pick, pw, bias, av, cv, kfv, gv, giv, maps, sx, ey, cx, ex, wv, ws, wb, wt, count,
    sb1, rb1, sb2, rb2, sb3, rb3, sb4,
    act_sem, cot_sem, tab_sem, w_send, w_recv, send_sem, recv_sem,
):
    gz = lax.axis_index("gz")
    gy = lax.axis_index("gy")
    p, sign, h = owner_of(gz)
    q = group_of(p, h, gy)
    mine = q * 16 + p
    edge = p * q == 0
    corner = p + q == 0

    def by_kind(fn):
        pl.when(p * q != 0)(lambda: fn(MAIN))
        pl.when((p * q == 0) & (p + q != 0))(lambda: fn(EDGE))
        pl.when(p + q == 0)(lambda: fn(FULL))

    variant = 2 * ((16 - p) // 16) + (8 - q) // 8

    def act_copy(c):
        return pltpu.make_async_copy(act.at[c], av.at[c], act_sem.at[c])

    def cot_copy(c):
        return pltpu.make_async_copy(cot.at[c], cv.at[c], cot_sem.at[c])

    table_copies = [
        pltpu.make_async_copy(kf.at[gy], kfv, tab_sem.at[0]),
        pltpu.make_async_copy(ki.at[gy], kiv, tab_sem.at[1]),
        pltpu.make_async_copy(g.at[variant], gv, tab_sem.at[2]),
        pltpu.make_async_copy(gi.at[variant], giv, tab_sem.at[3]),
        pltpu.make_async_copy(w, wv.at[pl.ds(0, WIN)], tab_sem.at[4]),
    ]
    early = [pltpu.make_async_copy(*pair, tab_sem.at[5 + i]) for i, pair in enumerate([(tf_in, tf), (pick_in, pick)])]
    late = [
        pltpu.make_async_copy(*pair, tab_sem.at[7 + i])
        for i, pair in enumerate([(pw_in, pw), (zf_in, zf), (zi_in, zi), (tw_in, tw), (e_in, e_ref), (ti_in, ti), (bias_in, bias)])
    ]
    late += table_copies[1:4]
    table_copies[0].start()
    early[0].start()
    loop(0, 4, lambda c: act_copy(c).start())
    table_copies[4].start()
    early[1].start()

    next_y = [gy] + [lax.rem(gy + j, GY) for j in range(1, GY)]

    def each_peer(fn, per_z):
        own = per_z(gz)
        for j in range(1, GY):
            fn(gz, next_y[j], own)

        def body(_, z):
            z = z + 1
            z = jnp.where(z == GZ, 0, z)
            known = per_z(z)
            for j in range(GY):
                fn(z, next_y[j], known)
            return z

        lax.fori_loop(1, GZ, body, gz)

    barrier = pltpu.get_barrier_semaphore()
    each_peer(
        lambda z, y, _: pl.semaphore_signal(barrier, 1, device_id=(z, y), device_id_type=MESH), lambda z: None
    )

    def exchange_out(n, src, dst):
        def start(z, y, to, at, rows):
            pltpu.make_async_remote_copy(
                src_ref=src.at[pl.ds(at, rows), to],
                dst_ref=dst.at[pl.ds(at, rows), gz * GY + gy],
                send_sem=send_sem.at[n],
                recv_sem=recv_sem.at[n],
                device_id=(z, y),
                device_id_type=MESH,
            ).start()

        def send(z, y, known):
            tp, _, th = known
            tq = group_of(tp, th, y)
            to = tq * 16 + tp
            some = tp * tq
            pl.when(some == 0)(lambda: start(z, y, to, 0, EDGE))
            pl.when(some != 0)(lambda: start(z, y, to, 0, MAIN))

        def keep(rows):
            pltpu.make_async_copy(
                src.at[pl.ds(0, rows), mine], dst.at[pl.ds(0, rows), gz * GY + gy], recv_sem.at[n]
            ).start()

        each_peer(send, owner_of)
        by_kind(keep)
        pl.when(p + q != 0)(lambda: start(0, 0, 0, EDGE, FULL - EDGE))

    def exchange_back(n, src, dst):
        def start_all(rows):
            def send(z, y, _):
                pltpu.make_async_remote_copy(
                    src_ref=src.at[pl.ds(0, rows), z],
                    dst_ref=dst.at[pl.ds(0, rows), mine],
                    send_sem=send_sem.at[n],
                    recv_sem=recv_sem.at[n],
                    device_id=(z, y),
                    device_id_type=MESH,
                ).start()

            pltpu.make_async_copy(src.at[pl.ds(0, rows), gz], dst.at[pl.ds(0, rows), mine], recv_sem.at[n]).start()
            each_peer(send, lambda z: None)

        by_kind(start_all)

    def await_rows(rows, sem):
        pltpu.make_async_copy(count.at[pl.ds(0, rows)], count.at[pl.ds(0, rows)], sem).wait()

    def received_out(n):
        by_kind(lambda rows: await_rows(ND * rows, recv_sem.at[n]))

    def received_back(n):
        await_rows(ND * MAIN + 23 * (EDGE - MAIN) + (FULL - EDGE), recv_sem.at[n])

    def sent_out(n):
        most = (ND - 1) * MAIN + (FULL - EDGE)
        others = {MAIN: most + 23 * (EDGE - MAIN), EDGE: most + 22 * (EDGE - MAIN), FULL: (ND - 1) * MAIN + 22 * (EDGE - MAIN)}
        by_kind(lambda rows: await_rows(others[rows], send_sem.at[n]))

    def sent_back(n):
        by_kind(lambda rows: await_rows((ND - 1) * rows, send_sem.at[n]))

    loop(4, C, lambda c: act_copy(c).start())
    for copy in late:
        copy.start()
    loop(0, C, lambda c: cot_copy(c).start())

    wv[pl.ds(WIN, 64), :] = jnp.zeros((64, 32), F32)
    table_copies[0].wait()
    early[0].wait()

    def first(n):
        act_copy(2 * n).wait()
        act_copy(2 * n + 1).wait()
        forward_pair([av[2 * n], av[2 * n + 1]], kfv, tf, sx, ey, n)

    loop(0, 2, first, 2)
    table_copies[4].wait()
    early[1].wait()
    pickv = pick[...]
    loop(0, 4, lambda k: weight_step(wv, ws, pickv, k))
    pl.semaphore_wait(barrier, ND - 1)
    slot = (sign * 4 + gy) * WROWS

    def send_weights(to):
        z, y = owner_device(p, to)

        @pl.when(to == q)
        def _():
            pltpu.make_async_copy(ws.at[pl.ds(to * WROWS, WROWS)], wb.at[pl.ds(slot, WROWS)], w_recv).start()

        @pl.when(to != q)
        def _():
            pltpu.make_async_remote_copy(
                src_ref=ws.at[pl.ds(to * WROWS, WROWS)],
                dst_ref=wb.at[pl.ds(slot, WROWS)],
                send_sem=w_send,
                recv_sem=w_recv,
                device_id=(z, y),
                device_id_type=MESH,
            ).start()

    loop(0, 8, send_weights)
    loop(2, PAIRS, first, 8)
    pack(sx, ey, sb1)
    exchange_out(0, sb1, rb1)

    for copy in late:
        copy.wait()
    fwd, adj = mix_maps(pw)
    maps[0] = fwd
    maps[1] = adj
    steps = CELLS // 8
    loop(0, steps // 2, lambda b: mix_step(maps.at[0], av, pm, b), 2)
    clear_rest(cx)

    def weights_ready():
        await_rows(8 * WROWS, w_recv)
        loop(0, 8, lambda n: weight_spread(wb, wt, n), 2)

    received_out(0)
    owner_step(rb1, sb2, wt, gv, giv, e_ref, zf, zi, tw, edge, corner, False, weights_ready)
    exchange_back(1, sb2, rb2)
    loop(steps // 2, steps, lambda b: mix_step(maps.at[0], av, pm, b), 2)
    received_back(1)
    unpack(rb2, cx, ex)

    def middle(n):
        pair = inverse_pair(cx, ex, n, kiv, ti)
        for j in range(2):
            o = 2 * n + j
            value, slope = activate(pm[o] + bias[0, o] + pair[j])
            pm[o] = value
            cv[o] = cv[o] * slope

    loop(0, C, lambda o: cot_copy(o).wait())
    loop(0, PAIRS, middle, PAIRS)
    loop(0, PAIRS, lambda n: forward_pair([cv[2 * n], cv[2 * n + 1]], kfv, tf, sx, ey, n), PAIRS)
    pack(sx, ey, sb3)
    exchange_out(2, sb3, rb3)
    loop(0, steps // 2, lambda b: mix_step(maps.at[1], cv, pg, b), 2)
    received_out(2)
    owner_step(rb3, sb4, wt, gv, giv, e_ref, zf, zi, tw, edge, corner, True, lambda: None)
    exchange_back(3, sb4, rb4)
    loop(steps // 2, steps, lambda b: mix_step(maps.at[1], cv, pg, b), 2)
    sent_out(0)
    sent_back(1)
    sent_out(2)
    await_rows(7 * WROWS, w_send)
    sent_back(3)
    received_back(3)


def final_kernel(rb, pg, tmp, ti, kiv, out, grad, cx, ex, gv, out_sem, grad_sem):

    def give(c):
        return pltpu.make_async_copy(tmp.at[c], out.at[c], out_sem.at[c])

    def grad_copy(c):
        return pltpu.make_async_copy(gv.at[c], grad.at[c], grad_sem.at[c])

    loop(0, C, lambda c: give(c).start())
    clear_rest(cx)
    unpack(rb, cx, ex)

    def finish(n):
        pair = inverse_pair(cx, ex, n, kiv, ti)
        for j in range(2):
            gv[2 * n + j] = pg[2 * n + j] + pair[j]

    half = C // 2
    for first in (0, half):
        loop(first // 2, (first + half) // 2, finish, half // 2)
        loop(first, first + half, lambda c: grad_copy(c).start())
    loop(0, C, lambda c: give(c).wait())
    loop(0, C, lambda c: grad_copy(c).wait())


def local(activation, pointwise, bias_term, spectral_weight, cotangent):
    t = {name: jnp.asarray(value) for name, value in tables().items()}
    volume = (C, CELLS, NX)
    any_spec = pl.BlockSpec(memory_space=pl.ANY)
    vmem = pl.BlockSpec(memory_space=pltpu.VMEM)
    message = pltpu.VMEM((FULL, ND, LANES), F32)
    reply = pltpu.VMEM((FULL, GZ, LANES), F32)
    weights = pltpu.VMEM((8 * WROWS, LANES), F32)
    fields = pltpu.VMEM((PAIRS, LANES, LANES), F32)
    edges = pltpu.VMEM((PAIRS, 32, LANES), F32)
    dma = pltpu.SemaphoreType.DMA

    def hbm(x):
        return pltpu.with_memory_space_constraint(x, pltpu.HBM)

    def kept(x):
        return pltpu.with_memory_space_constraint(x, pltpu.VMEM)

    tmp, pg, rb, ki, ti = pl.pallas_call(
        layer_kernel,
        out_shape=[pltpu.VMEM(volume, F32), pltpu.VMEM(volume, F32), message, pltpu.VMEM((CELLS, 512), BF), pltpu.VMEM((256, NX), BF)],
        in_specs=[
            any_spec, any_spec, any_spec, any_spec, any_spec,
            any_spec, any_spec, any_spec, any_spec, any_spec, any_spec, any_spec, any_spec, any_spec, any_spec, any_spec,
        ],
        out_specs=[vmem] * 5,
        scratch_shapes=[
            pltpu.VMEM((2, NX, 256), BF),
            pltpu.VMEM((64, ND), BF),
            pltpu.VMEM((GZ, 96), BF),
            pltpu.VMEM((2, 16, LANES), F32),
            pltpu.VMEM((8, LANES, LANES), BF),
            pltpu.VMEM((32, 32), BF),
            pltpu.VMEM((C, C), F32),
            pltpu.SMEM((1, C), F32),
            pltpu.VMEM(volume, F32),
            pltpu.VMEM(volume, F32),
            pltpu.VMEM((288, CELLS), BF),
            pltpu.VMEM((512, 256), BF),
            pltpu.VMEM((256, 512), BF),
            pltpu.VMEM((2, C * 16, C * 8), BF),
            fields,
            pltpu.VMEM((256, LANES), F32),
            fields,
            edges,
            pltpu.VMEM((WIN + 64, 32), F32),
            weights,
            weights,
            pltpu.VMEM((16 * MAIN * 16, LANES), F32),
            pltpu.VMEM((ND * FULL, LANES), F32),
        ]
        + [message, message, reply, message, message, message, reply]
        + [dma((C,)), dma((C,)), dma((14,)), dma, dma, dma((4,)), dma((4,))],
        compiler_params=pltpu.CompilerParams(
            collective_id=0, has_side_effects=True, vmem_limit_bytes=36 * 1024 * 1024
        ),
        name="layer",
    )(
        hbm(activation.reshape(volume)), hbm(cotangent.reshape(volume)),
        hbm(jnp.transpose(spectral_weight[0], (0, 2, 3, 1, 4)).reshape(WIN, 32)), hbm(pointwise), hbm(bias_term.reshape(1, C)),
        *(hbm(t[name]) for name in ("tf", "ti", "kf", "ki", "zf", "zi", "tw", "g", "gi", "e", "pick")),
    )
    out, grad = pl.pallas_call(
        final_kernel,
        out_shape=[jax.ShapeDtypeStruct(volume, F32), jax.ShapeDtypeStruct(volume, F32)],
        in_specs=[vmem] * 5,
        out_specs=[any_spec, any_spec],
        scratch_shapes=[
            fields, edges, pltpu.VMEM(volume, F32), dma((C,)), dma((C,)),
        ],
        compiler_params=pltpu.CompilerParams(vmem_limit_bytes=24 * 1024 * 1024),
        name="final",
    )(kept(rb), kept(pg), kept(tmp), kept(ti), kept(ki))
    shape = (C, ZL, YL, NX)
    return out.reshape(shape), grad.reshape(shape)


def solution(mesh):
    return jax.shard_map(
        local,
        mesh=mesh,
        in_specs=(
            P(None, "gz", "gy", None),
            P(),
            P(),
            P("gz", "gy", None, None, None, None),
            P(None, "gz", "gy", None),
        ),
        out_specs=(P(None, "gz", "gy", None), P(None, "gz", "gy", None)),
        check_vma=False,
    )
```

```python
import functools
import math

import jax
import jax.numpy as jnp
import ml_dtypes
import numpy as np
from jax import lax
from jax.experimental import pallas as pl
from jax.experimental.pallas import tpu as pltpu
from jax.sharding import PartitionSpec as P

C = 20
M = 16
NX = 256
NY = 256
NZ = 128
GZ = 32
GY = 4
ND = GZ * GY
ZL = NZ // GZ
YL = NY // GY
CELLS = ZL * YL
LANES = 128
PAIRS = C // 2
MAIN = 5
EDGE = 8
FULL = 11
WROWS = 128
WIN = ZL * C * C * 2
MESH = pl.DeviceIdType.MESH
BF = jnp.bfloat16
F32 = jnp.float32


def _cos(k, n, length):
    return np.cos(2.0 * np.pi * ((k * n) % length) / length)


def _sin(k, n, length):
    return np.sin(2.0 * np.pi * ((k * n) % length) / length)


def _halves(table):
    high = table.astype(np.float32).astype(ml_dtypes.bfloat16)
    low = (table - high.astype(np.float64)).astype(ml_dtypes.bfloat16)
    return high, low


def _x_table():
    x = np.arange(NX)
    rows = np.zeros((64, NX))
    for p in range(M):
        rows[p] = _cos(p, x, NX)
        rows[16 + p] = _sin(p, x, NX) if p else _cos(16, x, NX)
    rows[32] = _sin(16, x, NX)
    return rows


def _y_table(gy):
    y = gy * YL + np.arange(YL)
    rows = np.zeros((144, ZL, YL))
    for q in range(8):
        basis = [
            _cos(q, y, NY),
            _sin(q, y, NY) if q else _cos(16, y, NY),
            _cos(q + 8, y, NY),
            _sin(q + 8, y, NY),
        ]
        for yb in range(4):
            for zl in range(ZL):
                rows[q * 16 + yb * 4 + zl, zl] = basis[yb]
    for s in range(4):
        for zl in range(ZL):
            rows[128 + s * 4 + zl, zl] = _sin(16, y, NY)
    return rows.reshape(144, CELLS)


def _mode_tables(p_zero, q_zero):
    xs = [([1, 0, 0], [0, 0, 0]), ([0, 1, 0], [0, 0, -1])] if p_zero else [([1, 0, 0], [0, 1, 0]), ([1, 0, 0], [0, -1, 0])]
    ys = [
        ([1, 0, 0, 0, 0], [0, 0, 0, 0, 0]),
        ([0, 1, 0, 0, 0], [0, 0, 0, 0, -1]),
    ] if q_zero else [([1, 0, 0, 0, 0], [0, 1, 0, 0, 0]), ([1, 0, 0, 0, 0], [0, -1, 0, 0, 0])]
    ys = ys + [([0, 0, 1, 0, 0], [0, 0, 0, 1, 0]), ([0, 0, 1, 0, 0], [0, 0, 0, -1, 0])]
    u = np.zeros((16, 8))
    v = np.zeros((16, 8))
    for i, (cx, sx) in enumerate(xs):
        for j, (cy, sy) in enumerate(ys):
            both_u = np.outer(cx, cy) - np.outer(sx, sy)
            both_v = np.outer(sx, cy) + np.outer(cx, sy)
            for xb in range(3):
                for yb in range(5):
                    if yb < 4:
                        slot = xb * 4 + yb
                    else:
                        slot = 12 + xb
                    u[slot, i * 4 + j] = both_u[xb, yb]
                    v[slot, i * 4 + j] = both_v[xb, yb]
    return u, v


def _mode_maps():
    g = np.zeros((4, 512, 256))
    gi = np.zeros((4, 256, 512))
    for variant in range(4):
        u, v = _mode_tables(variant // 2, variant % 2)
        gv = np.zeros((2, 2, 4, 8, 4, 2, 4, 8, 4))
        giv = np.zeros((2, 4, 8, 4, 2, 2, 4, 8, 4))
        for half in range(2):
            us = u[half * 8 : half * 8 + 8]
            vs = v[half * 8 : half * 8 + 8]
            for ch in range(4):
                for zl in range(4):
                    for rep in range(4):
                        gv[half, 0, ch, :, zl, 0, rep, :, ch] = us
                        gv[half, 1, ch, :, zl, 0, rep, :, ch] = -vs
                        gv[half, 0, ch, :, zl, 1, rep, :, ch] = -vs
                        gv[half, 1, ch, :, zl, 1, rep, :, ch] = -us
                        giv[0, rep, :, ch, half, 0, ch, :, zl] = us.T
                        giv[1, rep, :, ch, half, 0, ch, :, zl] = -vs.T
                        giv[0, rep, :, ch, half, 1, ch, :, zl] = -vs.T
                        giv[1, rep, :, ch, half, 1, ch, :, zl] = -us.T
        g[variant] = gv.reshape(512, 256)
        gi[variant] = giv.reshape(256, 512)
    return g.astype(ml_dtypes.bfloat16), gi.astype(ml_dtypes.bfloat16)


def _expand_maps():
    e = np.zeros((8, 4, 8, 4, 4, 32))
    for m in range(8):
        for ch in range(4):
            e[m, 0, m, ch, ch, :] = 1
    return e.reshape(8, 128, 128).astype(ml_dtypes.bfloat16)


def _pick_map():
    pick = np.zeros((32, 32))
    for q in range(8):
        for j, k in enumerate([q, (-q if q else -16), q + 8, -(q + 8)]):
            pick[j * 8 + q, k % 32] = 1
    return pick.astype(ml_dtypes.bfloat16)


@functools.cache
def tables():
    xh, xl = _halves(_x_table())
    tf = np.zeros((2, NX, 256), ml_dtypes.bfloat16)
    for j in range(2):
        tf[j, :, 64 * j : 64 * j + 64] = xh.T
        tf[j, :, 128 + 64 * j : 192 + 64 * j] = xl.T
    ti = np.concatenate([xh, xh, xl, np.zeros_like(xl)], axis=0)
    kf, ki = [], []
    for gy in range(GY):
        h, l = _halves(_y_table(gy))
        kf.append(np.concatenate([h, l], axis=0))
        ht, lt = h.T, l.T
        pad = np.zeros((CELLS, 80), ml_dtypes.bfloat16)
        ki.append(np.concatenate([ht[:, :128], lt[:, :128], ht[:, :128], ht[:, 128:], ht[:, 128:], lt[:, 128:], pad], axis=1))
    kz = np.arange(M)[:, None]
    far = 4 * (np.arange(ND)[None, :] // GY)
    h, l = _halves(np.concatenate([_cos(kz, far, NZ), _sin(kz, far, NZ)], axis=0))
    zf = np.concatenate([h, l], axis=0)
    far = 4 * np.arange(GZ)[None, :]
    factor = np.where(kz == 0, 1.0, 2.0) / float(NX * NY * NZ)
    h, l = _halves(np.concatenate([factor * _cos(kz, far, NZ), factor * _sin(kz, far, NZ)], axis=0).T)
    zi = np.concatenate([h, h, l], axis=1)
    near = np.arange(LANES)[None, :] % 4
    tw = np.stack([_cos(kz, near, NZ), _sin(kz, near, NZ)]).astype(np.float32)
    g, gi = _mode_maps()
    return dict(tf=tf, ti=ti, kf=np.stack(kf), ki=np.stack(ki), zf=zf, zi=zi, tw=tw, g=g, gi=gi, e=_expand_maps(), pick=_pick_map())


def nn(a, b):
    return lax.dot_general(a, b, (((1,), (0,)), ((), ())), preferred_element_type=F32)


def nt(a, b):
    return lax.dot_general(a, b, (((1,), (1,)), ((), ())), preferred_element_type=F32)


def halves(value):
    high = value.astype(BF)
    low = (value - high.astype(F32)).astype(BF)
    return high, low


def lanes_of(value):
    return lax.broadcasted_iota(jnp.int32, value.shape, 1)


def swap_blocks(tiles, width):
    tiles = list(tiles)
    block = lax.rem(lanes_of(tiles[0]) // width, 8)
    for bit in (1, 2, 4):
        upper = lax.rem(block // bit, 2) == 1
        shift = bit * width
        for i in range(8):
            if i & bit:
                continue
            a, b = tiles[i], tiles[i | bit]
            tiles[i] = jnp.where(upper, pltpu.roll(b, shift, 1), a)
            tiles[i | bit] = jnp.where(upper, b, pltpu.roll(a, LANES - shift, 1))
    return tiles


def forward_pair(pair, kf, tf, sx, ey, n):
    parts = []
    for volume in pair:
        ah, al = halves(volume)
        b = nn(kf[...], ah)
        parts.append(halves(b[:144] + b[144:] + nn(kf[:144], al)))
    (h0, l0), (h1, l1) = parts
    o = nn(h0, tf[0]) + nn(h1, tf[1])
    o = o[:, :LANES] + o[:, LANES:] + nn(l0, tf[0, :, :LANES]) + nn(l1, tf[1, :, :LANES])
    sx[n] = o[:LANES].T
    ey[pl.ds(pl.multiple_of(n * 16, 16), 16), :] = o[LANES:]


def pack(sx, ey, sb):
    for r in range(MAIN):
        tiles = swap_blocks([sx[2 * r + i // 4, pl.ds((i // 2 % 2) * 64 + (i % 2) * 16, 16), :] for i in range(8)], 16)
        for q in range(8):
            sb[r, 16 * q : 16 * q + 16, :] = tiles[q]
    turned = [ey[0:LANES, :].T, ey[LANES : 2 * LANES, :].T]
    slot = lax.rem(lax.broadcasted_iota(jnp.int32, (16, LANES), 1) // 4, 4)
    block = lax.broadcasted_iota(jnp.int32, (16, LANES), 1) // 16
    zero = jnp.zeros((16, LANES), F32)
    by_ch = [
        [
            sum((jnp.where(slot == h, t[64 * ch + 16 * h : 64 * ch + 16 * h + 16], zero) for h in range(3)), zero)
            for ch in range(2)
        ]
        for t in turned
    ]
    none = jnp.zeros((8, LANES), F32)
    top = lax.broadcasted_iota(jnp.int32, (16, LANES), 0) == 0
    for e in range(EDGE - MAIN):
        tiles = []
        edge = zero
        for c in range(4):
            for k in range(2):
                r = 2 * e + k
                if r == MAIN:
                    tiles.append(none)
                    continue
                n = 2 * r + c // 2
                tiles.append(sx[n, pl.ds((c % 2) * 64 + 32, 8), :])
                to = 2 * c + 1 - k
                moved = pltpu.roll(by_ch[n // 8][c % 2], (to - n % 8) % 8 * 16, 1)
                edge = edge + jnp.where(block == to, moved, zero)
        tiles = swap_blocks(tiles, 16)
        sb[MAIN + e, 0:8, :] = jnp.where(top[:8], tiles[0], edge[:8])
        sb[MAIN + e, 8:16, :] = edge[8:]
        sb[EDGE + e, 0:16, :] = edge
        for q in range(1, 8):
            sb[MAIN + e, 16 * q : 16 * q + 8, :] = tiles[q]


def unpack(rb, cx, ex):
    for r in range(MAIN):
        tiles = swap_blocks([rb[r, 16 * q : 16 * q + 16, :] for q in range(8)], 16)
        for i in range(8):
            cx[2 * r + i // 4, pl.ds((i // 2 % 2) * 64 + (i % 2) * 16, 16), :] = tiles[i]
    top = lax.broadcasted_iota(jnp.int32, (16, LANES), 0) == 0
    rows = []
    for e in range(EDGE - MAIN):
        tiles = [rb[MAIN + e, 0:8, :]]
        tiles += [jnp.where(top[:8], rb[MAIN + e, 16 * q : 16 * q + 8, :], 0.0) for q in range(1, 8)]
        tiles = swap_blocks(tiles, 16)
        for c in range(4):
            for k in range(2):
                r = 2 * e + k
                if r < MAIN:
                    cx[2 * r + c // 2, pl.ds((c % 2) * 64 + 32, 8), :] = tiles[2 * c + k]
        rows.append(jnp.where(top, rb[EDGE + e, 0:16, :], rb[MAIN + e, 0:16, :]))
    turned = jnp.concatenate(rows + [jnp.zeros((80, LANES), F32)], axis=0).T
    row = lax.broadcasted_iota(jnp.int32, (16, LANES), 0)
    block = lax.broadcasted_iota(jnp.int32, (16, LANES), 1) // 16
    keep = lax.rem(block, 4) == row // 4
    zero = jnp.zeros((16, LANES), F32)
    for r in range(MAIN):
        for c in range(4):
            at = 32 * c + 16 * (1 - r % 2)
            e = jnp.where(block == r // 2, turned[at : at + 16], zero)
            for shift in (16, 32, 64):
                e = e + pltpu.roll(e, shift, 1)
            ex[2 * r + c // 2, pl.ds((c % 2) * 16, 16), :] = jnp.where(keep, e, zero)


def clear_rest(cx):
    for n in range(PAIRS):
        for ch in range(2):
            cx[n, pl.ds(64 * ch + 40, 24), :] = jnp.zeros((24, LANES), F32)


def inverse_pair(cx, ex, n, ki, ti):
    c = cx[n].T
    low = lanes_of(c) < 64
    other = pltpu.roll(c, 64, 1)
    d = jnp.concatenate([jnp.where(low, c, other), jnp.where(low, other, c)], axis=1)
    dh, dl = halves(d)
    e = ex[n]
    eh, el = halves(jnp.concatenate([e[:16], e[16:]], axis=1))
    one = jnp.concatenate([dh, dh], axis=0)
    two = jnp.concatenate([dl, eh, el, eh, jnp.zeros((80, 256), BF)], axis=0)
    h = nn(ki[:, :256], one) + nn(ki[:, 256:], two)
    hh, hl = halves(h)
    out = []
    for j in range(2):
        high = hh[:, LANES * j : LANES * j + LANES]
        rest = hl[:, LANES * j : LANES * j + LANES]
        mix = jnp.where(lanes_of(high) < 64, high.astype(F32), rest.astype(F32)).astype(BF)
        out.append(nn(jnp.concatenate([mix, high], axis=1), ti[...]))
    return out


def owner_step(rb, sb, wt, g, gi, e_ref, zf, zi, tw, edge, corner, adjoint, ready):
    d = jnp.concatenate([rb[r] for r in range(FULL)], axis=1)
    dh, dl = halves(d)
    zfv = zf[...]
    f = nn(zfv, dh)
    f = f[:32] + f[32:] + nn(zfv[:32], dl)
    cb = tw[0]
    sb_near = tw[1]

    first_half = lax.rem(lax.broadcasted_iota(jnp.int32, (32, LANES), 1) // 16, 2) == 0
    fields = [f[:, r * LANES : (r + 1) * LANES] for r in range(FULL)]
    extras = []
    for e in range(EDGE - MAIN):
        one = jnp.where(edge, fields[MAIN + e], 0.0)
        two = jnp.where(corner, fields[EDGE + e], one)
        extras.append(jnp.where(first_half, one, two))
        extras.append(jnp.where(first_half, pltpu.roll(one, LANES - 16, 1), pltpu.roll(two, 16, 1)))

    def turned(field):
        fc = field[:16]
        fs = field[16:]
        return jnp.concatenate([fc * cb - fs * sb_near, fs * cb + fc * sb_near], axis=1)

    z = jnp.concatenate(
        [jnp.concatenate([turned(fields[r]), turned(extras[r])], axis=1) for r in range(MAIN)], axis=0
    )
    zh, zlow = halves(z)
    x = nn(jnp.concatenate([zh, zlow], axis=0), g[...])
    x = x[:80] + x[80:]
    xre, xim = x[:, :LANES], x[:, LANES:]

    ready()

    def weight(ri, m, r):
        return wt[pl.ds(((ri * 8 + m) * MAIN + r) * 16, 16), :]

    zero = jnp.zeros((16, LANES), F32)
    if not adjoint:
        pieces = jnp.concatenate(halves(xre) + halves(xim), axis=0)
        yre, yim = [], []
        for m in range(8):
            xm = nn(pieces, e_ref[m])
            xmr = xm[:80] + xm[80:160]
            xmi = xm[160:240] + xm[240:]
            sr, si = zero, zero
            for r in range(MAIN):
                wr, wi = weight(0, m, r), weight(1, m, r)
                ar, ai = xmr[16 * r : 16 * r + 16], xmi[16 * r : 16 * r + 16]
                sr = sr + wr * ar - wi * ai
                si = si + wr * ai + wi * ar
            yre.append(sr)
            yim.append(si)
        vre = swap_blocks(yre, 4)[:MAIN]
        vim = swap_blocks(yim, 4)[:MAIN]
        v = jnp.concatenate([jnp.concatenate([a, b], axis=1) for a, b in zip(vre, vim)], axis=0)
    else:
        gre = swap_blocks([xre[16 * t : 16 * t + 16] for t in range(MAIN)] + [zero] * 3, 4)
        gim = swap_blocks([xim[16 * t : 16 * t + 16] for t in range(MAIN)] + [zero] * 3, 4)
        total = None
        for m in range(8):
            yr, yi = [], []
            for r in range(MAIN):
                wr, wi = weight(0, m, r), weight(1, m, r)
                yr.append(wr * gre[m] + wi * gim[m])
                yi.append(wr * gim[m] - wi * gre[m])
            pieces = jnp.concatenate(
                halves(jnp.concatenate(yr, axis=0)) + halves(jnp.concatenate(yi, axis=0)), axis=0
            )
            part = nt(pieces, e_ref[m])
            total = part if total is None else total + part
        v = jnp.concatenate([total[:80] + total[80:160], total[160:240] + total[240:]], axis=1)
    vh, vl = halves(v)
    c = nn(jnp.concatenate([vh, vl], axis=0), gi[...])
    c = c[:80] + c[80:]

    def back(t, half):
        cc = c[16 * t : 16 * t + 16, half * 256 : half * 256 + LANES]
        cs = c[16 * t : 16 * t + 16, half * 256 + LANES : half * 256 + 256]
        return jnp.concatenate([cc * cb + cs * sb_near, cs * cb - cc * sb_near], axis=0)

    edges, corners = [], []
    none = jnp.zeros((32, LANES), F32)
    for e in range(EDGE - MAIN):
        one = back(2 * e, 1)
        two = back(2 * e + 1, 1) if 2 * e + 1 < MAIN else none
        low = jnp.where(first_half, one, pltpu.roll(two, 16, 1))
        high = jnp.where(first_half, pltpu.roll(two, LANES - 16, 1), one)
        edges.append(low + jnp.where(corner, 0.0, high))
        corners.append(high)
    r = jnp.concatenate([back(t, 0) for t in range(MAIN)] + edges + corners, axis=1)
    rh, rl = halves(r)
    out = nn(zi[...], jnp.concatenate([rh, rl, rh], axis=0))
    for t in range(FULL):
        sb[t] = out[:, t * LANES : (t + 1) * LANES]


def owner_of(z):
    i = z // 16
    p = lax.rem(z * (1 - 2 * i) + 32 * i, 16)
    return p, i, lax.rem(i + p, 2)


def group_of(p, h, y):
    return 4 * h + lax.rem(y + 8 - p // 2, 4)


def owner_device(p, q):
    i = lax.rem(q // 4 + p, 2)
    first = (16 - p) // 16
    z = p + i * (32 - 2 * p - 16 * first)
    y = lax.rem(lax.rem(q, 4) + p // 2, 4)
    return z, y


def weight_step(wv, ws, pick, k):
    for ri in range(2):
        block = jnp.concatenate([wv[pl.ds(k * 800 + c * 40 + ri, 32, stride=2), :] for c in range(C)], axis=0)
        bh, bl = halves(block)
        rows = nt(pick, bh) + nt(pick, bl)
        for j in range(4):
            tiles = [rows[8 * j : 8 * j + 8, r * LANES : (r + 1) * LANES] for r in range(MAIN)]
            lane = lanes_of(tiles[0])
            for r in range(4):
                one = pltpu.roll(tiles[4], (20 - 32 * r) % LANES, 1)
                two = pltpu.roll(tiles[4], (40 - 32 * r) % LANES, 1)
                tile = jnp.where((lane >= 20) & (lane < 32), one, tiles[r])
                tile = jnp.where((lane >= 52) & (lane < 60), two, tile)
                ws[pl.ds(((ri * 4 + j) * 4 + r) * 4 + k, 8, stride=WROWS), :] = tile


def weight_spread(wb, wt, n):
    ri = n // 4
    j = lax.rem(n, 4)
    for k in range(4):
        tiles = [wb[pl.ds((n * 4 + r) * 4 + k, 8, stride=WROWS), :] for r in range(4)]
        lane = lanes_of(tiles[0])
        last = jnp.zeros_like(tiles[0])
        for r in range(4):
            one = pltpu.roll(tiles[r], (32 * r - 20) % LANES, 1)
            two = pltpu.roll(tiles[r], (32 * r - 40) % LANES, 1)
            last = jnp.where((lane >= 32 * r) & (lane < 32 * r + 12), one, last)
            last = jnp.where((lane >= 32 * r + 12) & (lane < 32 * r + 20), two, last)
        for r, v in enumerate(tiles + [last]):
            base = ((ri * 8 + j) * MAIN + r) * 16 + k
            for i in range(2):
                wt[pl.ds(base + i * 4 * MAIN * 16, 4, stride=4), :] = v[4 * i : 4 * i + 4]


def mix_maps(pw):
    ones = jnp.where(
        lax.broadcasted_iota(jnp.int32, (C * 8, C), 0) // 8 == lax.broadcasted_iota(jnp.int32, (C * 8, C), 1), 1.0, 0.0
    ).astype(BF)
    shape = (C * 8, C * 8)
    same = lax.rem(lax.broadcasted_iota(jnp.int32, shape, 0), 8) == lax.rem(lax.broadcasted_iota(jnp.int32, shape, 1), 8)
    fwd, adj = [], []
    for part in halves(pw[...]):
        rows = nn(ones, part).astype(BF)
        fwd.append(jnp.where(same, nt(ones, rows), 0.0).astype(BF))
        adj.append(jnp.where(same, nt(rows, ones), 0.0).astype(BF))
    return jnp.concatenate(fwd, axis=0), jnp.concatenate(adj, axis=0)


def mix_step(maps, src, dst, b):
    rows = pl.ds(pl.multiple_of(b * 8, 8), 8)
    sh, sl = halves(src[:, rows, :].reshape(C * 8, NX))
    o = nn(maps[...], sh)
    o = o[: C * 8] + o[C * 8 :] + nn(maps[: C * 8], sl)
    dst[:, rows, :] = o.reshape(C, 8, NX)


def activate(mixed):
    cdf = 0.5 * (1.0 + lax.erf(mixed * (1.0 / math.sqrt(2.0))))
    density = jnp.exp(-0.5 * mixed * mixed) * (1.0 / math.sqrt(2.0 * math.pi))
    return mixed * cdf, cdf + mixed * density


def loop(first, last, fn, unroll=1):
    def body(i, carry):
        fn(i)
        return carry

    lax.fori_loop(first, last, body, 0, unroll=unroll)


def layer_kernel(
    act, cot, w, pw_in, bias_in, tf_in, ti_in, kf, ki, zf_in, zi_in, tw_in, g, gi, e_in, pick_in,
    pm, pg, rb4, kiv, ti,
    tf, zf, zi, tw, e_ref, pick, pw, bias, av, cv, kfv, gv, giv, maps, sx, ey, cx, ex, wv, ws, wb, wt, count,
    sb1, rb1, sb2, rb2, sb3, rb3, sb4,
    act_sem, cot_sem, tab_sem, w_send, w_recv, send_sem, recv_sem,
):
    gz = lax.axis_index("gz")
    gy = lax.axis_index("gy")
    p, sign, h = owner_of(gz)
    q = group_of(p, h, gy)
    mine = q * 16 + p
    edge = p * q == 0
    corner = p + q == 0

    def by_kind(fn):
        pl.when(p * q != 0)(lambda: fn(MAIN))
        pl.when((p * q == 0) & (p + q != 0))(lambda: fn(EDGE))
        pl.when(p + q == 0)(lambda: fn(FULL))

    variant = 2 * ((16 - p) // 16) + (8 - q) // 8

    def act_copy(c):
        return pltpu.make_async_copy(act.at[c], av.at[c], act_sem.at[c])

    def cot_copy(c):
        return pltpu.make_async_copy(cot.at[c], cv.at[c], cot_sem.at[c])

    table_copies = [
        pltpu.make_async_copy(kf.at[gy], kfv, tab_sem.at[0]),
        pltpu.make_async_copy(ki.at[gy], kiv, tab_sem.at[1]),
        pltpu.make_async_copy(g.at[variant], gv, tab_sem.at[2]),
        pltpu.make_async_copy(gi.at[variant], giv, tab_sem.at[3]),
        pltpu.make_async_copy(w, wv.at[pl.ds(0, WIN)], tab_sem.at[4]),
    ]
    early = [pltpu.make_async_copy(*pair, tab_sem.at[5 + i]) for i, pair in enumerate([(tf_in, tf), (pick_in, pick)])]
    late = [
        pltpu.make_async_copy(*pair, tab_sem.at[7 + i])
        for i, pair in enumerate([(pw_in, pw), (zf_in, zf), (zi_in, zi), (tw_in, tw), (e_in, e_ref), (ti_in, ti), (bias_in, bias)])
    ]
    late += table_copies[1:4]
    table_copies[0].start()
    early[0].start()
    loop(0, 4, lambda c: act_copy(c).start())
    table_copies[4].start()
    early[1].start()

    next_y = [gy] + [lax.rem(gy + j, GY) for j in range(1, GY)]

    def each_peer(fn, per_z):
        own = per_z(gz)
        for j in range(1, GY):
            fn(gz, next_y[j], own)

        def body(_, z):
            z = z + 1
            z = jnp.where(z == GZ, 0, z)
            known = per_z(z)
            for j in range(GY):
                fn(z, next_y[j], known)
            return z

        lax.fori_loop(1, GZ, body, gz)

    barrier = pltpu.get_barrier_semaphore()
    each_peer(
        lambda z, y, _: pl.semaphore_signal(barrier, 1, device_id=(z, y), device_id_type=MESH), lambda z: None
    )

    def exchange_out(n, src, dst):
        def start(z, y, to, at, rows):
            pltpu.make_async_remote_copy(
                src_ref=src.at[pl.ds(at, rows), to],
                dst_ref=dst.at[pl.ds(at, rows), gz * GY + gy],
                send_sem=send_sem.at[n],
                recv_sem=recv_sem.at[n],
                device_id=(z, y),
                device_id_type=MESH,
            ).start()

        def send(z, y, known):
            tp, _, th = known
            tq = group_of(tp, th, y)
            to = tq * 16 + tp
            some = tp * tq
            pl.when(some == 0)(lambda: start(z, y, to, 0, EDGE))
            pl.when(some != 0)(lambda: start(z, y, to, 0, MAIN))

        def keep(rows):
            pltpu.make_async_copy(
                src.at[pl.ds(0, rows), mine], dst.at[pl.ds(0, rows), gz * GY + gy], recv_sem.at[n]
            ).start()

        each_peer(send, owner_of)
        by_kind(keep)
        pl.when(p + q != 0)(lambda: start(0, 0, 0, EDGE, FULL - EDGE))

    def exchange_back(n, src, dst):
        def start_all(rows):
            def send(z, y, _):
                pltpu.make_async_remote_copy(
                    src_ref=src.at[pl.ds(0, rows), z],
                    dst_ref=dst.at[pl.ds(0, rows), mine],
                    send_sem=send_sem.at[n],
                    recv_sem=recv_sem.at[n],
                    device_id=(z, y),
                    device_id_type=MESH,
                ).start()

            pltpu.make_async_copy(src.at[pl.ds(0, rows), gz], dst.at[pl.ds(0, rows), mine], recv_sem.at[n]).start()
            each_peer(send, lambda z: None)

        by_kind(start_all)

    def await_rows(rows, sem):
        pltpu.make_async_copy(count.at[pl.ds(0, rows)], count.at[pl.ds(0, rows)], sem).wait()

    def received_out(n):
        by_kind(lambda rows: await_rows(ND * rows, recv_sem.at[n]))

    def received_back(n):
        await_rows(ND * MAIN + 23 * (EDGE - MAIN) + (FULL - EDGE), recv_sem.at[n])

    def sent_out(n):
        most = (ND - 1) * MAIN + (FULL - EDGE)
        others = {MAIN: most + 23 * (EDGE - MAIN), EDGE: most + 22 * (EDGE - MAIN), FULL: (ND - 1) * MAIN + 22 * (EDGE - MAIN)}
        by_kind(lambda rows: await_rows(others[rows], send_sem.at[n]))

    def sent_back(n):
        by_kind(lambda rows: await_rows((ND - 1) * rows, send_sem.at[n]))

    loop(4, C, lambda c: act_copy(c).start())
    for copy in late:
        copy.start()
    loop(0, C, lambda c: cot_copy(c).start())

    wv[pl.ds(WIN, 64), :] = jnp.zeros((64, 32), F32)
    table_copies[0].wait()
    early[0].wait()

    def first(n):
        act_copy(2 * n).wait()
        act_copy(2 * n + 1).wait()
        forward_pair([av[2 * n], av[2 * n + 1]], kfv, tf, sx, ey, n)

    loop(0, 2, first, 2)
    table_copies[4].wait()
    early[1].wait()
    pickv = pick[...]
    loop(0, 4, lambda k: weight_step(wv, ws, pickv, k))
    pl.semaphore_wait(barrier, ND - 1)
    slot = (sign * 4 + gy) * WROWS

    def send_weights(to):
        z, y = owner_device(p, to)

        @pl.when(to == q)
        def _():
            pltpu.make_async_copy(ws.at[pl.ds(to * WROWS, WROWS)], wb.at[pl.ds(slot, WROWS)], w_recv).start()

        @pl.when(to != q)
        def _():
            pltpu.make_async_remote_copy(
                src_ref=ws.at[pl.ds(to * WROWS, WROWS)],
                dst_ref=wb.at[pl.ds(slot, WROWS)],
                send_sem=w_send,
                recv_sem=w_recv,
                device_id=(z, y),
                device_id_type=MESH,
            ).start()

    loop(0, 8, send_weights)
    loop(2, PAIRS, first, 8)
    pack(sx, ey, sb1)
    exchange_out(0, sb1, rb1)

    for copy in late:
        copy.wait()
    fwd, adj = mix_maps(pw)
    maps[0] = fwd
    maps[1] = adj
    steps = CELLS // 8
    loop(0, steps // 2, lambda b: mix_step(maps.at[0], av, pm, b), 2)
    clear_rest(cx)

    def weights_ready():
        await_rows(8 * WROWS, w_recv)
        loop(0, 8, lambda n: weight_spread(wb, wt, n), 2)

    received_out(0)
    owner_step(rb1, sb2, wt, gv, giv, e_ref, zf, zi, tw, edge, corner, False, weights_ready)
    exchange_back(1, sb2, rb2)
    loop(steps // 2, steps, lambda b: mix_step(maps.at[0], av, pm, b), 2)
    received_back(1)
    unpack(rb2, cx, ex)

    def middle(n):
        pair = inverse_pair(cx, ex, n, kiv, ti)
        for j in range(2):
            o = 2 * n + j
            value, slope = activate(pm[o] + bias[0, o] + pair[j])
            pm[o] = value
            cv[o] = cv[o] * slope

    loop(0, C, lambda o: cot_copy(o).wait())
    loop(0, PAIRS, middle, PAIRS)
    loop(0, PAIRS, lambda n: forward_pair([cv[2 * n], cv[2 * n + 1]], kfv, tf, sx, ey, n), PAIRS)
    pack(sx, ey, sb3)
    exchange_out(2, sb3, rb3)
    loop(0, steps // 2, lambda b: mix_step(maps.at[1], cv, pg, b), 2)
    received_out(2)
    owner_step(rb3, sb4, wt, gv, giv, e_ref, zf, zi, tw, edge, corner, True, lambda: None)
    exchange_back(3, sb4, rb4)
    loop(steps // 2, steps, lambda b: mix_step(maps.at[1], cv, pg, b), 2)
    sent_out(0)
    sent_back(1)
    sent_out(2)
    await_rows(7 * WROWS, w_send)
    sent_back(3)
    received_back(3)


def final_kernel(rb, pg, tmp, ti, kiv, out, grad, cx, ex, gv, out_sem, grad_sem):

    def give(c):
        return pltpu.make_async_copy(tmp.at[c], out.at[c], out_sem.at[c])

    def grad_copy(c):
        return pltpu.make_async_copy(gv.at[c], grad.at[c], grad_sem.at[c])

    loop(0, C, lambda c: give(c).start())
    clear_rest(cx)
    unpack(rb, cx, ex)

    def finish(n):
        pair = inverse_pair(cx, ex, n, kiv, ti)
        for j in range(2):
            gv[2 * n + j] = pg[2 * n + j] + pair[j]

    half = C // 2
    for first in (0, half):
        loop(first // 2, (first + half) // 2, finish, half // 2)
        loop(first, first + half, lambda c: grad_copy(c).start())
    loop(0, C, lambda c: give(c).wait())
    loop(0, C, lambda c: grad_copy(c).wait())


def local(activation, pointwise, bias_term, spectral_weight, cotangent):
    t = {name: jnp.asarray(value) for name, value in tables().items()}
    volume = (C, CELLS, NX)
    any_spec = pl.BlockSpec(memory_space=pl.ANY)
    vmem = pl.BlockSpec(memory_space=pltpu.VMEM)
    message = pltpu.VMEM((FULL, ND, LANES), F32)
    reply = pltpu.VMEM((FULL, GZ, LANES), F32)
    weights = pltpu.VMEM((9 * WROWS, LANES), F32)
    fields = pltpu.VMEM((PAIRS, LANES, LANES), F32)
    edges = pltpu.VMEM((PAIRS, 32, LANES), F32)
    dma = pltpu.SemaphoreType.DMA

    def hbm(x):
        return pltpu.with_memory_space_constraint(x, pltpu.HBM)

    def kept(x):
        return pltpu.with_memory_space_constraint(x, pltpu.VMEM)

    tmp, pg, rb, ki, ti = pl.pallas_call(
        layer_kernel,
        out_shape=[pltpu.VMEM(volume, F32), pltpu.VMEM(volume, F32), message, pltpu.VMEM((CELLS, 512), BF), pltpu.VMEM((256, NX), BF)],
        in_specs=[
            any_spec, any_spec, any_spec, any_spec, any_spec,
            any_spec, any_spec, any_spec, any_spec, any_spec, any_spec, any_spec, any_spec, any_spec, any_spec, any_spec,
        ],
        out_specs=[vmem] * 5,
        scratch_shapes=[
            pltpu.VMEM((2, NX, 256), BF),
            pltpu.VMEM((64, ND), BF),
            pltpu.VMEM((GZ, 96), BF),
            pltpu.VMEM((2, 16, LANES), F32),
            pltpu.VMEM((8, LANES, LANES), BF),
            pltpu.VMEM((32, 32), BF),
            pltpu.VMEM((C, C), F32),
            pltpu.SMEM((1, C), F32),
            pltpu.VMEM(volume, F32),
            pltpu.VMEM(volume, F32),
            pltpu.VMEM((288, CELLS), BF),
            pltpu.VMEM((512, 256), BF),
            pltpu.VMEM((256, 512), BF),
            pltpu.VMEM((2, C * 16, C * 8), BF),
            fields,
            pltpu.VMEM((256, LANES), F32),
            fields,
            edges,
            pltpu.VMEM((WIN + 64, 32), F32),
            weights,
            weights,
            pltpu.VMEM((16 * MAIN * 16 + 16, LANES), F32),
            pltpu.VMEM((ND * FULL, LANES), F32),
        ]
        + [message, message, reply, message, message, message, reply]
        + [dma((C,)), dma((C,)), dma((14,)), dma, dma, dma((4,)), dma((4,))],
        compiler_params=pltpu.CompilerParams(
            collective_id=0, has_side_effects=True, vmem_limit_bytes=36 * 1024 * 1024
        ),
        name="layer",
    )(
        hbm(activation.reshape(volume)), hbm(cotangent.reshape(volume)),
        hbm(jnp.transpose(spectral_weight[0], (0, 2, 3, 1, 4)).reshape(WIN, 32)), hbm(pointwise), hbm(bias_term.reshape(1, C)),
        *(hbm(t[name]) for name in ("tf", "ti", "kf", "ki", "zf", "zi", "tw", "g", "gi", "e", "pick")),
    )
    out, grad = pl.pallas_call(
        final_kernel,
        out_shape=[jax.ShapeDtypeStruct(volume, F32), jax.ShapeDtypeStruct(volume, F32)],
        in_specs=[vmem] * 5,
        out_specs=[any_spec, any_spec],
        scratch_shapes=[
            fields, edges, pltpu.VMEM(volume, F32), dma((C,)), dma((C,)),
        ],
        compiler_params=pltpu.CompilerParams(vmem_limit_bytes=24 * 1024 * 1024),
        name="final",
    )(kept(rb), kept(pg), kept(tmp), kept(ti), kept(ki))
    shape = (C, ZL, YL, NX)
    return out.reshape(shape), grad.reshape(shape)


def solution(mesh):
    return jax.shard_map(
        local,
        mesh=mesh,
        in_specs=(
            P(None, "gz", "gy", None),
            P(),
            P(),
            P("gz", "gy", None, None, None, None),
            P(None, "gz", "gy", None),
        ),
        out_specs=(P(None, "gz", "gy", None), P(None, "gz", "gy", None)),
        check_vma=False,
    )
```
